256 devices in a mesh: batch: 16 (over z, core), proto: 16 (over y, x).
Axes of the slice: x: 4, y: 4, z: 8, core: 2. Of those that a mesh axis runs over, the one named last changes fastest.
Arguments:
- teacher_feats: bfloat16 [64, 256, 256], P('batch'), may hold values from -64 to 64
- student_feats: bfloat16 [64, 256, 256], P('batch'), may hold values from -64 to 64
- prototypes: bfloat16 [256, 65536], P(None, 'proto'), may hold values from -1 to 1
- mask_index: int32 [64, 128], P('batch'), may hold values from 0 to 255, as said below
Outputs:
- grad_student: float32 [64, 256, 256], P('batch')
- grad_protos: float32 [256, 65536], P('batch', 'proto')
The draws below stay inside these ranges and needn't reach their ends.
Inputs may be any that keep to these rules, and one draw needn't show every extreme that they name: `mask_index`: within each image the 128 indices are distinct.
All inputs are finite; a program needn't handle non-finite values.
Results may differ from the reference program's by a relative error of at most 0.0083.
Values sent between devices are 32-bit elements; how exact they have to be, the bound alone decides.
No kernel may reach another device: no remote copies, remote signals or barrier semaphores. Data moves between devices by JAX's collectives and lax.ppermute only.
A program may use at most 64 MiB of HBM per device.

```python
import math
import jax
import jax.numpy as jnp
from jax import lax

D = 256
K = 65536
PATCHES = 256
MASKED = 128
ITERS = 3
IMAGES = 64


def shared_parts(key):
    proto_key, pick_key, weight_key, noise_key = jax.random.split(key, 4)
    protos = jax.random.normal(proto_key, (D, K), jnp.float32) / math.sqrt(D)
    chosen = jax.random.randint(pick_key, (IMAGES, PATCHES, 4), 0, K)
    weights = jax.random.uniform(weight_key, (IMAGES, PATCHES, 4), jnp.float32, 0.5, 2.0)
    columns = jnp.take(protos.T, chosen, axis=0)
    noise = jax.random.normal(noise_key, (IMAGES, PATCHES, D), jnp.float32)
    base = jnp.sum(columns * weights[..., None], axis=2) + 0.5 / math.sqrt(D) * noise
    return (protos, base)


def draw_prototypes(key, part):
    protos, base = shared_parts(key)
    return protos.astype(jnp.bfloat16)


def draw_teacher_feats(key, part):
    protos, base = shared_parts(key)
    values = base
    return values.astype(jnp.bfloat16)


def draw_student_feats(key, part):
    protos, base = shared_parts(key)
    key = jax.random.fold_in(key, 3)
    noise = jax.random.normal(key, (IMAGES, PATCHES, D), jnp.float32)
    values = base + 0.3 / math.sqrt(D) * noise
    return values.astype(jnp.bfloat16)


def draw_mask_index(key, part):
    key = jax.random.fold_in(key, 4)
    image_keys = jax.random.split(key, IMAGES)

    def pick_patches(image_key):
        return jax.random.permutation(image_key, PATCHES)[:MASKED]
    return jax.vmap(pick_patches)(image_keys).astype(jnp.int32)


def setup_inputs(seed: int = 0) -> dict:
    keys = jax.random.split(jax.random.key(seed), 5)
    teacher_feats = draw_teacher_feats(jax.random.fold_in(keys[4], 71), 0)
    student_feats = draw_student_feats(jax.random.fold_in(keys[4], 71), 0)
    prototypes = draw_prototypes(jax.random.fold_in(keys[4], 71), 0)
    mask_index = draw_mask_index(jax.random.fold_in(keys[4], 71), 0)
    return {"teacher_feats": teacher_feats, "student_feats": student_feats, "prototypes": prototypes, "mask_index": mask_index}


TEACHER_TEMP = 0.04
STUDENT_TEMP = 0.1
EPSILON = 1e-06

def reference(teacher_feats, student_feats, prototypes, mask_index):
    picks = mask_index[:, :, None]
    teacher_rows = jnp.take_along_axis(teacher_feats, picks, axis=1).reshape(-1, D).astype(jnp.float32)
    student_rows = jnp.take_along_axis(student_feats, picks, axis=1).reshape(-1, D).astype(jnp.float32)
    teacher_norm = jnp.sqrt(lax.optimization_barrier(jnp.sum(teacher_rows * teacher_rows, axis=1, keepdims=True)) + EPSILON)
    teacher_unit = (teacher_rows / teacher_norm).astype(jnp.bfloat16)
    student_norm = jnp.sqrt(lax.optimization_barrier(jnp.sum(student_rows * student_rows, axis=1, keepdims=True)) + EPSILON)
    student_full = student_rows / student_norm
    student_unit = student_full.astype(jnp.bfloat16)
    proto_float = prototypes.astype(jnp.float32)
    proto_norm = jnp.sqrt(lax.optimization_barrier(jnp.sum(proto_float * proto_float, axis=0, keepdims=True)) + EPSILON)
    proto_full = proto_float / proto_norm
    proto_unit = proto_full.astype(jnp.bfloat16)
    block_width = min(K, 4096)
    block_count = K // block_width
    blocks = proto_unit.reshape(D, block_count, block_width).transpose(1, 0, 2)
    token_count = teacher_unit.shape[0]

    def teacher_block(block):
        return jnp.exp(jnp.dot(teacher_unit, block, preferred_element_type=jnp.float32) / TEACHER_TEMP)
    row_scale = jnp.ones((token_count,), jnp.float32)
    col_scale = jnp.ones((block_count, block_width), jnp.float32)
    for sweep in range(ITERS):
        current_rows = row_scale

        def column_mass(block):
            return jnp.dot(current_rows, teacher_block(block), precision=lax.Precision.HIGHEST)
        col_scale = 1.0 / lax.map(column_mass, blocks)

        def add_rows(total, item):
            block, scales = item
            return (total + jnp.dot(teacher_block(block), scales, precision=lax.Precision.HIGHEST), None)
        row_total, unused = lax.scan(add_rows, jnp.zeros((token_count,), jnp.float32), (blocks, col_scale))
        row_scale = 1.0 / row_total

    def add_student(total, block):
        cosine = jnp.dot(student_unit, block, preferred_element_type=jnp.float32)
        return (total + lax.optimization_barrier(jnp.sum(jnp.exp(cosine / STUDENT_TEMP), axis=1)), None)
    mass, unused = lax.scan(add_student, jnp.zeros((token_count,), jnp.float32), blocks)

    def final_block(total, item):
        block, scales = item
        targets = row_scale[:, None] * teacher_block(block) * scales[None, :]
        cosine = jnp.dot(student_unit, block, preferred_element_type=jnp.float32)
        probs = jnp.exp(cosine / STUDENT_TEMP) / mass[:, None]
        diff = ((probs - targets) / STUDENT_TEMP).astype(jnp.bfloat16)
        total = total + jnp.dot(diff, block.T, preferred_element_type=jnp.float32)
        proto_part = lax.dot_general(student_unit, diff, (((0,), (0,)), ((), ())), preferred_element_type=jnp.float32)
        return (total, proto_part)
    grad_z, proto_parts = lax.scan(final_block, jnp.zeros((token_count, D), jnp.float32), (blocks, col_scale))
    grad_pn = proto_parts.transpose(1, 0, 2).reshape(D, K)
    col_proj = lax.optimization_barrier(jnp.sum(proto_unit.astype(jnp.float32) * grad_pn, axis=0, keepdims=True))
    grad_protos = (grad_pn - proto_full * col_proj) / proto_norm
    row_proj = lax.optimization_barrier(jnp.sum(student_full * grad_z, axis=1, keepdims=True))
    grad_rows = (grad_z - student_full * row_proj) / student_norm
    image_index = jnp.arange(IMAGES, dtype=jnp.int32)[:, None]
    grad_student = jnp.zeros(teacher_feats.shape, jnp.float32)
    grad_student = grad_student.at[image_index, mask_index].set(grad_rows.reshape(IMAGES, MASKED, D))
    return (grad_student, grad_protos)
```

```python
import functools

import jax
import jax.numpy as jnp
from jax import lax
from jax.experimental import pallas as pl
from jax.experimental.pallas import tpu as pltpu
from jax.sharding import PartitionSpec as P

ITERS = 3
TEACHER_TEMP = 0.04
STUDENT_TEMP = 0.1
EPSILON = 1e-06
LANES = 128
Z = 8
RING = 16
WIDE = 256
MIB = 1024 * 1024
F32 = jnp.float32
BF16 = jnp.bfloat16

VMEM = pltpu.VMEM
Z_GROUPS = [[2 * z + c for z in range(Z)] for c in range(2)]
ROW_GROUPS = [[32 * z + i for i in range(32)] for z in range(Z)]


def whole():
    return pl.BlockSpec(memory_space=VMEM)


def params(vmem=24):
    return pltpu.CompilerParams(vmem_limit_bytes=vmem * MIB)


def one_hot_t(mask_row, patches, dtype):
    slots = mask_row.shape[1]
    patch = lax.broadcasted_iota(jnp.int32, (patches, slots), 0)
    return jnp.where(patch == mask_row, 1.0, 0.0).astype(dtype)


def prep_kernel(teacher_ref, student_ref, mask_ref, zt_ref, zs_ref, zsf_ref, norm_ref):
    images, patches, width = teacher_ref.shape
    slots = mask_ref.shape[1]
    for i in range(images):
        hot = one_hot_t(mask_ref[i : i + 1, :], patches, BF16)
        rows = pl.ds(i * slots, slots)

        def taken(ref):
            return lax.dot_general(
                hot, ref[i], (((0,), (0,)), ((), ())), preferred_element_type=F32
            )

        xt = taken(teacher_ref)
        t_norm = jnp.sqrt(jnp.sum(xt * xt, axis=1, keepdims=True) + EPSILON)
        zt_ref[rows, :] = (xt / t_norm).astype(BF16).astype(F32)
        xs = taken(student_ref)
        s_norm = jnp.sqrt(jnp.sum(xs * xs, axis=1, keepdims=True) + EPSILON)
        zsf = xs / s_norm
        zsf_ref[rows, :] = zsf
        zs_ref[rows, :] = zsf.astype(BF16).astype(F32)
        norm_ref[rows, :] = s_norm


def write_lanes(out_ref, value, copies, first=0):
    for i in range(value.shape[1] // LANES):
        piece = value[:, i * LANES : (i + 1) * LANES]
        for m in range(copies):
            out_ref[m, first + i : first + i + 1, :] = piece


def write_rows(out_ref, acc, first=0):
    for i in range(acc.shape[0] // LANES):
        piece = jnp.sum(acc[i * LANES : (i + 1) * LANES, :].T, axis=0, keepdims=True)
        for m in range(out_ref.shape[0]):
            out_ref[m, first + i : first + i + 1, :] = piece


def unit_protos(proto_ref):
    p = proto_ref[...].astype(F32)
    norm = jnp.sqrt(jnp.sum(p * p, axis=0, keepdims=True) + EPSILON)
    return p / norm, norm


def core_rows(where_ref, side, half):
    return pl.ds(pl.multiple_of(lax.rem(where_ref[0] + side, 2) * half, half), half)


def exp_kernel(
    where_ref, proto_ref, zt0_ref, zt1_ref, zs0_ref, zs1_ref,
    e_ref, s_ref, pn_ref, col_ref, mass_ref,
):
    step = pl.program_id(0)
    full, _ = unit_protos(proto_ref)
    unit = full.astype(BF16)
    columns = pl.ds(pl.multiple_of(step * WIDE, WIDE), WIDE)
    pn_ref[:, columns] = unit
    half = zt0_ref.shape[0]
    total = jnp.zeros((1, WIDE), F32)
    for side, (zt, zs) in enumerate(((zt0_ref, zs0_ref), (zt1_ref, zs1_ref))):
        rows = core_rows(where_ref, side, half)
        e = jnp.exp(
            jnp.dot(zt[...].astype(BF16), unit, preferred_element_type=F32)
            * (1.0 / TEACHER_TEMP)
        )
        e_ref[rows, columns] = e
        total += jnp.sum(e, axis=0, keepdims=True)
        s = jnp.exp(
            jnp.dot(zs[...].astype(BF16), unit, preferred_element_type=F32)
            * (1.0 / STUDENT_TEMP)
        )
        s_ref[rows, columns] = s
        part = sum(s[:, j * LANES : (j + 1) * LANES] for j in range(WIDE // LANES))

        @pl.when(step == 0)
        def _():
            mass_ref[rows, :] = part

        @pl.when(step > 0)
        def _():
            mass_ref[rows, :] += part

    for i in range(WIDE // LANES):
        piece = total[:, i * LANES : (i + 1) * LANES]
        for m in range(Z):
            col_ref[m, pl.ds(step * (WIDE // LANES) + i, 1), :] = piece


def row_sums(e_ref, c, acc_ref):
    tiles = c.shape[0]
    block = 64

    def body(b, carry):
        rows = pl.ds(pl.multiple_of(b * block, block), block)
        acc = jnp.zeros((block, LANES), F32)
        for j in range(tiles):
            acc += e_ref[rows, j * LANES : (j + 1) * LANES] * c[j : j + 1, :]
        acc_ref[rows, :] = acc
        return carry

    lax.fori_loop(0, e_ref.shape[0] // block, body, 0)


def row_kernel(e_ref, parts_ref, out_ref, c_ref, acc_ref):
    c = 1.0 / jnp.sum(parts_ref[...], axis=0)
    c_ref[...] = c
    row_sums(e_ref, c, acc_ref)
    write_rows(out_ref, acc_ref[...])


def row_mass_kernel(e_ref, parts_ref, mass_ref, out_ref, c_ref, acc_ref):
    row_kernel(e_ref, parts_ref, out_ref, c_ref, acc_ref)
    write_rows(out_ref, mass_ref[...], first=8)


def spread(ref, value):
    for i in range(value.shape[0]):
        ref[i * LANES : (i + 1) * LANES, :] = jnp.broadcast_to(
            value[i : i + 1, :], (LANES, LANES)
        ).T


def col_kernel(e_ref, parts_ref, out_ref, r_ref):
    spread(r_ref, 1.0 / jnp.sum(parts_ref[:, :8, :], axis=0))
    width = e_ref.shape[1]
    block = 32

    def body(b, acc):
        rows = pl.ds(pl.multiple_of(b * block, block), block)
        r = r_ref[rows, :]
        out = []
        for j in range(width // LANES):
            value = acc[j]
            tile = e_ref[rows, j * LANES : (j + 1) * LANES] * r
            for g in range(block // 8):
                value = value + tile[g * 8 : (g + 1) * 8, :]
            out.append(value)
        return tuple(out)

    zero = tuple(jnp.zeros((8, LANES), F32) for _ in range(width // LANES))
    acc = lax.fori_loop(0, e_ref.shape[0] // block, body, zero)
    for j in range(width // LANES):
        piece = jnp.sum(acc[j], axis=0, keepdims=True)
        for m in range(Z):
            out_ref[m, j : j + 1, :] = piece


def grad_kernel(
    where_ref, proto_ref, e_ref, s_ref, pn_ref, zs0_ref, zs1_ref, c_ref, parts_ref, mass_ref,
    gz_ref, rel0, rel1, rel2, rel3, rel4, rel5, rel6, rel7, r_ref, m_ref, g_ref,
):
    step = pl.program_id(0)
    outs = (rel0, rel1, rel2, rel3, rel4, rel5, rel6, rel7)

    @pl.when(step == 0)
    def _():
        spread(r_ref, 1.0 / jnp.sum(parts_ref[...], axis=0))
        spread(m_ref, 1.0 / jnp.sum(mass_ref[:, 8:, :], axis=0))

    full, norm = unit_protos(proto_ref)
    columns = pl.ds(pl.multiple_of(step * WIDE, WIDE), WIDE)
    unit = pn_ref[:, columns]
    half = zs0_ref.shape[0]
    scale = 1.0 / STUDENT_TEMP
    grad = jnp.zeros((unit.shape[0], WIDE), F32)
    for side, zs in enumerate((zs0_ref, zs1_ref)):
        rows = core_rows(where_ref, side, half)
        pieces = []
        for j in range(WIDE // LANES):
            lanes = pl.ds(pl.multiple_of(step * WIDE + j * LANES, LANES), LANES)
            c = c_ref[pl.ds(step * (WIDE // LANES) + j, 1), :]
            targets = (r_ref[rows, :] * e_ref[rows, lanes]) * c
            probs = s_ref[rows, lanes] * m_ref[rows, :]
            pieces.append(((probs - targets) * scale).astype(BF16))
        diff = jnp.concatenate(pieces, axis=1)
        grad += lax.dot_general(
            zs[...].astype(BF16), diff, (((0,), (0,)), ((), ())), preferred_element_type=F32
        )
        part = lax.dot_general(
            diff, unit, (((1,), (1,)), ((), ())), preferred_element_type=F32
        )

        kept = pl.ds(side * half, half)

        @pl.when(step == 0)
        def _():
            gz_ref[kept, :] = part

        @pl.when(step > 0)
        def _():
            gz_ref[kept, :] += part

    proj = jnp.sum(unit.astype(F32) * grad, axis=0, keepdims=True)
    g_ref[...] = (grad - full * proj) / norm
    z = where_ref[1]
    deep = g_ref.shape[0] // Z
    for j, out in enumerate(outs):
        first = pl.multiple_of(lax.rem(z + j, Z) * deep, deep)
        out[:, columns] = g_ref[pl.ds(first, deep), :]


def last_kernel(gz_ref, zsf_ref, norm_ref, mask_ref, out_ref):
    images, patches, _ = out_ref.shape
    slots = mask_ref.shape[1]
    for i in range(images):
        rows = pl.ds(i * slots, slots)
        gz = gz_ref[rows, :]
        zsf = zsf_ref[rows, :]
        proj = jnp.sum(zsf * gz, axis=1, keepdims=True)
        grad = (gz - zsf * proj) / norm_ref[rows, :]
        hot = one_hot_t(mask_ref[i : i + 1, :], patches, F32)
        out_ref[i] = jnp.dot(
            hot, grad, precision=lax.Precision.HIGHEST, preferred_element_type=F32
        )


def shape(*dims, dtype=F32):
    return jax.ShapeDtypeStruct(dims, dtype)


def hold(*dims, dtype=F32):
    return pltpu.VMEM(dims, dtype)


def call(kernel, outs, *args, scratch=(), vmem=24):
    return pl.pallas_call(
        kernel,
        out_shape=outs,
        in_specs=[whole()] * len(args),
        out_specs=[whole()] * len(outs),
        scratch_shapes=list(scratch),
        compiler_params=params(vmem),
    )(*args)


def other_core(x):
    return lax.ppermute(x, "batch", [(i, i ^ 1) for i in range(RING)])


def along_z(x, d):
    return lax.ppermute(
        x, "batch", [(i, ((i // 2 + d) % Z) * 2 + i % 2) for i in range(RING)]
    )


def all_columns(x):
    return lax.all_to_all(x, "batch", 0, 0, axis_index_groups=Z_GROUPS)


def all_rows(x):
    return lax.all_to_all(x, ("batch", "proto"), 0, 0, axis_index_groups=ROW_GROUPS)


def ring_sum(rel):
    deep = rel[0].shape[0]
    near = deep // 2
    up = along_z(rel[4][:near], 1)
    down = along_z(rel[4][near:], -1)
    up = jnp.concatenate([rel[3][:near] + up, rel[3][near:]])
    down = jnp.concatenate([rel[5][:near], rel[5][near:] + down])
    for j in (2, 1, 0):
        up = along_z(up, 1)
        down = along_z(down, -1)
        if j:
            up = rel[j] + up
            down = rel[8 - j] + down
    return rel[0] + up + down


def on_device(teacher_feats, student_feats, prototypes, mask_index):
    images, patches, width = teacher_feats.shape
    own = images * mask_index.shape[1]
    tokens = 2 * own
    wide = prototypes.shape[1] // 2
    steps = wide // WIDE
    place = lax.axis_index("batch")
    where = jnp.stack([lax.rem(place, 2), lax.div(place, 2)]).astype(jnp.int32)

    zt, zs, zsf, s_norm = call(
        prep_kernel,
        [shape(own, width), shape(own, width), shape(own, width), shape(own, 1)],
        teacher_feats, student_feats, mask_index,
    )
    zt_other = other_core(zt)
    zs_other = other_core(zs)

    proto_spec = pl.BlockSpec((width, WIDE), lambda j, w: (0, w[0] * steps + j))
    e, s, unit, col_out, mass_acc = pl.pallas_call(
        exp_kernel,
        grid_spec=pltpu.PrefetchScalarGridSpec(
            num_scalar_prefetch=1,
            grid=(steps,),
            in_specs=[proto_spec] + [whole()] * 4,
            out_specs=[whole()] * 5,
        ),
        out_shape=[
            hold(tokens, wide), hold(tokens, wide), hold(width, wide, dtype=BF16),
            shape(Z, wide // LANES, LANES), shape(tokens, LANES),
        ],
        compiler_params=params(),
    )(where, prototypes, zt, zt_other, zs, zs_other)

    r_rows = tokens // LANES
    mass = None
    for sweep in range(ITERS):
        col_parts = all_columns(col_out)
        if sweep == 0:
            row_out, c = call(
                row_mass_kernel,
                [shape(32, 2 * r_rows, LANES), shape(wide // LANES, LANES)],
                e, col_parts, mass_acc,
                scratch=[VMEM((tokens, LANES), F32)],
            )
        else:
            row_out, c = call(
                row_kernel,
                [shape(32, r_rows, LANES), shape(wide // LANES, LANES)],
                e, col_parts,
                scratch=[VMEM((tokens, LANES), F32)],
            )
        row_parts = all_rows(row_out)
        if sweep == 0:
            mass = row_parts
        if sweep < ITERS - 1:
            (col_out,) = call(
                col_kernel, [shape(Z, wide // LANES, LANES)], e, row_parts,
                scratch=[VMEM((tokens, LANES), F32)],
            )

    deep = width // Z
    gz, *rel = pl.pallas_call(
        grad_kernel,
        grid_spec=pltpu.PrefetchScalarGridSpec(
            num_scalar_prefetch=1,
            grid=(steps,),
            in_specs=[proto_spec] + [whole()] * 8,
            out_specs=[whole()] * 9,
            scratch_shapes=[
                VMEM((tokens, LANES), F32), VMEM((tokens, LANES), F32), VMEM((width, WIDE), F32),
            ],
        ),
        out_shape=[shape(tokens, width)] + [shape(deep, wide)] * 8,
        compiler_params=params(),
    )(where, prototypes, e, s, unit, zs, zs_other, c, row_parts, mass)

    gz = gz[:own] + other_core(gz[own:])
    gz = jnp.sum(lax.all_to_all(gz.reshape(RING, own // RING, width), "proto", 0, 0), axis=0)
    gz = lax.all_to_all(
        jnp.broadcast_to(gz[None], (RING, own // RING, width)), "proto", 0, 0
    ).reshape(own, width)
    (grad_student,) = call(
        last_kernel, [shape(images, patches, width)], gz, zsf, s_norm, mask_index
    )

    done = ring_sum(rel)
    core = where[0]
    keep = lax.dynamic_slice_in_dim(done, core * (deep // 2), deep // 2, 0)
    give = lax.dynamic_slice_in_dim(done, (1 - core) * (deep // 2), deep // 2, 0)
    got = other_core(give)
    grad_protos = jnp.where(
        core == 0, jnp.concatenate([keep, got], axis=1), jnp.concatenate([got, keep], axis=1)
    )
    return (grad_student, grad_protos)


def solution(mesh):
    in_specs = (P("batch", None, None), P("batch", None, None), P(None, "proto"), P("batch", None))
    out_specs = (P("batch", None, None), P("batch", "proto"))
    return jax.shard_map(
        on_device, mesh=mesh, in_specs=in_specs, out_specs=out_specs, check_vma=False
    )
```

```python
import jax
import jax.numpy as jnp
from jax import lax
from jax.experimental import pallas as pl
from jax.experimental.pallas import tpu as pltpu
from jax.sharding import PartitionSpec as P

ITERS = 3
TEACHER_TEMP = 0.04
STUDENT_TEMP = 0.1
EPSILON = 1e-06
LANES = 128
Z = 8
RING = 16
ROWS = 32
WIDE = 256
MIB = 1024 * 1024
F32 = jnp.float32
BF16 = jnp.bfloat16

VMEM = pltpu.VMEM
Z_GROUPS = [[2 * z + c for z in range(Z)] for c in range(2)]
ROW_GROUPS = [[ROWS * z + i for i in range(ROWS)] for z in range(Z)]


def whole():
    return pl.BlockSpec(memory_space=VMEM)


def cost(flops, transcendentals=0, moved=0):
    return pl.CostEstimate(
        flops=flops, transcendentals=transcendentals, bytes_accessed=moved
    )


def params(vmem):
    return pltpu.CompilerParams(vmem_limit_bytes=vmem * MIB)


def call(kernel, outs, *args, scratch=(), vmem=16, cost_estimate=None):
    return pl.pallas_call(
        kernel,
        out_shape=outs,
        in_specs=[whole()] * len(args),
        out_specs=[whole()] * len(outs),
        scratch_shapes=list(scratch),
        compiler_params=params(vmem),
        cost_estimate=cost_estimate,
    )(*args)


def one_hot_t(mask_row, patches, dtype):
    slots = mask_row.shape[1]
    patch = lax.broadcasted_iota(jnp.int32, (patches, slots), 0)
    return jnp.where(patch == mask_row, 1.0, 0.0).astype(dtype)


def masked_rows(feats_ref, mask_ref):
    hot = one_hot_t(mask_ref[0], feats_ref.shape[1], BF16)
    rows = lax.dot_general(
        hot, feats_ref[0], (((0,), (0,)), ((), ())), preferred_element_type=F32
    )
    return rows, jnp.sqrt(jnp.sum(rows * rows, axis=1, keepdims=True) + EPSILON)


def teacher_kernel(feats_ref, mask_ref, unit_ref):
    rows, norm = masked_rows(feats_ref, mask_ref)
    unit_ref[...] = (rows / norm).astype(BF16).astype(F32)


def student_kernel(feats_ref, mask_ref, unit_ref, full_ref, norm_ref):
    rows, norm = masked_rows(feats_ref, mask_ref)
    full = rows / norm
    full_ref[...] = full
    unit_ref[...] = full.astype(BF16).astype(F32)
    norm_ref[...] = norm


def core_rows(where_ref, side, half):
    return pl.ds(pl.multiple_of(lax.rem(where_ref[0] + side, 2) * half, half), half)


def write_lanes(out_ref, value, row, copies):
    for m in range(copies):
        out_ref[m, pl.ds(row, 1), :] = value


def write_rows(out_ref, acc_ref):
    pieces = []
    for i in range(acc_ref.shape[0] // LANES):
        tile = acc_ref[i * LANES : (i + 1) * LANES, :].T
        pieces.append(jnp.sum(tile, axis=0, keepdims=True))
    value = jnp.concatenate(pieces, axis=0)
    for m in range(out_ref.shape[0]):
        out_ref[m] = value


def teacher_exp_kernel(
    where_ref, proto_ref, own_ref, other_ref, e_ref, full_ref, norm_ref, col_ref, rows_ref
):
    step = pl.program_id(0)
    half = own_ref.shape[0]

    @pl.when(step == 0)
    def _():
        rows_ref[core_rows(where_ref, 0, half), :] = own_ref[...].astype(BF16)
        rows_ref[core_rows(where_ref, 1, half), :] = other_ref[...].astype(BF16)

    p = proto_ref[...].astype(F32)
    norm = jnp.sqrt(jnp.sum(p * p, axis=0, keepdims=True) + EPSILON)
    full = p / norm
    unit = full.astype(BF16)
    columns = pl.ds(pl.multiple_of(step * WIDE, WIDE), WIDE)
    full_ref[:, columns] = full
    norm_ref[:, columns] = norm
    total = jnp.zeros((8, WIDE), F32)
    block = 128
    for b in range(rows_ref.shape[0] // block):
        rows = pl.ds(b * block, block)
        e = jnp.exp(
            jnp.dot(rows_ref[rows, :], unit, preferred_element_type=F32) * (1.0 / TEACHER_TEMP)
        )
        e_ref[rows, columns] = e
        for g in range(block // 8):
            total += e[g * 8 : (g + 1) * 8, :]
    total = jnp.sum(total, axis=0, keepdims=True)
    for i in range(WIDE // LANES):
        write_lanes(
            col_ref, total[:, i * LANES : (i + 1) * LANES], step * (WIDE // LANES) + i, Z
        )


def student_exp_kernel(
    where_ref, full_ref, own_ref, other_ref, s_ref, mass_ref, turned_ref, rows_ref, acc_ref
):
    step = pl.program_id(0)
    half = own_ref.shape[0]

    @pl.when(step == 0)
    def _():
        for side, ref in enumerate((own_ref, other_ref)):
            rows = core_rows(where_ref, side, half)
            rows_ref[rows, :] = ref[...].astype(BF16)
            turned_ref[:, rows] = ref[...].T.astype(BF16)
        acc_ref[...] = jnp.zeros_like(acc_ref)

    columns = pl.ds(pl.multiple_of(step * WIDE, WIDE), WIDE)
    unit = full_ref[:, columns].astype(BF16)
    block = 128
    for b in range(rows_ref.shape[0] // block):
        rows = pl.ds(b * block, block)
        s = jnp.exp(
            jnp.dot(rows_ref[rows, :], unit, preferred_element_type=F32) * (1.0 / STUDENT_TEMP)
        )
        s_ref[rows, columns] = s
        acc_ref[rows, :] += sum(s[:, j * LANES : (j + 1) * LANES] for j in range(WIDE // LANES))

    @pl.when(step == pl.num_programs(0) - 1)
    def _():
        write_rows(mass_ref, acc_ref)


def row_kernel(e_ref, parts_ref, out_ref, c_ref, acc_ref):
    c = 1.0 / jnp.sum(parts_ref[...], axis=0)
    c_ref[...] = c
    tiles = c.shape[0]
    block = 64

    def body(b, carry):
        rows = pl.ds(pl.multiple_of(b * block, block), block)
        acc = jnp.zeros((block, LANES), F32)
        for j in range(tiles):
            acc += e_ref[rows, j * LANES : (j + 1) * LANES] * c[j : j + 1, :]
        acc_ref[rows, :] = acc
        return carry

    lax.fori_loop(0, e_ref.shape[0] // block, body, 0)
    write_rows(out_ref, acc_ref)


def spread(ref, value):
    for i in range(value.shape[0]):
        ref[i * LANES : (i + 1) * LANES, :] = jnp.broadcast_to(
            value[i : i + 1, :], (LANES, LANES)
        ).T


def col_kernel(e_ref, parts_ref, out_ref, r_ref):
    spread(r_ref, 1.0 / jnp.sum(parts_ref[...], axis=0))
    tiles = e_ref.shape[1] // LANES
    block = 32

    def body(b, acc):
        rows = pl.ds(pl.multiple_of(b * block, block), block)
        r = r_ref[rows, :]
        out = []
        for j in range(tiles):
            value = acc[j]
            tile = e_ref[rows, j * LANES : (j + 1) * LANES] * r
            for g in range(block // 8):
                value = value + tile[g * 8 : (g + 1) * 8, :]
            out.append(value)
        return tuple(out)

    zero = tuple(jnp.zeros((8, LANES), F32) for _ in range(tiles))
    acc = lax.fori_loop(0, e_ref.shape[0] // block, body, zero)
    value = jnp.concatenate([jnp.sum(a, axis=0, keepdims=True) for a in acc], axis=0)
    for m in range(Z):
        out_ref[m] = value


def diff_kernel(part):
    def kernel(
        where_ref, e_ref, s_ref, full_ref, norm_ref, turned_ref, c_ref, parts_ref, mass_ref,
        diff_ref, rel0, rel1, rel2, rel3, rel4, rel5, rel6, rel7, r_ref, m_ref, g_ref,
    ):
        step = pl.program_id(0)
        outs = (rel0, rel1, rel2, rel3, rel4, rel5, rel6, rel7)

        @pl.when(step == 0)
        def _():
            spread(r_ref, 1.0 / jnp.sum(parts_ref[...], axis=0))
            spread(m_ref, 1.0 / jnp.sum(mass_ref[...], axis=0))

        first = part * rel0.shape[1] + step * WIDE
        columns = pl.ds(pl.multiple_of(first, WIDE), WIDE)
        here = pl.ds(pl.multiple_of(step * WIDE, WIDE), WIDE)
        block = 128
        for j in range(WIDE // LANES):
            lanes = pl.ds(pl.multiple_of(first + j * LANES, LANES), LANES)
            inside = pl.ds(pl.multiple_of(step * WIDE + j * LANES, LANES), LANES)
            tile = part * (rel0.shape[1] // LANES) + step * (WIDE // LANES) + j
            c = c_ref[pl.ds(tile, 1), :]
            for b in range(e_ref.shape[0] // block):
                rows = pl.ds(b * block, block)
                targets = (r_ref[rows, :] * e_ref[rows, lanes]) * c
                probs = s_ref[rows, lanes] * m_ref[rows, :]
                diff_ref[rows, inside] = ((probs - targets) * (1.0 / STUDENT_TEMP)).astype(BF16)
        grad = jnp.dot(turned_ref[...], diff_ref[:, here], preferred_element_type=F32)
        full = full_ref[:, columns]
        proj = jnp.sum(full.astype(BF16).astype(F32) * grad, axis=0, keepdims=True)
        g_ref[...] = (grad - full * proj) / norm_ref[:, columns]
        core, z = where_ref[0], where_ref[1]
        deep = g_ref.shape[0] // Z
        near = deep // 2
        for j, out in enumerate(outs):
            top = lax.rem(z + j, Z) * deep
            for side in range(2):
                take = pl.multiple_of(top + lax.rem(core + side, 2) * near, near)
                out[side * near : (side + 1) * near, here] = g_ref[pl.ds(take, near), :]

    return kernel


def token_grad_kernel(diff0_ref, diff1_ref, full_ref, out_ref):
    half = diff0_ref.shape[1]
    block = out_ref.shape[1]
    dims = (((1,), (1,)), ((), ()))
    unit0 = full_ref[:, :half].astype(BF16)
    unit1 = full_ref[:, half:].astype(BF16)
    for m in range(out_ref.shape[0] // 8):
        rows = pl.ds(m * 8 * block, 8 * block)
        grad = lax.dot_general(diff0_ref[rows, :], unit0, dims, preferred_element_type=F32)
        grad += lax.dot_general(diff1_ref[rows, :], unit1, dims, preferred_element_type=F32)
        for i in range(8):
            out_ref[m * 8 + i] = grad[i * block : (i + 1) * block, :]


def share_kernel(parts_ref, out_ref):
    total = jnp.sum(parts_ref[...], axis=0)
    for m in range(out_ref.shape[0]):
        out_ref[m] = total


def last_kernel(gz_ref, zsf_ref, norm_ref, mask_ref, out_ref):
    zsf = zsf_ref[...]
    gz = gz_ref[...]
    proj = jnp.sum(zsf * gz, axis=1, keepdims=True)
    grad = (gz - zsf * proj) / norm_ref[...]
    hot = one_hot_t(mask_ref[0], out_ref.shape[1], BF16)
    total = jnp.zeros(out_ref.shape[1:], F32)
    for _ in range(3):
        piece = grad.astype(BF16)
        total += jnp.dot(hot, piece, preferred_element_type=F32)
        grad = grad - piece.astype(F32)
    out_ref[0] = total


def first_sum_kernel(rel_ref, got_ref, top_ref):
    near = got_ref.shape[0]
    top_ref[:near, :] = rel_ref[:near, :] + got_ref[...]
    top_ref[near:, :] = rel_ref[near:, :]


def first_sum_low_kernel(rel_ref, got_ref, top_ref):
    near = got_ref.shape[0]
    top_ref[:near, :] = rel_ref[:near, :]
    top_ref[near:, :] = rel_ref[near:, :] + got_ref[...]


def sum_kernel(rel_ref, got_ref, out_ref):
    out_ref[...] = rel_ref[...] + got_ref[...]


def last_sum_kernel(rel_ref, up_ref, down_ref, keep_ref, give_ref):
    near = keep_ref.shape[0]
    keep_ref[...] = rel_ref[:near, :] + up_ref[:near, :] + down_ref[:near, :]
    give_ref[...] = rel_ref[near:, :] + up_ref[near:, :] + down_ref[near:, :]


def place_kernel(where_ref, keep0_ref, keep1_ref, got0_ref, got1_ref, out_ref):
    core = where_ref[0]
    half = keep0_ref.shape[1]
    for side, pair in enumerate(((keep0_ref, keep1_ref), (got0_ref, got1_ref))):
        first = lax.rem(core + side, 2) * 2 * half
        for i, ref in enumerate(pair):
            out_ref[:, pl.ds(pl.multiple_of(first + i * half, half), half)] = ref[...]


def shape(*dims, dtype=F32):
    return jax.ShapeDtypeStruct(dims, dtype)


def hold(*dims, dtype=F32):
    return pltpu.VMEM(dims, dtype)


def other_core(x):
    return lax.ppermute(x, "batch", [(i, i ^ 1) for i in range(RING)])


def along_z(x, d):
    return lax.ppermute(
        x, "batch", [(i, ((i // 2 + d) % Z) * 2 + i % 2) for i in range(RING)]
    )


def all_columns(x):
    return lax.all_to_all(x, "batch", 0, 0, axis_index_groups=Z_GROUPS)


def all_rows(x):
    return lax.all_to_all(x, ("batch", "proto"), 0, 0, axis_index_groups=ROW_GROUPS)


def tie(x, y):
    return lax.optimization_barrier((x, y))[0]


def on_device(teacher_feats, student_feats, prototypes, mask_index):
    images, patches, width = teacher_feats.shape
    slots = mask_index.shape[1]
    own = images * slots
    tokens = 2 * own
    wide = prototypes.shape[1] // 2
    steps = wide // WIDE
    lane_tiles = wide // LANES
    place = lax.axis_index("batch")
    where = jnp.stack([lax.rem(place, 2), lax.div(place, 2)]).astype(jnp.int32)
    mask = mask_index.reshape(images, 1, slots)

    feats_spec = pl.BlockSpec((1, patches, width), lambda i: (i, 0, 0))
    mask_spec = pl.BlockSpec((1, 1, slots), lambda i: (i, 0, 0))
    rows_spec = pl.BlockSpec((slots, width), lambda i: (i, 0))
    norm_spec = pl.BlockSpec((slots, 1), lambda i: (i, 0))
    zt = pl.pallas_call(
        teacher_kernel,
        grid=(images,),
        in_specs=[feats_spec, mask_spec],
        out_specs=rows_spec,
        out_shape=shape(own, width),
        compiler_params=params(16),
    )(teacher_feats, mask)
    zt_other = other_core(zt)
    zs, zsf, s_norm = pl.pallas_call(
        student_kernel,
        grid=(images,),
        in_specs=[feats_spec, mask_spec],
        out_specs=[rows_spec, rows_spec, norm_spec],
        out_shape=[shape(own, width), shape(own, width), shape(own, 1)],
        compiler_params=params(16),
    )(student_feats, mask)
    zs_other = other_core(zs)

    e, full, p_norm, col_out = pl.pallas_call(
        teacher_exp_kernel,
        grid_spec=pltpu.PrefetchScalarGridSpec(
            num_scalar_prefetch=1,
            grid=(steps,),
            in_specs=[pl.BlockSpec((width, WIDE), lambda j, w: (0, w[0] * steps + j))]
            + [whole()] * 2,
            out_specs=[whole()] * 4,
            scratch_shapes=[VMEM((tokens, width), BF16)],
        ),
        out_shape=[
            hold(tokens, wide), hold(width, wide), hold(1, wide), shape(Z, lane_tiles, LANES),
        ],
        compiler_params=params(16),
        cost_estimate=cost(2 * tokens * wide * width, tokens * wide),
    )(where, prototypes, zt, zt_other)

    s, mass_out, turned = pl.pallas_call(
        student_exp_kernel,
        grid_spec=pltpu.PrefetchScalarGridSpec(
            num_scalar_prefetch=1,
            grid=(steps,),
            in_specs=[whole()] * 3,
            out_specs=[whole()] * 3,
            scratch_shapes=[VMEM((tokens, width), BF16), VMEM((tokens, LANES), F32)],
        ),
        out_shape=[
            hold(tokens, wide), shape(ROWS, tokens // LANES, LANES),
            hold(width, tokens, dtype=BF16),
        ],
        compiler_params=params(16),
        cost_estimate=cost(2 * tokens * wide * width, tokens * wide),
    )(where, full, zs, zs_other)

    mass = None
    for sweep in range(ITERS):
        col_parts = all_columns(col_out)
        if sweep == 0:
            col_parts, mass_out = lax.optimization_barrier((col_parts, mass_out))
            mass = all_rows(mass_out)
        row_out, c = call(
            row_kernel,
            [shape(ROWS, tokens // LANES, LANES), shape(lane_tiles, LANES)],
            e, col_parts,
            scratch=[VMEM((tokens, LANES), F32)],
        )
        row_parts = all_rows(row_out)
        if sweep < ITERS - 1:
            (col_out,) = call(
                col_kernel, [shape(Z, lane_tiles, LANES)], e, row_parts,
                scratch=[VMEM((tokens, LANES), F32)],
            )

    deep = width // Z
    near = deep // 2
    half = wide // 2
    diffs, rels = [], []
    for part in range(2):
        diff, *rel = pl.pallas_call(
            diff_kernel(part),
            grid_spec=pltpu.PrefetchScalarGridSpec(
                num_scalar_prefetch=1,
                grid=(steps // 2,),
                in_specs=[whole()] * 8,
                out_specs=[whole()] * 9,
                scratch_shapes=[
                    VMEM((tokens, LANES), F32), VMEM((tokens, LANES), F32),
                    VMEM((width, WIDE), F32),
                ],
            ),
            out_shape=[hold(tokens, half, dtype=BF16)] + [hold(deep, half)] * 8,
            compiler_params=params(16),
            cost_estimate=cost(tokens * wide * width),
        )(where, e, s, full, p_norm, turned, c, row_parts, mass)
        diffs.append(diff)
        rels.append(rel)

    (gz_out,) = call(
        token_grad_kernel, [shape(ROWS, tokens // ROWS, width)], *diffs, full,
        cost_estimate=cost(2 * tokens * wide * width),
    )
    gz_parts = all_rows(gz_out)
    (gz_share,) = call(share_kernel, [shape(RING, own // RING, width)], gz_parts)
    gz = lax.all_to_all(gz_share, "proto", 0, 0).reshape(own, width)
    grad_student = pl.pallas_call(
        last_kernel,
        grid=(images,),
        in_specs=[rows_spec, rows_spec, norm_spec, mask_spec],
        out_specs=feats_spec,
        out_shape=shape(images, patches, width),
        compiler_params=params(16),
    )(gz, zsf, s_norm, mask)

    ups = [along_z(rel[4][:near], 1) for rel in rels]
    downs = [along_z(rel[4][near:], -1) for rel in rels]
    part_shape = [hold(deep, half)]
    ups = [along_z(call(first_sum_kernel, part_shape, r[3], u)[0], 1) for r, u in zip(rels, ups)]
    downs = [
        along_z(call(first_sum_low_kernel, part_shape, r[5], d)[0], -1)
        for r, d in zip(rels, downs)
    ]
    for j in (2, 1):
        ups = [along_z(call(sum_kernel, part_shape, r[j], u)[0], 1) for r, u in zip(rels, ups)]
        downs = [
            along_z(call(sum_kernel, part_shape, r[8 - j], d)[0], -1)
            for r, d in zip(rels, downs)
        ]
    keeps, gots = [], []
    for rel, up, down in zip(rels, ups, downs):
        keep, give = call(last_sum_kernel, [hold(near, half)] * 2, rel[0], up, down)
        keeps.append(keep)
        gots.append(other_core(give))
    grad_protos = pl.pallas_call(
        place_kernel,
        grid_spec=pltpu.PrefetchScalarGridSpec(
            num_scalar_prefetch=1,
            grid=(1,),
            in_specs=[whole()] * 4,
            out_specs=whole(),
        ),
        out_shape=shape(near, 2 * wide),
        compiler_params=params(16),
    )(where, *keeps, *gots)
    return (grad_student, grad_protos)


def solution(mesh):
    in_specs = (P("batch", None, None), P("batch", None, None), P(None, "proto"), P("batch", None))
    out_specs = (P("batch", None, None), P("batch", "proto"))
    return jax.shard_map(
        on_device, mesh=mesh, in_specs=in_specs, out_specs=out_specs, check_vma=False
    )
```

```python
import jax
import jax.numpy as jnp
from jax import lax
from jax.experimental import pallas as pl
from jax.experimental.pallas import tpu as pltpu
from jax.sharding import PartitionSpec as P

ITERS = 3
TEACHER_TEMP = 0.04
STUDENT_TEMP = 0.1
EPSILON = 1e-06
LANES = 128
Z = 8
RING = 16
ROWS = 32
WIDE = 1024
MIB = 1024 * 1024
F32 = jnp.float32
BF16 = jnp.bfloat16

VMEM = pltpu.VMEM
Z_GROUPS = [[2 * z + c for z in range(Z)] for c in range(2)]
ROW_GROUPS = [[ROWS * z + i for i in range(ROWS)] for z in range(Z)]


def whole():
    return pl.BlockSpec(memory_space=VMEM)


def cost(flops, transcendentals=0, moved=0):
    return pl.CostEstimate(
        flops=flops, transcendentals=transcendentals, bytes_accessed=moved
    )


def params(vmem):
    return pltpu.CompilerParams(vmem_limit_bytes=vmem * MIB)


def call(kernel, outs, *args, scratch=(), vmem=16, cost_estimate=None):
    return pl.pallas_call(
        kernel,
        out_shape=outs,
        in_specs=[whole()] * len(args),
        out_specs=[whole()] * len(outs),
        scratch_shapes=list(scratch),
        compiler_params=params(vmem),
        cost_estimate=cost_estimate,
    )(*args)


def one_hot_t(mask_row, patches, dtype):
    slots = mask_row.shape[1]
    patch = lax.broadcasted_iota(jnp.int32, (patches, slots), 0)
    return jnp.where(patch == mask_row, 1.0, 0.0).astype(dtype)


def fetch(pairs, sems):
    copies = [pltpu.make_async_copy(src, dst, sems.at[i]) for i, (src, dst) in enumerate(pairs)]
    for copy in copies:
        copy.start()
    return copies


def masked_rows(feats, mask_row):
    hot = one_hot_t(mask_row, feats.shape[0], BF16)
    rows = lax.dot_general(hot, feats, (((0,), (0,)), ((), ())), preferred_element_type=F32)
    return rows, jnp.sqrt(jnp.sum(rows * rows, axis=1, keepdims=True) + EPSILON)


def teacher_kernel(feats_hbm, mask_hbm, unit_ref, feats_ref, mask_ref, sems):
    for copy in fetch(((feats_hbm, feats_ref), (mask_hbm, mask_ref)), sems):
        copy.wait()
    slots = mask_ref.shape[1]
    for i in range(feats_ref.shape[0]):
        rows, norm = masked_rows(feats_ref[i], mask_ref[i : i + 1, :])
        unit_ref[i * slots : (i + 1) * slots, :] = (rows / norm).astype(BF16).astype(F32)


def student_kernel(
    feats_hbm, mask_hbm, unit_ref, full_ref, norm_ref, feats_ref, mask_ref, sems
):
    for copy in fetch(((feats_hbm, feats_ref), (mask_hbm, mask_ref)), sems):
        copy.wait()
    slots = mask_ref.shape[1]
    for i in range(feats_ref.shape[0]):
        take = pl.ds(i * slots, slots)
        rows, norm = masked_rows(feats_ref[i], mask_ref[i : i + 1, :])
        full = rows / norm
        full_ref[take, :] = full
        unit_ref[take, :] = full.astype(BF16).astype(F32)
        norm_ref[take, :] = norm


def proto_kernel(where_ref, proto_ref, full_ref, unit_ref, norm_ref):
    p = proto_ref[...].astype(F32)
    norm = jnp.sqrt(jnp.sum(p * p, axis=0, keepdims=True) + EPSILON)
    full = p / norm
    full_ref[...] = full
    unit_ref[...] = full.astype(BF16)
    norm_ref[...] = norm


def core_rows(where_ref, side, half):
    return pl.ds(pl.multiple_of(lax.rem(where_ref[0] + side, 2) * half, half), half)


def write_lanes(out_ref, value, row, copies):
    for m in range(copies):
        out_ref[m, pl.ds(row, 1), :] = value


def write_rows(out_ref, acc_ref, first=0):
    pieces = []
    for i in range(acc_ref.shape[0] // LANES):
        tile = acc_ref[i * LANES : (i + 1) * LANES, :].T
        pieces.append(jnp.sum(tile, axis=0, keepdims=True))
    value = jnp.concatenate(pieces, axis=0)
    for m in range(out_ref.shape[0]):
        out_ref[m, first : first + 8, :] = value


def teacher_exp_kernel(where_ref, own_ref, other_ref, unit_ref, e_ref, col_ref):
    half = own_ref.shape[0]
    wide = unit_ref.shape[1]
    block = 256
    for w in range(wide // WIDE):
        columns = pl.ds(w * WIDE, WIDE)
        unit = unit_ref[:, columns]
        total = jnp.zeros((8, WIDE), F32)
        for side, ref in enumerate((own_ref, other_ref)):
            place = core_rows(where_ref, side, half)
            for b in range(half // block):
                z = ref[b * block : (b + 1) * block, :].astype(BF16)
                e = jnp.exp(
                    jnp.dot(z, unit, preferred_element_type=F32) * (1.0 / TEACHER_TEMP)
                )
                e_ref[pl.ds(place.start + b * block, block), columns] = e
                for g in range(block // 8):
                    total += e[g * 8 : (g + 1) * 8, :]
        total = jnp.sum(total, axis=0, keepdims=True)
        for i in range(WIDE // LANES):
            write_lanes(
                col_ref, total[:, i * LANES : (i + 1) * LANES], w * (WIDE // LANES) + i, Z
            )


def student_exp_kernel(
    where_ref, own_ref, other_ref, unit_ref, s_ref, mass_ref, turned_ref
):
    half = own_ref.shape[0]
    wide = unit_ref.shape[1]
    block = 256
    for side, ref in enumerate((own_ref, other_ref)):
        turned_ref[:, core_rows(where_ref, side, half)] = ref[...].T.astype(BF16)
    for w in range(wide // WIDE):
        columns = pl.ds(w * WIDE, WIDE)
        unit = unit_ref[:, columns]
        for side, ref in enumerate((own_ref, other_ref)):
            place = core_rows(where_ref, side, half)
            for b in range(half // block):
                rows = pl.ds(place.start + b * block, block)
                z = ref[b * block : (b + 1) * block, :].astype(BF16)
                s = jnp.exp(
                    jnp.dot(z, unit, preferred_element_type=F32) * (1.0 / STUDENT_TEMP)
                )
                s_ref[rows, columns] = s
                part = sum(s[:, j * LANES : (j + 1) * LANES] for j in range(WIDE // LANES))
                if w:
                    mass_ref[rows, :] += part
                else:
                    mass_ref[rows, :] = part


def row_kernel(e_ref, parts_ref, out_ref, c_ref, acc_ref):
    c = 1.0 / jnp.sum(parts_ref[...], axis=0)
    c_ref[...] = c
    tiles = c.shape[0]
    block = 64

    def body(b, carry):
        rows = pl.ds(pl.multiple_of(b * block, block), block)
        acc = jnp.zeros((block, LANES), F32)
        for j in range(tiles):
            acc += e_ref[rows, j * LANES : (j + 1) * LANES] * c[j : j + 1, :]
        acc_ref[rows, :] = acc
        return carry

    lax.fori_loop(0, e_ref.shape[0] // block, body, 0)
    write_rows(out_ref, acc_ref)


def row_mass_kernel(e_ref, parts_ref, mass_ref, out_ref, c_ref, acc_ref):
    row_kernel(e_ref, parts_ref, out_ref, c_ref, acc_ref)
    write_rows(out_ref, mass_ref, first=8)


def spread(ref, value):
    for i in range(value.shape[0]):
        ref[i * LANES : (i + 1) * LANES, :] = jnp.broadcast_to(
            value[i : i + 1, :], (LANES, LANES)
        ).T


def col_kernel(e_ref, parts_ref, out_ref, r_ref):
    spread(r_ref, 1.0 / jnp.sum(parts_ref[:, :8, :], axis=0))
    tiles = e_ref.shape[1] // LANES
    block = 32

    def body(b, acc):
        rows = pl.ds(pl.multiple_of(b * block, block), block)
        r = r_ref[rows, :]
        out = []
        for j in range(tiles):
            value = acc[j]
            tile = e_ref[rows, j * LANES : (j + 1) * LANES] * r
            for g in range(block // 8):
                value = value + tile[g * 8 : (g + 1) * 8, :]
            out.append(value)
        return tuple(out)

    zero = tuple(jnp.zeros((8, LANES), F32) for _ in range(tiles))
    acc = lax.fori_loop(0, e_ref.shape[0] // block, body, zero)
    value = jnp.concatenate([jnp.sum(a, axis=0, keepdims=True) for a in acc], axis=0)
    for m in range(Z):
        out_ref[m] = value


def diff_kernel(part):
    def kernel(
        where_ref, e_ref, s_ref, full_ref, norm_ref, turned_ref, c_ref, parts_ref, mass_ref,
        diff_ref, rel0, rel1, rel2, rel3, rel4u, rel4d, rel5, rel6, rel7,
        r_ref, m_ref, g_ref,
    ):
        spread(r_ref, 1.0 / jnp.sum(parts_ref[...], axis=0))
        spread(m_ref, (1.0 / STUDENT_TEMP) / jnp.sum(mass_ref[:, 8:, :], axis=0))
        half = rel0.shape[1]
        tiles = half // LANES
        block = 16

        def body(b, carry):
            rows = pl.ds(pl.multiple_of(b * block, block), block)
            r = r_ref[rows, :] * (1.0 / STUDENT_TEMP)
            m = m_ref[rows, :]
            for j in range(tiles):
                tile = part * tiles + j
                lanes = slice(tile * LANES, (tile + 1) * LANES)
                targets = (r * e_ref[rows, lanes]) * c_ref[tile : tile + 1, :]
                probs = s_ref[rows, lanes] * m
                diff_ref[rows, j * LANES : (j + 1) * LANES] = (probs - targets).astype(BF16)
            return carry

        lax.fori_loop(0, e_ref.shape[0] // block, body, 0, unroll=2)
        columns = slice(part * half, (part + 1) * half)
        grad = jnp.dot(turned_ref[...], diff_ref[...], preferred_element_type=F32)
        full = full_ref[:, columns]
        proj = jnp.sum(full.astype(BF16).astype(F32) * grad, axis=0, keepdims=True)
        g_ref[...] = (grad - full * proj) / norm_ref[:, columns]
        core, z = where_ref[0], where_ref[1]
        deep = g_ref.shape[0] // Z
        near = deep // 2
        outs = (rel0, rel1, rel2, rel3, (rel4u, rel4d), rel5, rel6, rel7)
        for j, out in enumerate(outs):
            top = lax.rem(z + j, Z) * deep
            for side in range(2):
                take = pl.multiple_of(top + lax.rem(core + side, 2) * near, near)
                value = g_ref[pl.ds(take, near), :]
                if j == 4:
                    out[side][...] = value
                else:
                    out[side * near : (side + 1) * near, :] = value

    return kernel


def token_grad_kernel(where_ref, diff0_ref, diff1_ref, unit_ref, own_ref, other_ref):
    half = diff0_ref.shape[1]
    dims = (((1,), (1,)), ((), ()))
    unit0 = unit_ref[:, :half]
    unit1 = unit_ref[:, half:]
    for side, out in enumerate((own_ref, other_ref)):
        rows = core_rows(where_ref, side, out.shape[0])
        grad = lax.dot_general(diff0_ref[rows, :], unit0, dims, preferred_element_type=F32)
        out[...] = grad + lax.dot_general(
            diff1_ref[rows, :], unit1, dims, preferred_element_type=F32
        )


def share_kernel(parts_ref, out_ref):
    total = sum(parts_ref[i] for i in range(parts_ref.shape[0]))
    for m in range(out_ref.shape[0]):
        out_ref[m] = total


def last_kernel(gz_ref, zsf_ref, norm_ref, mask_ref, out_ref):
    slots = mask_ref.shape[1]
    for i in range(out_ref.shape[0]):
        rows = pl.ds(i * slots, slots)
        zsf = zsf_ref[rows, :]
        gz = gz_ref[rows, :]
        proj = jnp.sum(zsf * gz, axis=1, keepdims=True)
        grad = (gz - zsf * proj) / norm_ref[rows, :]
        hot = one_hot_t(mask_ref[i : i + 1, :], out_ref.shape[1], BF16)
        total = jnp.zeros(out_ref.shape[1:], F32)
        for _ in range(3):
            piece = grad.astype(BF16)
            total += jnp.dot(hot, piece, preferred_element_type=F32)
            grad = grad - piece.astype(F32)
        out_ref[i] = total


def first_sum_kernel(rel_ref, got_ref, top_ref):
    near = got_ref.shape[0]
    top_ref[:near, :] = rel_ref[:near, :] + got_ref[...]
    top_ref[near:, :] = rel_ref[near:, :]


def first_sum_low_kernel(rel_ref, got_ref, top_ref):
    near = got_ref.shape[0]
    top_ref[:near, :] = rel_ref[:near, :]
    top_ref[near:, :] = rel_ref[near:, :] + got_ref[...]


def sum_kernel(rel_ref, got_ref, out_ref):
    out_ref[...] = rel_ref[...] + got_ref[...]


def last_sum_kernel(rel_ref, up_ref, down_ref, keep_ref, give_ref):
    near = keep_ref.shape[0]
    keep_ref[...] = rel_ref[:near, :] + up_ref[:near, :] + down_ref[:near, :]
    give_ref[...] = rel_ref[near:, :] + up_ref[near:, :] + down_ref[near:, :]


def place_kernel(where_ref, keep0_ref, keep1_ref, got0_ref, got1_ref, out_ref):
    core = where_ref[0]
    half = keep0_ref.shape[1]
    for side, pair in enumerate(((keep0_ref, keep1_ref), (got0_ref, got1_ref))):
        first = lax.rem(core + side, 2) * 2 * half
        for i, ref in enumerate(pair):
            out_ref[:, pl.ds(pl.multiple_of(first + i * half, half), half)] = ref[...]


def shape(*dims, dtype=F32):
    return jax.ShapeDtypeStruct(dims, dtype)


def hold(*dims, dtype=F32):
    return pltpu.VMEM(dims, dtype)


def other_core(x):
    return lax.ppermute(x, "batch", [(i, i ^ 1) for i in range(RING)])


def along_z(x, d):
    return lax.ppermute(
        x, "batch", [(i, ((i // 2 + d) % Z) * 2 + i % 2) for i in range(RING)]
    )


def all_columns(x):
    return lax.all_to_all(x, "batch", 0, 0, axis_index_groups=Z_GROUPS)


def all_rows(x):
    return lax.all_to_all(x, ("batch", "proto"), 0, 0, axis_index_groups=ROW_GROUPS)


def tie(x, y):
    return lax.optimization_barrier((x, y))[0]


def on_device(teacher_feats, student_feats, prototypes, mask_index):
    images, patches, width = teacher_feats.shape
    slots = mask_index.shape[1]
    own = images * slots
    tokens = 2 * own
    wide = prototypes.shape[1] // 2
    lane_tiles = wide // LANES
    row_tiles = tokens // LANES
    place = lax.axis_index("batch")
    where = jnp.stack([lax.rem(place, 2), lax.div(place, 2)]).astype(jnp.int32)
    scalars = pl.BlockSpec(memory_space=pltpu.SMEM)

    def in_hbm(x):
        return pltpu.with_memory_space_constraint(x, pltpu.HBM)

    def prep(kernel, outs, feats):
        return pl.pallas_call(
            kernel,
            in_specs=[pl.BlockSpec(memory_space=pl.ANY)] * 2,
            out_specs=[whole()] * len(outs),
            out_shape=outs,
            scratch_shapes=[
                VMEM(feats.shape, BF16), VMEM(mask_index.shape, jnp.int32),
                pltpu.SemaphoreType.DMA((2,)),
            ],
            compiler_params=params(16),
        )(in_hbm(feats), in_hbm(mask_index))

    def placed(kernel, outs, *args, **kw):
        return pl.pallas_call(
            kernel,
            in_specs=[scalars] + [whole()] * len(args),
            out_specs=[whole()] * len(outs),
            out_shape=outs,
            scratch_shapes=kw.get("scratch", []),
            compiler_params=params(16),
            cost_estimate=kw.get("cost_estimate"),
        )(where, *args)

    (zt,) = prep(teacher_kernel, [shape(own, width)], teacher_feats)
    zt_other = other_core(zt)
    zs, zsf, s_norm = prep(
        student_kernel, [shape(own, width), shape(own, width), shape(own, 1)], student_feats
    )
    zs_other = other_core(zs)
    steps = 2
    column_spec = pl.BlockSpec((width, wide // steps), lambda j, w: (0, j))
    full, unit, p_norm = pl.pallas_call(
        proto_kernel,
        grid_spec=pltpu.PrefetchScalarGridSpec(
            num_scalar_prefetch=1,
            grid=(steps,),
            in_specs=[
                pl.BlockSpec((width, wide // steps), lambda j, w: (0, w[0] * steps + j))
            ],
            out_specs=[
                column_spec, column_spec,
                pl.BlockSpec((1, wide // steps), lambda j, w: (0, j)),
            ],
        ),
        out_shape=[shape(width, wide), shape(width, wide, dtype=BF16), shape(1, wide)],
        compiler_params=params(16),
    )(where, in_hbm(prototypes))

    exp_cost = cost(2 * tokens * wide * width, tokens * wide)
    e, col_out = placed(
        teacher_exp_kernel,
        [hold(tokens, wide), shape(Z, lane_tiles, LANES)],
        zt, zt_other, unit, cost_estimate=exp_cost,
    )
    s, mass_acc, turned = placed(
        student_exp_kernel,
        [hold(tokens, wide), shape(tokens, LANES), shape(width, tokens, dtype=BF16)],
        zs, zs_other, unit, cost_estimate=exp_cost,
    )
    col_out = tie(col_out, mass_acc)

    mass = None
    for sweep in range(ITERS):
        col_parts = all_columns(col_out)
        extra = [mass_acc] if sweep == 0 else []
        row_out, c = call(
            row_kernel if sweep else row_mass_kernel,
            [shape(ROWS, row_tiles * (1 + len(extra)), LANES), shape(lane_tiles, LANES)],
            e, col_parts, *extra,
            scratch=[VMEM((tokens, LANES), F32)],
        )
        row_parts = all_rows(row_out)
        if sweep == 0:
            mass = row_parts
        if sweep < ITERS - 1:
            (col_out,) = call(
                col_kernel, [shape(Z, lane_tiles, LANES)], e, row_parts,
                scratch=[VMEM((tokens, LANES), F32)],
            )

    deep = width // Z
    near = deep // 2
    half = wide // 2
    diffs, rels = [], []
    for part in range(2):
        diff, *rel = placed(
            diff_kernel(part),
            [shape(tokens, half, dtype=BF16)] + [shape(deep, half)] * 4
            + [shape(near, half)] * 2 + [shape(deep, half)] * 3,
            e, s, full, p_norm, turned, c, row_parts, mass,
            scratch=[
                VMEM((tokens, LANES), F32), VMEM((tokens, LANES), F32), VMEM((width, half), F32),
            ],
            cost_estimate=cost(tokens * wide * width),
        )
        diffs.append(diff)
        rels.append(rel)

    ups = [along_z(rel[4], 1) for rel in rels]
    downs = [along_z(rel[5], -1) for rel in rels]
    rels = [rel[:4] + [None] + rel[6:] for rel in rels]

    diff0 = tie(diffs[0], ups[0])
    gz, gz_give = placed(
        token_grad_kernel, [shape(own, width)] * 2, diff0, diffs[1], unit,
        cost_estimate=cost(2 * tokens * wide * width),
    )
    gz = gz + other_core(gz_give)
    gz_parts = lax.all_to_all(gz.reshape(RING, own // RING, width), "proto", 0, 0)
    (gz_share,) = call(share_kernel, [shape(RING, own // RING, width)], gz_parts)
    gz = lax.all_to_all(gz_share, "proto", 0, 0).reshape(own, width)
    (grad_student,) = call(
        last_kernel, [shape(images, patches, width)], gz, zsf, s_norm, mask_index
    )

    part_shape = [shape(deep, half)]
    ups = [along_z(call(first_sum_kernel, part_shape, r[3], u)[0], 1) for r, u in zip(rels, ups)]
    downs = [
        along_z(call(first_sum_low_kernel, part_shape, r[5], d)[0], -1)
        for r, d in zip(rels, downs)
    ]
    for j in (2, 1):
        ups = [along_z(call(sum_kernel, part_shape, r[j], u)[0], 1) for r, u in zip(rels, ups)]
        downs = [
            along_z(call(sum_kernel, part_shape, r[8 - j], d)[0], -1)
            for r, d in zip(rels, downs)
        ]
    keeps, gots = [], []
    for rel, up, down in zip(rels, ups, downs):
        keep, give = call(last_sum_kernel, [shape(near, half)] * 2, rel[0], up, down)
        keeps.append(keep)
        gots.append(other_core(give))
    (grad_protos,) = placed(place_kernel, [shape(near, 2 * wide)], *keeps, *gots)
    return (grad_student, grad_protos)


def solution(mesh):
    in_specs = (P("batch", None, None), P("batch", None, None), P(None, "proto"), P("batch", None))
    out_specs = (P("batch", None, None), P("batch", "proto"))
    return jax.shard_map(
        on_device, mesh=mesh, in_specs=in_specs, out_specs=out_specs, check_vma=False
    )
```

```python
import jax
import jax.numpy as jnp
from jax import lax
from jax.experimental import pallas as pl
from jax.experimental.pallas import tpu as pltpu
from jax.sharding import PartitionSpec as P

ITERS = 3
TEACHER_TEMP = 0.04
STUDENT_TEMP = 0.1
EPSILON = 1e-06
LANES = 128
Z = 8
RING = 16
ROWS = 32
WIDE = 1024
MIB = 1024 * 1024
F32 = jnp.float32
BF16 = jnp.bfloat16

VMEM = pltpu.VMEM
Z_GROUPS = [[2 * z + c for z in range(Z)] for c in range(2)]
ROW_GROUPS = [[ROWS * z + i for i in range(ROWS)] for z in range(Z)]


def whole():
    return pl.BlockSpec(memory_space=VMEM)


def cost(flops, transcendentals=0, moved=0):
    return pl.CostEstimate(
        flops=flops, transcendentals=transcendentals, bytes_accessed=moved
    )


def params(vmem):
    return pltpu.CompilerParams(vmem_limit_bytes=vmem * MIB)


def call(kernel, outs, *args, scratch=(), vmem=16, cost_estimate=None):
    return pl.pallas_call(
        kernel,
        out_shape=outs,
        in_specs=[whole()] * len(args),
        out_specs=[whole()] * len(outs),
        scratch_shapes=list(scratch),
        compiler_params=params(vmem),
        cost_estimate=cost_estimate,
    )(*args)


def one_hot_t(mask_row, patches, dtype):
    slots = mask_row.shape[1]
    patch = lax.broadcasted_iota(jnp.int32, (patches, slots), 0)
    return jnp.where(patch == mask_row, 1.0, 0.0).astype(dtype)


def fetch(pairs, sems):
    copies = [pltpu.make_async_copy(src, dst, sems.at[i]) for i, (src, dst) in enumerate(pairs)]
    for copy in copies:
        copy.start()
    return copies


def masked_rows(feats, mask_row):
    hot = one_hot_t(mask_row, feats.shape[0], BF16)
    rows = lax.dot_general(hot, feats, (((0,), (0,)), ((), ())), preferred_element_type=F32)
    return rows, jnp.sqrt(jnp.sum(rows * rows, axis=1, keepdims=True) + EPSILON)


def prep_kernel(
    teacher_hbm, student_hbm, mask_hbm, zt_ref, zs_ref, full_ref, norm_ref,
    teacher_ref, student_ref, mask_ref, sems,
):
    mask_copy, teacher_copy, student_copy = fetch(
        ((mask_hbm, mask_ref), (teacher_hbm, teacher_ref), (student_hbm, student_ref)), sems
    )
    mask_copy.wait()
    teacher_copy.wait()
    slots = mask_ref.shape[1]
    for i in range(teacher_ref.shape[0]):
        rows, norm = masked_rows(teacher_ref[i], mask_ref[i : i + 1, :])
        zt_ref[i * slots : (i + 1) * slots, :] = (rows / norm).astype(BF16).astype(F32)
    student_copy.wait()
    for i in range(student_ref.shape[0]):
        take = pl.ds(i * slots, slots)
        rows, norm = masked_rows(student_ref[i], mask_ref[i : i + 1, :])
        full = rows / norm
        full_ref[take, :] = full
        zs_ref[take, :] = full.astype(BF16).astype(F32)
        norm_ref[take, :] = norm


def proto_kernel(where_ref, proto_ref, full_ref, unit_ref, back_ref, norm_ref):
    p = proto_ref[...].astype(F32)
    norm = jnp.sqrt(jnp.sum(p * p, axis=0, keepdims=True) + EPSILON)
    full = p / norm
    full_ref[...] = full
    unit_ref[...] = full.astype(BF16)
    back_ref[...] = full.T.astype(BF16)
    norm_ref[...] = norm


def core_rows(where_ref, side, half):
    return pl.ds(pl.multiple_of(lax.rem(where_ref[0] + side, 2) * half, half), half)


def write_lanes(out_ref, value, row, copies):
    for m in range(copies):
        out_ref[m, pl.ds(row, 1), :] = value


def write_rows(out_ref, acc_ref, first=0):
    pieces = []
    for i in range(acc_ref.shape[0] // LANES):
        tile = acc_ref[i * LANES : (i + 1) * LANES, :].T
        pieces.append(jnp.sum(tile, axis=0, keepdims=True))
    value = jnp.concatenate(pieces, axis=0)
    for m in range(out_ref.shape[0]):
        out_ref[m, first : first + 8, :] = value


def teacher_exp_kernel(where_ref, own_ref, other_ref, unit_ref, e_ref, col_ref):
    half = own_ref.shape[0]
    wide = unit_ref.shape[1]
    block = 256
    for w in range(wide // WIDE):
        columns = pl.ds(w * WIDE, WIDE)
        unit = unit_ref[:, columns]
        total = jnp.zeros((8, WIDE), F32)
        for side, ref in enumerate((own_ref, other_ref)):
            place = core_rows(where_ref, side, half)
            for b in range(half // block):
                z = ref[b * block : (b + 1) * block, :].astype(BF16)
                e = jnp.exp(
                    jnp.dot(z, unit, preferred_element_type=F32) * (1.0 / TEACHER_TEMP)
                )
                e_ref[pl.ds(place.start + b * block, block), columns] = e
                for g in range(block // 8):
                    total += e[g * 8 : (g + 1) * 8, :]
        total = jnp.sum(total, axis=0, keepdims=True)
        for i in range(WIDE // LANES):
            write_lanes(
                col_ref, total[:, i * LANES : (i + 1) * LANES], w * (WIDE // LANES) + i, Z
            )


def student_exp_kernel(
    where_ref, own_ref, other_ref, unit_ref, back_ref,
    s_ref, mass_ref, turned_ref, pull_ref, give_ref,
):
    half = own_ref.shape[0]
    wide = unit_ref.shape[1]
    block = 256
    for side, ref in enumerate((own_ref, other_ref)):
        turned_ref[:, core_rows(where_ref, side, half)] = ref[...].T.astype(BF16)
    for w in range(wide // WIDE):
        columns = pl.ds(w * WIDE, WIDE)
        unit = unit_ref[:, columns]
        for side, ref in enumerate((own_ref, other_ref)):
            place = core_rows(where_ref, side, half)
            for b in range(half // block):
                rows = pl.ds(pl.multiple_of(place.start + b * block, block), block)
                z = ref[b * block : (b + 1) * block, :].astype(BF16)
                s = jnp.exp(
                    jnp.dot(z, unit, preferred_element_type=F32) * (1.0 / STUDENT_TEMP)
                )
                s_ref[rows, columns] = s.astype(BF16)
                part = sum(s[:, j * LANES : (j + 1) * LANES] for j in range(WIDE // LANES))
                if w:
                    mass_ref[rows, :] += part
                else:
                    mass_ref[rows, :] = part
    for side, out in enumerate((pull_ref, give_ref)):
        rows = core_rows(where_ref, side, half)
        out[...] = jnp.dot(s_ref[rows, :], back_ref[...], preferred_element_type=F32)


def row_kernel(e_ref, parts_ref, out_ref, c_ref, acc_ref):
    c = 1.0 / jnp.sum(parts_ref[...], axis=0)
    c_ref[...] = c
    tiles = c.shape[0]
    block = 64

    def body(b, carry):
        rows = pl.ds(pl.multiple_of(b * block, block), block)
        acc = jnp.zeros((block, LANES), F32)
        for j in range(tiles):
            acc += e_ref[rows, j * LANES : (j + 1) * LANES] * c[j : j + 1, :]
        acc_ref[rows, :] = acc
        return carry

    lax.fori_loop(0, e_ref.shape[0] // block, body, 0)
    write_rows(out_ref, acc_ref)


def row_mass_kernel(e_ref, parts_ref, mass_ref, out_ref, c_ref, acc_ref):
    row_kernel(e_ref, parts_ref, out_ref, c_ref, acc_ref)
    write_rows(out_ref, mass_ref, first=8)


def row_pull_kernel(
    where_ref, e_ref, parts_ref, back_ref, own_ref, give_ref, c_ref, acc_ref, weighted_ref
):
    c = 1.0 / jnp.sum(parts_ref[...], axis=0)
    c_ref[...] = c
    half = own_ref.shape[0]
    tiles = c.shape[0]
    block = 64

    def body(b, carry):
        rows = pl.ds(pl.multiple_of(b * block, block), block)
        acc = jnp.zeros((block, LANES), F32)
        for j in range(tiles):
            x = e_ref[rows, j * LANES : (j + 1) * LANES] * c[j : j + 1, :]
            acc += x
            weighted_ref[rows, j * LANES : (j + 1) * LANES] = x.astype(BF16)
        acc_ref[rows, :] = acc
        return carry

    lax.fori_loop(0, e_ref.shape[0] // block, body, 0)
    for side, out in enumerate((own_ref, give_ref)):
        rows = core_rows(where_ref, side, half)
        out[:half, :] = jnp.dot(
            weighted_ref[rows, :], back_ref[...], preferred_element_type=F32
        )
    for i in range(acc_ref.shape[0] // LANES):
        tile = acc_ref[i * LANES : (i + 1) * LANES, :].T
        give_ref[half + i : half + i + 1, :LANES] = jnp.sum(tile, axis=0, keepdims=True)
    give_ref[half : half + 8, LANES:] = jnp.zeros((8, LANES), F32)


def pack_kernel(own_ref, mine_ref, got_ref, out_ref):
    half, _ = own_ref.shape
    share = out_ref.shape[1] - 8
    sums = mine_ref[half:, :] + got_ref[half:, :]
    for j in range(out_ref.shape[0]):
        rows = slice(j * share, (j + 1) * share)
        out_ref[j, :share, :] = own_ref[rows, :] + got_ref[rows, :]
        out_ref[j, share:, :] = sums


def share_kernel(parts_ref, out_ref, sums_ref):
    total = sum(parts_ref[i] for i in range(parts_ref.shape[0]))
    share = out_ref.shape[1]
    sums_ref[0] = total[share:, :LANES]
    for m in range(out_ref.shape[0]):
        out_ref[m] = total[:share, :]


def spread(ref, value):
    for i in range(value.shape[0]):
        ref[i * LANES : (i + 1) * LANES, :] = jnp.broadcast_to(
            value[i : i + 1, :], (LANES, LANES)
        ).T


def col_kernel(e_ref, parts_ref, out_ref, r_ref):
    spread(r_ref, 1.0 / jnp.sum(parts_ref[:, :8, :], axis=0))
    tiles = e_ref.shape[1] // LANES
    block = 32

    def body(b, acc):
        rows = pl.ds(pl.multiple_of(b * block, block), block)
        r = r_ref[rows, :]
        out = []
        for j in range(tiles):
            value = acc[j]
            tile = e_ref[rows, j * LANES : (j + 1) * LANES] * r
            for g in range(block // 8):
                value = value + tile[g * 8 : (g + 1) * 8, :]
            out.append(value)
        return tuple(out)

    zero = tuple(jnp.zeros((8, LANES), F32) for _ in range(tiles))
    acc = lax.fori_loop(0, e_ref.shape[0] // block, body, zero)
    value = jnp.concatenate([jnp.sum(a, axis=0, keepdims=True) for a in acc], axis=0)
    for m in range(Z):
        out_ref[m] = value


def diff_kernel(part):
    def kernel(
        where_ref, e_ref, s_ref, full_ref, norm_ref, turned_ref, c_ref, parts_ref, mass_ref,
        rel0, rel1, rel2, rel3, rel4u, rel4d, rel5, rel6, rel7,
        r_ref, m_ref, g_ref, diff_ref,
    ):
        spread(r_ref, 1.0 / jnp.sum(parts_ref[...], axis=0))
        spread(m_ref, (1.0 / STUDENT_TEMP) / jnp.sum(mass_ref[:, 8:, :], axis=0))
        half = rel0.shape[1]
        tiles = half // LANES
        block = 16

        def body(b, carry):
            rows = pl.ds(pl.multiple_of(b * block, block), block)
            r = r_ref[rows, :] * (1.0 / STUDENT_TEMP)
            m = m_ref[rows, :]
            for j in range(tiles):
                tile = part * tiles + j
                lanes = slice(tile * LANES, (tile + 1) * LANES)
                targets = (r * e_ref[rows, lanes]) * c_ref[tile : tile + 1, :]
                probs = s_ref[rows, lanes].astype(F32) * m
                diff_ref[rows, j * LANES : (j + 1) * LANES] = (probs - targets).astype(BF16)
            return carry

        lax.fori_loop(0, e_ref.shape[0] // block, body, 0, unroll=2)
        columns = slice(part * half, (part + 1) * half)
        grad = jnp.dot(turned_ref[...], diff_ref[...], preferred_element_type=F32)
        full = full_ref[:, columns]
        proj = jnp.sum(full.astype(BF16).astype(F32) * grad, axis=0, keepdims=True)
        g_ref[...] = (grad - full * proj) / norm_ref[:, columns]
        core, z = where_ref[0], where_ref[1]
        deep = g_ref.shape[0] // Z
        near = deep // 2
        outs = (rel0, rel1, rel2, rel3, (rel4u, rel4d), rel5, rel6, rel7)
        for j, out in enumerate(outs):
            top = lax.rem(z + j, Z) * deep
            for side in range(2):
                take = pl.multiple_of(top + lax.rem(core + side, 2) * near, near)
                value = g_ref[pl.ds(take, near), :]
                if j == 4:
                    out[side][...] = value
                else:
                    out[side * near : (side + 1) * near, :] = value

    return kernel


def last_kernel(
    where_ref, probs_ref, targets_ref, mass_ref, sums_ref, zsf_ref, norm_ref, mask_ref, out_ref,
    r_ref, m_ref,
):
    spread(r_ref, (1.0 / STUDENT_TEMP) / sums_ref[0])
    spread(m_ref, (1.0 / STUDENT_TEMP) / jnp.sum(mass_ref[:, 8:, :], axis=0))
    slots = mask_ref.shape[1]
    half = zsf_ref.shape[0]
    width = zsf_ref.shape[1]
    first = core_rows(where_ref, 0, half).start
    for i in range(out_ref.shape[0]):
        rows = pl.ds(i * slots, slots)
        own = pl.ds(pl.multiple_of(first + i * slots, slots), slots)
        zsf = zsf_ref[rows, :]
        r, m = (jnp.concatenate([x[own, :]] * (width // LANES), axis=1) for x in (r_ref, m_ref))
        gz = probs_ref[rows, :] * m - targets_ref[rows, :] * r
        proj = jnp.sum(zsf * gz, axis=1, keepdims=True)
        grad = (gz - zsf * proj) / norm_ref[rows, :]
        hot = one_hot_t(mask_ref[i : i + 1, :], out_ref.shape[1], BF16)
        total = jnp.zeros(out_ref.shape[1:], F32)
        for _ in range(3):
            piece = grad.astype(BF16)
            total += jnp.dot(hot, piece, preferred_element_type=F32)
            grad = grad - piece.astype(F32)
        out_ref[i] = total


def first_sum_kernel(rel_ref, got_ref, top_ref):
    near = got_ref.shape[0]
    top_ref[:near, :] = rel_ref[:near, :] + got_ref[...]
    top_ref[near:, :] = rel_ref[near:, :]


def first_sum_low_kernel(rel_ref, got_ref, top_ref):
    near = got_ref.shape[0]
    top_ref[:near, :] = rel_ref[:near, :]
    top_ref[near:, :] = rel_ref[near:, :] + got_ref[...]


def sum_kernel(rel_ref, got_ref, out_ref):
    out_ref[...] = rel_ref[...] + got_ref[...]


def last_sum_kernel(rel_ref, up_ref, down_ref, keep_ref, give_ref):
    near = keep_ref.shape[0]
    keep_ref[...] = rel_ref[:near, :] + up_ref[:near, :] + down_ref[:near, :]
    give_ref[...] = rel_ref[near:, :] + up_ref[near:, :] + down_ref[near:, :]


def place_kernel(where_ref, keep0_ref, keep1_ref, got0_ref, got1_ref, out_ref):
    core = where_ref[0]
    half = keep0_ref.shape[1]
    for side, pair in enumerate(((keep0_ref, keep1_ref), (got0_ref, got1_ref))):
        first = lax.rem(core + side, 2) * 2 * half
        for i, ref in enumerate(pair):
            out_ref[:, pl.ds(pl.multiple_of(first + i * half, half), half)] = ref[...]


def shape(*dims, dtype=F32):
    return jax.ShapeDtypeStruct(dims, dtype)


def hold(*dims, dtype=F32):
    return pltpu.VMEM(dims, dtype)


def other_core(x):
    return lax.ppermute(x, "batch", [(i, i ^ 1) for i in range(RING)])


def along_z(x, d):
    return lax.ppermute(
        x, "batch", [(i, ((i // 2 + d) % Z) * 2 + i % 2) for i in range(RING)]
    )


def all_columns(x):
    return lax.all_to_all(x, "batch", 0, 0, axis_index_groups=Z_GROUPS)


def all_rows(x):
    return lax.all_to_all(x, ("batch", "proto"), 0, 0, axis_index_groups=ROW_GROUPS)


def tie(x, y):
    return lax.optimization_barrier((x, y))[0]


def on_device(teacher_feats, student_feats, prototypes, mask_index):
    images, patches, width = teacher_feats.shape
    slots = mask_index.shape[1]
    own = images * slots
    tokens = 2 * own
    wide = prototypes.shape[1] // 2
    lane_tiles = wide // LANES
    row_tiles = tokens // LANES
    place = lax.axis_index("batch")
    where = jnp.stack([lax.rem(place, 2), lax.div(place, 2)]).astype(jnp.int32)
    scalars = pl.BlockSpec(memory_space=pltpu.SMEM)

    def in_hbm(x):
        return pltpu.with_memory_space_constraint(x, pltpu.HBM)

    def placed(kernel, outs, *args, **kw):
        return pl.pallas_call(
            kernel,
            in_specs=[scalars] + [whole()] * len(args),
            out_specs=[whole()] * len(outs),
            out_shape=outs,
            scratch_shapes=kw.get("scratch", []),
            compiler_params=params(16),
            cost_estimate=kw.get("cost_estimate"),
        )(where, *args)

    zt, zs, zsf, s_norm = pl.pallas_call(
        prep_kernel,
        in_specs=[pl.BlockSpec(memory_space=pl.ANY)] * 3,
        out_specs=[whole()] * 4,
        out_shape=[
            shape(own, width), shape(own, width), shape(own, width), shape(own, 1),
        ],
        scratch_shapes=[
            VMEM(teacher_feats.shape, BF16), VMEM(student_feats.shape, BF16),
            VMEM(mask_index.shape, jnp.int32), pltpu.SemaphoreType.DMA((3,)),
        ],
        compiler_params=params(16),
    )(in_hbm(teacher_feats), in_hbm(student_feats), in_hbm(mask_index))
    zt_other = other_core(zt)
    zs_other = other_core(zs)
    steps = 2
    column_spec = pl.BlockSpec((width, wide // steps), lambda j, w: (0, j))
    full, unit, back, p_norm = pl.pallas_call(
        proto_kernel,
        grid_spec=pltpu.PrefetchScalarGridSpec(
            num_scalar_prefetch=1,
            grid=(steps,),
            in_specs=[
                pl.BlockSpec((width, wide // steps), lambda j, w: (0, w[0] * steps + j))
            ],
            out_specs=[
                column_spec, column_spec,
                pl.BlockSpec((wide // steps, width), lambda j, w: (j, 0)),
                pl.BlockSpec((1, wide // steps), lambda j, w: (0, j)),
            ],
        ),
        out_shape=[
            shape(width, wide), shape(width, wide, dtype=BF16),
            shape(wide, width, dtype=BF16), shape(1, wide),
        ],
        compiler_params=params(16),
    )(where, in_hbm(prototypes))

    exp_cost = cost(2 * tokens * wide * width, tokens * wide)
    e, col_out = placed(
        teacher_exp_kernel,
        [hold(tokens, wide), shape(Z, lane_tiles, LANES)],
        zt, zt_other, unit, cost_estimate=exp_cost,
    )
    s, mass_acc, turned, probs, probs_give = placed(
        student_exp_kernel,
        [
            hold(tokens, wide, dtype=BF16), shape(tokens, LANES),
            shape(width, tokens, dtype=BF16),
            shape(own, width), shape(own, width),
        ],
        zs, zs_other, unit, back, cost_estimate=exp_cost,
    )
    probs = lax.psum(probs + other_core(probs_give), "proto")
    col_out = tie(col_out, mass_acc)

    mass = None
    for sweep in range(ITERS):
        col_parts = all_columns(col_out)
        extra = [mass_acc] if sweep == 0 else []
        if sweep == ITERS - 1:
            break
        extra = [mass_acc] if sweep == 0 else []
        row_out, _ = call(
            row_kernel if sweep else row_mass_kernel,
            [shape(ROWS, row_tiles * (1 + len(extra)), LANES), shape(lane_tiles, LANES)],
            e, col_parts, *extra,
            scratch=[VMEM((tokens, LANES), F32)],
        )
        row_parts = all_rows(row_out)
        if sweep == 0:
            mass = row_parts
        (col_out,) = call(
            col_kernel, [shape(Z, lane_tiles, LANES)], e, row_parts,
            scratch=[VMEM((tokens, LANES), F32)],
        )

    share = own // RING
    pull, pull_give, c = placed(
        row_pull_kernel,
        [shape(own, width), shape(own + 8, width), shape(lane_tiles, LANES)],
        e, col_parts, back,
        scratch=[VMEM((tokens, LANES), F32), VMEM((tokens, wide), BF16)],
        cost_estimate=cost(4 * tokens * wide * width),
    )
    (pull_out,) = call(
        pack_kernel, [shape(RING, share + 8, width)], pull, pull_give, other_core(pull_give)
    )
    pull_parts = lax.all_to_all(pull_out, "proto", 0, 0)
    pull_share, row_parts = call(
        share_kernel, [shape(RING, share, width), shape(1, row_tiles, LANES)], pull_parts
    )

    deep = width // Z
    near = deep // 2
    half = wide // 2
    rels = []
    for part in range(2):
        rel = placed(
            diff_kernel(part),
            [shape(deep, half)] * 4 + [shape(near, half)] * 2 + [shape(deep, half)] * 3,
            e, s, full, p_norm, turned, c, row_parts, mass,
            scratch=[
                VMEM((tokens, LANES), F32), VMEM((tokens, LANES), F32), VMEM((width, half), F32),
                VMEM((tokens, half), BF16),
            ],
            cost_estimate=cost(tokens * wide * width),
        )
        rels.append(list(rel))

    ups = [along_z(rel[4], 1) for rel in rels]
    downs = [along_z(rel[5], -1) for rel in rels]
    rels = [rel[:4] + [None] + rel[6:] for rel in rels]

    targets = lax.all_to_all(tie(pull_share, [rel[0] for rel in rels]), "proto", 0, 0).reshape(own, width)
    (grad_student,) = placed(
        last_kernel, [shape(images, patches, width)],
        probs, targets, mass, row_parts, zsf, s_norm, mask_index,
        scratch=[VMEM((tokens, LANES), F32), VMEM((tokens, LANES), F32)],
    )

    part_shape = [shape(deep, half)]
    ups = [along_z(call(first_sum_kernel, part_shape, r[3], u)[0], 1) for r, u in zip(rels, ups)]
    downs = [
        along_z(call(first_sum_low_kernel, part_shape, r[5], d)[0], -1)
        for r, d in zip(rels, downs)
    ]
    for j in (2, 1):
        ups = [along_z(call(sum_kernel, part_shape, r[j], u)[0], 1) for r, u in zip(rels, ups)]
        downs = [
            along_z(call(sum_kernel, part_shape, r[8 - j], d)[0], -1)
            for r, d in zip(rels, downs)
        ]
    keeps, gots = [], []
    for rel, up, down in zip(rels, ups, downs):
        keep, give = call(last_sum_kernel, [shape(near, half)] * 2, rel[0], up, down)
        keeps.append(keep)
        gots.append(other_core(give))
    (grad_protos,) = placed(place_kernel, [shape(near, 2 * wide)], *keeps, *gots)
    return (grad_student, grad_protos)


def solution(mesh):
    in_specs = (P("batch", None, None), P("batch", None, None), P(None, "proto"), P("batch", None))
    out_specs = (P("batch", None, None), P("batch", "proto"))
    return jax.shard_map(
        on_device, mesh=mesh, in_specs=in_specs, out_specs=out_specs, check_vma=False
    )
```

```python
import jax
import jax.numpy as jnp
from jax import lax
from jax.experimental import pallas as pl
from jax.experimental.pallas import tpu as pltpu
from jax.sharding import PartitionSpec as P

ITERS = 3
TEACHER_TEMP = 0.04
STUDENT_TEMP = 0.1
EPSILON = 1e-06
LANES = 128
Z = 8
RING = 16
ROWS = 32
WIDE = 1024
MIB = 1024 * 1024
F32 = jnp.float32
BF16 = jnp.bfloat16

VMEM = pltpu.VMEM
Z_GROUPS = [[2 * z + c for z in range(Z)] for c in range(2)]
ROW_GROUPS = [[ROWS * z + i for i in range(ROWS)] for z in range(Z)]


def whole():
    return pl.BlockSpec(memory_space=VMEM)


def cost(flops, transcendentals=0, moved=0):
    return pl.CostEstimate(
        flops=flops, transcendentals=transcendentals, bytes_accessed=moved
    )


def params(vmem):
    return pltpu.CompilerParams(vmem_limit_bytes=vmem * MIB)


def call(kernel, outs, *args, scratch=(), vmem=16, cost_estimate=None):
    return pl.pallas_call(
        kernel,
        out_shape=outs,
        in_specs=[whole()] * len(args),
        out_specs=[whole()] * len(outs),
        scratch_shapes=list(scratch),
        compiler_params=params(vmem),
        cost_estimate=cost_estimate,
    )(*args)


def one_hot_t(mask_row, patches, dtype):
    slots = mask_row.shape[1]
    patch = lax.broadcasted_iota(jnp.int32, (patches, slots), 0)
    return jnp.where(patch == mask_row, 1.0, 0.0).astype(dtype)


def fetch(pairs, sems):
    copies = [pltpu.make_async_copy(src, dst, sems.at[i]) for i, (src, dst) in enumerate(pairs)]
    for copy in copies:
        copy.start()
    return copies


def masked_rows(feats, mask_row):
    hot = one_hot_t(mask_row, feats.shape[0], BF16)
    rows = lax.dot_general(hot, feats, (((0,), (0,)), ((), ())), preferred_element_type=F32)
    return rows, jnp.sqrt(jnp.sum(rows * rows, axis=1, keepdims=True) + EPSILON)


def prep_kernel(
    teacher_hbm, student_hbm, mask_hbm, zt_ref, zs_ref, teacher_ref, student_ref, mask_ref, sems
):
    mask_copy, teacher_copy, student_copy = fetch(
        ((mask_hbm, mask_ref), (teacher_hbm, teacher_ref), (student_hbm, student_ref)), sems
    )
    mask_copy.wait()
    slots = mask_ref.shape[1]
    for copy, feats, out in (
        (teacher_copy, teacher_ref, zt_ref), (student_copy, student_ref, zs_ref)
    ):
        copy.wait()
        for i in range(feats.shape[0]):
            rows, norm = masked_rows(feats[i], mask_ref[i : i + 1, :])
            out[i * slots : (i + 1) * slots, :] = (rows / norm).astype(BF16).astype(F32)


def proto_kernel(where_ref, proto_ref, full_ref, unit_ref, back_ref, norm_ref):
    p = proto_ref[...].astype(F32)
    norm = jnp.sqrt(jnp.sum(p * p, axis=0, keepdims=True) + EPSILON)
    full = p / norm
    full_ref[...] = full
    unit_ref[...] = full.astype(BF16)
    back_ref[...] = full.T.astype(BF16)
    norm_ref[...] = norm


def core_rows(where_ref, side, half):
    return pl.ds(pl.multiple_of(lax.rem(where_ref[0] + side, 2) * half, half), half)


def write_lanes(out_ref, value, row, copies):
    for m in range(copies):
        out_ref[m, pl.ds(row, 1), :] = value


def write_rows(out_ref, acc_ref, first=0):
    pieces = []
    for i in range(acc_ref.shape[0] // LANES):
        tile = acc_ref[i * LANES : (i + 1) * LANES, :].T
        pieces.append(jnp.sum(tile, axis=0, keepdims=True))
    value = jnp.concatenate(pieces, axis=0)
    for m in range(out_ref.shape[0]):
        out_ref[m, first : first + 8, :] = value


def teacher_exp_kernel(where_ref, own_ref, other_ref, unit_ref, e_ref, col_ref):
    half = own_ref.shape[0]
    wide = unit_ref.shape[1]
    block = 256
    for w in range(wide // WIDE):
        columns = pl.ds(w * WIDE, WIDE)
        unit = unit_ref[:, columns]
        total = jnp.zeros((8, WIDE), F32)
        for side, ref in enumerate((own_ref, other_ref)):
            place = core_rows(where_ref, side, half)
            for b in range(half // block):
                z = ref[b * block : (b + 1) * block, :].astype(BF16)
                e = jnp.exp(
                    jnp.dot(z, unit, preferred_element_type=F32) * (1.0 / TEACHER_TEMP)
                )
                e_ref[pl.ds(place.start + b * block, block), columns] = e
                for g in range(block // 8):
                    total += e[g * 8 : (g + 1) * 8, :]
        total = jnp.sum(total, axis=0, keepdims=True)
        for i in range(WIDE // LANES):
            write_lanes(
                col_ref, total[:, i * LANES : (i + 1) * LANES], w * (WIDE // LANES) + i, Z
            )


def student_exp_kernel(
    where_ref, own_ref, other_ref, unit_ref, s_ref, mass_ref, turned_ref
):
    half = own_ref.shape[0]
    wide = unit_ref.shape[1]
    block = 256
    for side, ref in enumerate((own_ref, other_ref)):
        turned_ref[:, core_rows(where_ref, side, half)] = ref[...].T.astype(BF16)
    for w in range(wide // WIDE):
        columns = pl.ds(w * WIDE, WIDE)
        unit = unit_ref[:, columns]
        for side, ref in enumerate((own_ref, other_ref)):
            place = core_rows(where_ref, side, half)
            for b in range(half // block):
                rows = pl.ds(place.start + b * block, block)
                z = ref[b * block : (b + 1) * block, :].astype(BF16)
                s = jnp.exp(
                    jnp.dot(z, unit, preferred_element_type=F32) * (1.0 / STUDENT_TEMP)
                )
                s_ref[rows, columns] = s
                part = sum(s[:, j * LANES : (j + 1) * LANES] for j in range(WIDE // LANES))
                if w:
                    mass_ref[rows, :] += part
                else:
                    mass_ref[rows, :] = part


def row_kernel(e_ref, parts_ref, out_ref, c_ref, acc_ref):
    c = 1.0 / jnp.sum(parts_ref[...], axis=0)
    c_ref[...] = c
    tiles = c.shape[0]
    block = 64

    def body(b, carry):
        rows = pl.ds(pl.multiple_of(b * block, block), block)
        acc = jnp.zeros((block, LANES), F32)
        for j in range(tiles):
            acc += e_ref[rows, j * LANES : (j + 1) * LANES] * c[j : j + 1, :]
        acc_ref[rows, :] = acc
        return carry

    lax.fori_loop(0, e_ref.shape[0] // block, body, 0)
    write_rows(out_ref, acc_ref)


def row_mass_kernel(e_ref, parts_ref, mass_ref, out_ref, c_ref, acc_ref):
    row_kernel(e_ref, parts_ref, out_ref, c_ref, acc_ref)
    write_rows(out_ref, mass_ref, first=8)


def spread(ref, value):
    for i in range(value.shape[0]):
        ref[i * LANES : (i + 1) * LANES, :] = jnp.broadcast_to(
            value[i : i + 1, :], (LANES, LANES)
        ).T


def col_kernel(e_ref, parts_ref, out_ref, r_ref):
    spread(r_ref, 1.0 / jnp.sum(parts_ref[:, :8, :], axis=0))
    tiles = e_ref.shape[1] // LANES
    block = 32

    def body(b, acc):
        rows = pl.ds(pl.multiple_of(b * block, block), block)
        r = r_ref[rows, :]
        out = []
        for j in range(tiles):
            value = acc[j]
            tile = e_ref[rows, j * LANES : (j + 1) * LANES] * r
            for g in range(block // 8):
                value = value + tile[g * 8 : (g + 1) * 8, :]
            out.append(value)
        return tuple(out)

    zero = tuple(jnp.zeros((8, LANES), F32) for _ in range(tiles))
    acc = lax.fori_loop(0, e_ref.shape[0] // block, body, zero)
    value = jnp.concatenate([jnp.sum(a, axis=0, keepdims=True) for a in acc], axis=0)
    for m in range(Z):
        out_ref[m] = value


def diff_kernel(
    e_ref, s_ref, c_ref, parts_ref, mass_ref, diff_ref, r_ref, m_ref
):
    scale = 1.0 / STUDENT_TEMP
    spread(r_ref, scale / jnp.sum(parts_ref[...], axis=0))
    spread(m_ref, scale / jnp.sum(mass_ref[:, 8:, :], axis=0))
    tiles = e_ref.shape[1] // LANES
    block = 16

    def body(b, carry):
        rows = pl.ds(pl.multiple_of(b * block, block), block)
        r = r_ref[rows, :]
        m = m_ref[rows, :]
        for j in range(tiles):
            lanes = slice(j * LANES, (j + 1) * LANES)
            targets = (r * e_ref[rows, lanes]) * c_ref[j : j + 1, :]
            probs = s_ref[rows, lanes] * m
            diff_ref[rows, lanes] = (probs - targets).astype(BF16)
        return carry

    lax.fori_loop(0, e_ref.shape[0] // block, body, 0)


def token_kernel(where_ref, diff_ref, back_ref, own_ref, give_ref):
    for side, out in enumerate((own_ref, give_ref)):
        rows = core_rows(where_ref, side, out.shape[0])
        out[...] = jnp.dot(diff_ref[rows, :], back_ref[...], preferred_element_type=F32)


def grad_kernel(where_ref, diff_ref, full_ref, norm_ref, turned_ref, *refs):
    outs, (g_ref, sems) = refs[:-2], refs[-2:]
    wide = full_ref.shape[1]
    for w in range(wide // WIDE):
        columns = slice(w * WIDE, (w + 1) * WIDE)
        grad = jnp.dot(turned_ref[...], diff_ref[:, columns], preferred_element_type=F32)
        full = full_ref[:, columns]
        proj = jnp.sum(full.astype(BF16).astype(F32) * grad, axis=0, keepdims=True)
        g_ref[:, columns] = (grad - full * proj) / norm_ref[:, columns]
    core, z = where_ref[0], where_ref[1]
    deep = g_ref.shape[0] // Z
    near = deep // 2
    pairs = []
    for j in range(Z):
        top = lax.rem(z + j, Z) * deep
        for side in range(2):
            take = pl.multiple_of(top + lax.rem(core + side, 2) * near, near)
            if j == 4:
                out = outs[4 + side]
            else:
                out = outs[j + (j > 4)].at[pl.ds(side * near, near), :]
            pairs.append((g_ref.at[pl.ds(take, near), :], out))
    for copy in fetch(pairs, sems):
        copy.wait()


def share_kernel(parts_ref, out_ref):
    total = sum(parts_ref[i] for i in range(parts_ref.shape[0]))
    for m in range(out_ref.shape[0]):
        out_ref[m] = total


def last_kernel(gz_ref, feats_ref, mask_ref, out_ref):
    slots = mask_ref.shape[1]
    for i in range(out_ref.shape[0]):
        mask = mask_ref[i : i + 1, :]
        xs, norm = masked_rows(feats_ref[i], mask)
        zsf = xs / norm
        gz = gz_ref[i * slots : (i + 1) * slots, :]
        proj = jnp.sum(zsf * gz, axis=1, keepdims=True)
        grad = (gz - zsf * proj) / norm
        hot = one_hot_t(mask, out_ref.shape[1], BF16)
        high = grad.astype(BF16)
        low = (grad - high.astype(F32)).astype(BF16)
        out_ref[i] = jnp.dot(hot, high, preferred_element_type=F32) + jnp.dot(
            hot, low, preferred_element_type=F32
        )


def sum_kernel(a_ref, b_ref, out_ref):
    out_ref[...] = a_ref[...] + b_ref[...]


def first_step_kernel(low):
    def kernel(rel_hbm, got_ref, out_ref, sem):
        for copy in fetch(((rel_hbm, out_ref),), sem):
            copy.wait()
        near = got_ref.shape[0]
        rows = slice(near, 2 * near) if low else slice(0, near)
        out_ref[rows, :] += got_ref[...]

    return kernel


def step_kernel(rel_hbm, got_ref, out_ref, sem):
    for copy in fetch(((rel_hbm, out_ref),), sem):
        copy.wait()
    out_ref[...] += got_ref[...]


def last_sum_kernel(rel_hbm, up_ref, down_ref, keep_ref, give_ref, rel, sem):
    for copy in fetch(((rel_hbm, rel),), sem):
        copy.wait()
    near = keep_ref.shape[0]
    total = rel[...] + (up_ref[...] + down_ref[...])
    keep_ref[...] = total[:near, :]
    give_ref[...] = total[near:, :]


def place_kernel(where_ref, keep_ref, got_ref, out_ref):
    wide = keep_ref.shape[1]
    for side, ref in enumerate((keep_ref, got_ref)):
        first = lax.rem(where_ref[0] + side, 2) * wide
        out_ref[:, pl.ds(pl.multiple_of(first, wide), wide)] = ref[...]


def shape(*dims, dtype=F32):
    return jax.ShapeDtypeStruct(dims, dtype)


def hold(*dims, dtype=F32):
    return pltpu.VMEM(dims, dtype)


def far(*dims):
    return pltpu.HBM(dims, F32)


def in_hbm(x):
    return pltpu.with_memory_space_constraint(x, pltpu.HBM)


def other_core(x):
    return lax.ppermute(x, "batch", [(i, i ^ 1) for i in range(RING)])


def along_z(x, d):
    return lax.ppermute(
        x, "batch", [(i, ((i // 2 + d) % Z) * 2 + i % 2) for i in range(RING)]
    )


def all_columns(x):
    return lax.all_to_all(x, "batch", 0, 0, axis_index_groups=Z_GROUPS)


def all_rows(x):
    return lax.all_to_all(x, ("batch", "proto"), 0, 0, axis_index_groups=ROW_GROUPS)


def tie(x, y):
    return lax.optimization_barrier((x, y))[0]


def on_device(teacher_feats, student_feats, prototypes, mask_index):
    images, patches, width = teacher_feats.shape
    slots = mask_index.shape[1]
    own = images * slots
    tokens = 2 * own
    wide = prototypes.shape[1] // 2
    lane_tiles = wide // LANES
    row_tiles = tokens // LANES
    place = lax.axis_index("batch")
    where = jnp.stack([lax.rem(place, 2), lax.div(place, 2)]).astype(jnp.int32)
    scalars = pl.BlockSpec(memory_space=pltpu.SMEM)

    def placed(kernel, outs, *args, **kw):
        return pl.pallas_call(
            kernel,
            in_specs=[scalars] + [whole()] * len(args),
            out_specs=[whole()] * len(outs),
            out_shape=outs,
            scratch_shapes=kw.get("scratch", []),
            compiler_params=params(16),
            cost_estimate=kw.get("cost_estimate"),
        )(where, *args)

    zt, zs = pl.pallas_call(
        prep_kernel,
        in_specs=[pl.BlockSpec(memory_space=pl.ANY)] * 3,
        out_specs=[whole()] * 2,
        out_shape=[shape(own, width), shape(own, width)],
        scratch_shapes=[
            VMEM(teacher_feats.shape, BF16), VMEM(student_feats.shape, BF16),
            VMEM(mask_index.shape, jnp.int32), pltpu.SemaphoreType.DMA((3,)),
        ],
        compiler_params=params(16),
    )(in_hbm(teacher_feats), in_hbm(student_feats), in_hbm(mask_index))
    zt_other = other_core(zt)
    zs_other = other_core(zs)
    steps = 2
    column_spec = pl.BlockSpec((width, wide // steps), lambda j, w: (0, j))
    full, unit, back, p_norm = pl.pallas_call(
        proto_kernel,
        grid_spec=pltpu.PrefetchScalarGridSpec(
            num_scalar_prefetch=1,
            grid=(steps,),
            in_specs=[
                pl.BlockSpec((width, wide // steps), lambda j, w: (0, w[0] * steps + j))
            ],
            out_specs=[
                column_spec, column_spec,
                pl.BlockSpec((wide // steps, width), lambda j, w: (j, 0)),
                pl.BlockSpec((1, wide // steps), lambda j, w: (0, j)),
            ],
        ),
        out_shape=[
            shape(width, wide), shape(width, wide, dtype=BF16),
            shape(wide, width, dtype=BF16), shape(1, wide),
        ],
        compiler_params=params(16),
    )(where, in_hbm(prototypes))

    exp_cost = cost(2 * tokens * wide * width, tokens * wide)
    e, col_out = placed(
        teacher_exp_kernel,
        [hold(tokens, wide), shape(Z, lane_tiles, LANES)],
        zt, zt_other, unit, cost_estimate=exp_cost,
    )
    s, mass_acc, turned = placed(
        student_exp_kernel,
        [hold(tokens, wide), shape(tokens, LANES), shape(width, tokens, dtype=BF16)],
        zs, zs_other, unit, cost_estimate=exp_cost,
    )
    col_out = tie(col_out, mass_acc)

    mass = None
    for sweep in range(ITERS):
        col_parts = all_columns(col_out)
        extra = [mass_acc] if sweep == 0 else []
        row_out, c = call(
            row_kernel if sweep else row_mass_kernel,
            [shape(ROWS, row_tiles * (1 + len(extra)), LANES), shape(lane_tiles, LANES)],
            e, col_parts, *extra,
            scratch=[VMEM((tokens, LANES), F32)],
        )
        row_parts = all_rows(row_out)
        if sweep == 0:
            mass = row_parts
        if sweep < ITERS - 1:
            (col_out,) = call(
                col_kernel, [shape(Z, lane_tiles, LANES)], e, row_parts,
                scratch=[VMEM((tokens, LANES), F32)],
            )

    (diff,) = call(
        diff_kernel, [shape(tokens, wide, dtype=BF16)], e, s, c, row_parts, mass,
        scratch=[VMEM((tokens, LANES), F32), VMEM((tokens, LANES), F32)],
    )
    deep = width // Z
    near = deep // 2
    anywhere = pl.BlockSpec(memory_space=pltpu.HBM)
    rel = pl.pallas_call(
        grad_kernel,
        in_specs=[scalars] + [whole()] * 4,
        out_specs=[anywhere] * 9,
        out_shape=[far(deep, wide)] * 4 + [far(near, wide)] * 2 + [far(deep, wide)] * 3,
        scratch_shapes=[VMEM((width, wide), F32), pltpu.SemaphoreType.DMA((2 * Z,))],
        compiler_params=params(16),
        cost_estimate=cost(2 * tokens * wide * width),
    )(where, diff, full, p_norm, turned)

    def step(kernel, term, got):
        return pl.pallas_call(
            kernel,
            in_specs=[anywhere, whole()],
            out_specs=whole(),
            out_shape=shape(deep, wide),
            scratch_shapes=[pltpu.SemaphoreType.DMA((1,))],
            compiler_params=params(16),
        )(term, got)

    up, down = along_z(rel[4], 1), along_z(rel[5], -1)
    gz, gz_give = placed(
        token_kernel, [shape(own, width)] * 2, tie(diff, rel), back,
        cost_estimate=cost(2 * tokens * wide * width),
    )
    gz_got = other_core(gz_give)
    up = step(first_step_kernel(False), rel[3], up)
    down = step(first_step_kernel(True), rel[6], down)
    (gz,) = call(sum_kernel, [shape(own, width)], gz, gz_got)
    gz_parts = lax.all_to_all(
        tie(gz, (up, down)).reshape(RING, own // RING, width), "proto", 0, 0
    )
    up = step(step_kernel, rel[2], along_z(up, 1))
    down = step(step_kernel, rel[7], along_z(down, -1))
    (gz_share,) = call(share_kernel, [shape(RING, own // RING, width)], gz_parts)
    gz = lax.all_to_all(tie(gz_share, (up, down)), "proto", 0, 0).reshape(own, width)
    up = step(step_kernel, rel[1], along_z(up, 1))
    down = step(step_kernel, rel[8], along_z(down, -1))
    up, down = along_z(up, 1), along_z(down, -1)
    keep, give = pl.pallas_call(
        last_sum_kernel,
        in_specs=[anywhere, whole(), whole()],
        out_specs=[whole()] * 2,
        out_shape=[shape(near, wide)] * 2,
        scratch_shapes=[VMEM((deep, wide), F32), pltpu.SemaphoreType.DMA((1,))],
        compiler_params=params(16),
    )(rel[0], up, down)
    got = other_core(give)
    (grad_student,) = call(
        last_kernel, [shape(images, patches, width)], gz, student_feats, mask_index
    )
    (grad_protos,) = placed(place_kernel, [shape(near, 2 * wide)], keep, got)
    return (grad_student, grad_protos)


def solution(mesh):
    in_specs = (P("batch", None, None), P("batch", None, None), P(None, "proto"), P("batch", None))
    out_specs = (P("batch", None, None), P("batch", "proto"))
    return jax.shard_map(
        on_device, mesh=mesh, in_specs=in_specs, out_specs=out_specs, check_vma=False
    )
```

```python
import jax
import jax.numpy as jnp
from jax import lax
from jax.experimental import pallas as pl
from jax.experimental.pallas import tpu as pltpu
from jax.sharding import PartitionSpec as P

ITERS = 3
TEACHER_TEMP = 0.04
STUDENT_TEMP = 0.1
EPSILON = 1e-06
LANES = 128
Z = 8
RING = 16
ROWS = 32
WIDE = 1024
MIB = 1024 * 1024
F32 = jnp.float32
BF16 = jnp.bfloat16

VMEM = pltpu.VMEM
Z_GROUPS = [[2 * z + c for z in range(Z)] for c in range(2)]
ROW_GROUPS = [[ROWS * z + i for i in range(ROWS)] for z in range(Z)]


def whole():
    return pl.BlockSpec(memory_space=VMEM)


def cost(flops, transcendentals=0, moved=0):
    return pl.CostEstimate(
        flops=flops, transcendentals=transcendentals, bytes_accessed=moved
    )


def params(vmem):
    return pltpu.CompilerParams(vmem_limit_bytes=vmem * MIB)


def call(kernel, outs, *args, scratch=(), vmem=16, cost_estimate=None):
    return pl.pallas_call(
        kernel,
        out_shape=outs,
        in_specs=[whole()] * len(args),
        out_specs=[whole()] * len(outs),
        scratch_shapes=list(scratch),
        compiler_params=params(vmem),
        cost_estimate=cost_estimate,
    )(*args)


def one_hot_t(mask_row, patches, dtype):
    slots = mask_row.shape[1]
    patch = lax.broadcasted_iota(jnp.int32, (patches, slots), 0)
    return jnp.where(patch == mask_row, 1.0, 0.0).astype(dtype)


def fetch(pairs, sems):
    copies = [pltpu.make_async_copy(src, dst, sems.at[i]) for i, (src, dst) in enumerate(pairs)]
    for copy in copies:
        copy.start()
    return copies


def masked_rows(feats, mask_row):
    hot = one_hot_t(mask_row, feats.shape[0], BF16)
    rows = lax.dot_general(hot, feats, (((0,), (0,)), ((), ())), preferred_element_type=F32)
    return rows, jnp.sqrt(jnp.sum(rows * rows, axis=1, keepdims=True) + EPSILON)


def prep_kernel(
    teacher_hbm, student_hbm, mask_hbm, zt_ref, zs_ref, teacher_ref, student_ref, mask_ref, sems
):
    mask_copy, teacher_copy, student_copy = fetch(
        ((mask_hbm, mask_ref), (teacher_hbm, teacher_ref), (student_hbm, student_ref)), sems
    )
    mask_copy.wait()
    slots = mask_ref.shape[1]
    for copy, feats, out in (
        (teacher_copy, teacher_ref, zt_ref), (student_copy, student_ref, zs_ref)
    ):
        copy.wait()
        for i in range(feats.shape[0]):
            rows, norm = masked_rows(feats[i], mask_ref[i : i + 1, :])
            out[i * slots : (i + 1) * slots, :] = (rows / norm).astype(BF16).astype(F32)


def proto_kernel(where_ref, proto_ref, full_ref, unit_ref, back_ref, norm_ref):
    p = proto_ref[...].astype(F32)
    norm = jnp.sqrt(jnp.sum(p * p, axis=0, keepdims=True) + EPSILON)
    full = p / norm
    full_ref[...] = full
    unit_ref[...] = full.astype(BF16)
    back_ref[...] = full.T.astype(BF16)
    norm_ref[...] = norm


def core_rows(where_ref, side, half):
    return pl.ds(pl.multiple_of(lax.rem(where_ref[0] + side, 2) * half, half), half)


def write_lanes(out_ref, value, row, copies):
    for m in range(copies):
        out_ref[m, pl.ds(row, 1), :] = value


def write_rows(out_ref, acc_ref, first=0):
    pieces = []
    for i in range(acc_ref.shape[0] // LANES):
        tile = acc_ref[i * LANES : (i + 1) * LANES, :].T
        pieces.append(jnp.sum(tile, axis=0, keepdims=True))
    value = jnp.concatenate(pieces, axis=0)
    for m in range(out_ref.shape[0]):
        out_ref[m, first : first + 8, :] = value


def teacher_exp_kernel(where_ref, own_ref, other_ref, unit_ref, e_ref, col_ref):
    half = own_ref.shape[0]
    wide = unit_ref.shape[1]
    block = 256
    for w in range(wide // WIDE):
        columns = pl.ds(w * WIDE, WIDE)
        unit = unit_ref[:, columns]
        total = jnp.zeros((8, WIDE), F32)
        for side, ref in enumerate((own_ref, other_ref)):
            place = core_rows(where_ref, side, half)
            for b in range(half // block):
                z = ref[b * block : (b + 1) * block, :].astype(BF16)
                e = jnp.exp(
                    jnp.dot(z, unit, preferred_element_type=F32) * (1.0 / TEACHER_TEMP)
                )
                e_ref[pl.ds(place.start + b * block, block), columns] = e
                for g in range(block // 8):
                    total += e[g * 8 : (g + 1) * 8, :]
        total = jnp.sum(total, axis=0, keepdims=True)
        for i in range(WIDE // LANES):
            write_lanes(
                col_ref, total[:, i * LANES : (i + 1) * LANES], w * (WIDE // LANES) + i, Z
            )


def student_exp_kernel(
    where_ref, own_ref, other_ref, unit_ref, s_ref, mass_ref, turned_ref
):
    half = own_ref.shape[0]
    wide = unit_ref.shape[1]
    block = 256
    for side, ref in enumerate((own_ref, other_ref)):
        turned_ref[:, core_rows(where_ref, side, half)] = ref[...].T.astype(BF16)
    for w in range(wide // WIDE):
        columns = pl.ds(w * WIDE, WIDE)
        unit = unit_ref[:, columns]
        for side, ref in enumerate((own_ref, other_ref)):
            place = core_rows(where_ref, side, half)
            for b in range(half // block):
                rows = pl.ds(place.start + b * block, block)
                z = ref[b * block : (b + 1) * block, :].astype(BF16)
                s = jnp.exp(
                    jnp.dot(z, unit, preferred_element_type=F32) * (1.0 / STUDENT_TEMP)
                )
                s_ref[rows, columns] = s
                part = sum(s[:, j * LANES : (j + 1) * LANES] for j in range(WIDE // LANES))
                if w:
                    mass_ref[rows, :] += part
                else:
                    mass_ref[rows, :] = part


def row_kernel(e_ref, parts_ref, out_ref, c_ref, acc_ref):
    c = 1.0 / jnp.sum(parts_ref[...], axis=0)
    c_ref[...] = c
    tiles = c.shape[0]
    block = 64

    def body(b, carry):
        rows = pl.ds(pl.multiple_of(b * block, block), block)
        acc = jnp.zeros((block, LANES), F32)
        for j in range(tiles):
            acc += e_ref[rows, j * LANES : (j + 1) * LANES] * c[j : j + 1, :]
        acc_ref[rows, :] = acc
        return carry

    lax.fori_loop(0, e_ref.shape[0] // block, body, 0)
    write_rows(out_ref, acc_ref)


def row_mass_kernel(e_ref, parts_ref, mass_ref, out_ref, c_ref, acc_ref):
    row_kernel(e_ref, parts_ref, out_ref, c_ref, acc_ref)
    write_rows(out_ref, mass_ref, first=8)


def spread(ref, value):
    for i in range(value.shape[0]):
        ref[i * LANES : (i + 1) * LANES, :] = jnp.broadcast_to(
            value[i : i + 1, :], (LANES, LANES)
        ).T


def col_kernel(e_ref, parts_ref, out_ref, r_ref):
    spread(r_ref, 1.0 / jnp.sum(parts_ref[:, :8, :], axis=0))
    tiles = e_ref.shape[1] // LANES
    block = 32

    def body(b, acc):
        rows = pl.ds(pl.multiple_of(b * block, block), block)
        r = r_ref[rows, :]
        out = []
        for j in range(tiles):
            value = acc[j]
            tile = e_ref[rows, j * LANES : (j + 1) * LANES] * r
            for g in range(block // 8):
                value = value + tile[g * 8 : (g + 1) * 8, :]
            out.append(value)
        return tuple(out)

    zero = tuple(jnp.zeros((8, LANES), F32) for _ in range(tiles))
    acc = lax.fori_loop(0, e_ref.shape[0] // block, body, zero)
    value = jnp.concatenate([jnp.sum(a, axis=0, keepdims=True) for a in acc], axis=0)
    for m in range(Z):
        out_ref[m] = value


def diff_kernel(
    e_ref, s_ref, c_ref, parts_ref, mass_ref, diff_ref, r_ref, m_ref
):
    scale = 1.0 / STUDENT_TEMP
    spread(r_ref, scale / jnp.sum(parts_ref[...], axis=0))
    spread(m_ref, scale / jnp.sum(mass_ref[:, 8:, :], axis=0))
    tiles = e_ref.shape[1] // LANES
    block = 16

    def body(b, carry):
        rows = pl.ds(pl.multiple_of(b * block, block), block)
        r = r_ref[rows, :]
        m = m_ref[rows, :]
        for j in range(tiles):
            lanes = slice(j * LANES, (j + 1) * LANES)
            targets = (r * e_ref[rows, lanes]) * c_ref[j : j + 1, :]
            probs = s_ref[rows, lanes] * m
            diff_ref[rows, lanes] = (probs - targets).astype(BF16)
        return carry

    lax.fori_loop(0, e_ref.shape[0] // block, body, 0)


def token_kernel(where_ref, diff_ref, back_ref, own_ref, give_ref):
    for side, out in enumerate((own_ref, give_ref)):
        rows = core_rows(where_ref, side, out.shape[0])
        out[...] = jnp.dot(diff_ref[rows, :], back_ref[...], preferred_element_type=F32)


def grad_kernel(where_ref, diff_ref, full_ref, norm_ref, turned_ref, *refs):
    outs, (g_ref, sems) = refs[:-2], refs[-2:]
    wide = full_ref.shape[1]
    for w in range(wide // WIDE):
        columns = slice(w * WIDE, (w + 1) * WIDE)
        grad = jnp.dot(turned_ref[...], diff_ref[:, columns], preferred_element_type=F32)
        full = full_ref[:, columns]
        proj = jnp.sum(full.astype(BF16).astype(F32) * grad, axis=0, keepdims=True)
        g_ref[:, columns] = (grad - full * proj) / norm_ref[:, columns]
    core, z = where_ref[0], where_ref[1]
    deep = g_ref.shape[0] // Z
    near = deep // 2
    pairs = []
    for j in range(Z):
        top = lax.rem(z + j, Z) * deep
        for side in range(2):
            take = pl.multiple_of(top + lax.rem(core + side, 2) * near, near)
            if j == 4:
                out = outs[4 + side]
            else:
                out = outs[j + (j > 4)].at[pl.ds(side * near, near), :]
            pairs.append((g_ref.at[pl.ds(take, near), :], out))
    for copy in fetch(pairs, sems):
        copy.wait()


def share_kernel(parts_ref, out_ref):
    total = sum(parts_ref[i] for i in range(parts_ref.shape[0]))
    for m in range(out_ref.shape[0]):
        out_ref[m] = total


def last_kernel(gz_ref, feats_ref, mask_ref, out_ref):
    slots = mask_ref.shape[1]
    for i in range(out_ref.shape[0]):
        mask = mask_ref[i : i + 1, :]
        xs, norm = masked_rows(feats_ref[i], mask)
        zsf = xs / norm
        gz = gz_ref[i * slots : (i + 1) * slots, :]
        proj = jnp.sum(zsf * gz, axis=1, keepdims=True)
        grad = (gz - zsf * proj) / norm
        hot = one_hot_t(mask, out_ref.shape[1], BF16)
        high = grad.astype(BF16)
        low = (grad - high.astype(F32)).astype(BF16)
        out_ref[i] = jnp.dot(hot, high, preferred_element_type=F32) + jnp.dot(
            hot, low, preferred_element_type=F32
        )


def sum_kernel(a_ref, b_ref, out_ref):
    out_ref[...] = a_ref[...] + b_ref[...]


def first_step_kernel(low):
    def kernel(rel_hbm, got_ref, out_ref, sem):
        for copy in fetch(((rel_hbm, out_ref),), sem):
            copy.wait()
        near = got_ref.shape[0]
        rows = slice(near, 2 * near) if low else slice(0, near)
        out_ref[rows, :] += got_ref[...]

    return kernel


def step_kernel(rel_hbm, got_ref, out_ref, sem):
    for copy in fetch(((rel_hbm, out_ref),), sem):
        copy.wait()
    out_ref[...] += got_ref[...]


def last_sum_kernel(rel_hbm, up_ref, down_ref, keep_ref, give_ref, rel, sem):
    for copy in fetch(((rel_hbm, rel),), sem):
        copy.wait()
    near = keep_ref.shape[0]
    total = rel[...] + (up_ref[...] + down_ref[...])
    keep_ref[...] = total[:near, :]
    give_ref[...] = total[near:, :]


def place_kernel(where_ref, keep_ref, got_ref, out_ref):
    wide = keep_ref.shape[1]
    for side, ref in enumerate((keep_ref, got_ref)):
        first = lax.rem(where_ref[0] + side, 2) * wide
        out_ref[:, pl.ds(pl.multiple_of(first, wide), wide)] = ref[...]


def shape(*dims, dtype=F32):
    return jax.ShapeDtypeStruct(dims, dtype)


def hold(*dims, dtype=F32):
    return pltpu.VMEM(dims, dtype)


def far(*dims):
    return pltpu.HBM(dims, F32)


def in_hbm(x):
    return pltpu.with_memory_space_constraint(x, pltpu.HBM)


def other_core(x):
    return lax.ppermute(x, "batch", [(i, i ^ 1) for i in range(RING)])


def along_z(x, d):
    return lax.ppermute(
        x, "batch", [(i, ((i // 2 + d) % Z) * 2 + i % 2) for i in range(RING)]
    )


def all_columns(x):
    return lax.all_to_all(x, "batch", 0, 0, axis_index_groups=Z_GROUPS)


def all_rows(x):
    return lax.all_to_all(x, ("batch", "proto"), 0, 0, axis_index_groups=ROW_GROUPS)


def tie(x, y):
    return lax.optimization_barrier((x, y))[0]


def on_device(teacher_feats, student_feats, prototypes, mask_index):
    images, patches, width = teacher_feats.shape
    slots = mask_index.shape[1]
    own = images * slots
    tokens = 2 * own
    wide = prototypes.shape[1] // 2
    lane_tiles = wide // LANES
    row_tiles = tokens // LANES
    place = lax.axis_index("batch")
    where = jnp.stack([lax.rem(place, 2), lax.div(place, 2)]).astype(jnp.int32)
    scalars = pl.BlockSpec(memory_space=pltpu.SMEM)

    def placed(kernel, outs, *args, **kw):
        return pl.pallas_call(
            kernel,
            in_specs=[scalars] + [whole()] * len(args),
            out_specs=[whole()] * len(outs),
            out_shape=outs,
            scratch_shapes=kw.get("scratch", []),
            compiler_params=params(16),
            cost_estimate=kw.get("cost_estimate"),
        )(where, *args)

    zt, zs = pl.pallas_call(
        prep_kernel,
        in_specs=[pl.BlockSpec(memory_space=pl.ANY)] * 3,
        out_specs=[whole()] * 2,
        out_shape=[shape(own, width), shape(own, width)],
        scratch_shapes=[
            VMEM(teacher_feats.shape, BF16), VMEM(student_feats.shape, BF16),
            VMEM(mask_index.shape, jnp.int32), pltpu.SemaphoreType.DMA((3,)),
        ],
        compiler_params=params(16),
    )(in_hbm(teacher_feats), in_hbm(student_feats), in_hbm(mask_index))
    zt_other = other_core(zt)
    zs_other = other_core(zs)
    steps = 2
    column_spec = pl.BlockSpec((width, wide // steps), lambda j, w: (0, j))
    full, unit, back, p_norm = pl.pallas_call(
        proto_kernel,
        grid_spec=pltpu.PrefetchScalarGridSpec(
            num_scalar_prefetch=1,
            grid=(steps,),
            in_specs=[
                pl.BlockSpec((width, wide // steps), lambda j, w: (0, w[0] * steps + j))
            ],
            out_specs=[
                column_spec, column_spec,
                pl.BlockSpec((wide // steps, width), lambda j, w: (j, 0)),
                pl.BlockSpec((1, wide // steps), lambda j, w: (0, j)),
            ],
        ),
        out_shape=[
            shape(width, wide), shape(width, wide, dtype=BF16),
            shape(wide, width, dtype=BF16), shape(1, wide),
        ],
        compiler_params=params(16),
    )(where, in_hbm(prototypes))

    exp_cost = cost(2 * tokens * wide * width, tokens * wide)
    e, col_out = placed(
        teacher_exp_kernel,
        [hold(tokens, wide), shape(Z, lane_tiles, LANES)],
        zt, zt_other, unit, cost_estimate=exp_cost,
    )
    s, mass_acc, turned = placed(
        student_exp_kernel,
        [hold(tokens, wide), shape(tokens, LANES), shape(width, tokens, dtype=BF16)],
        zs, zs_other, unit, cost_estimate=exp_cost,
    )
    col_out = tie(col_out, mass_acc)

    mass = None
    for sweep in range(ITERS):
        col_parts = all_columns(col_out)
        extra = [mass_acc] if sweep == 0 else []
        row_out, c = call(
            row_kernel if sweep else row_mass_kernel,
            [shape(ROWS, row_tiles * (1 + len(extra)), LANES), shape(lane_tiles, LANES)],
            e, col_parts, *extra,
            scratch=[VMEM((tokens, LANES), F32)],
        )
        row_parts = all_rows(row_out)
        if sweep == 0:
            mass = row_parts
        if sweep < ITERS - 1:
            (col_out,) = call(
                col_kernel, [shape(Z, lane_tiles, LANES)], e, row_parts,
                scratch=[VMEM((tokens, LANES), F32)],
            )

    (diff,) = call(
        diff_kernel, [shape(tokens, wide, dtype=BF16)], e, s, c, row_parts, mass,
        scratch=[VMEM((tokens, LANES), F32), VMEM((tokens, LANES), F32)],
    )
    gz, gz_give = placed(
        token_kernel, [shape(own, width)] * 2, diff, back,
        cost_estimate=cost(2 * tokens * wide * width),
    )
    gz_got = other_core(gz_give)
    deep = width // Z
    near = deep // 2
    anywhere = pl.BlockSpec(memory_space=pltpu.HBM)
    rel = pl.pallas_call(
        grad_kernel,
        in_specs=[scalars] + [whole()] * 4,
        out_specs=[anywhere] * 9,
        out_shape=[far(deep, wide)] * 4 + [far(near, wide)] * 2 + [far(deep, wide)] * 3,
        scratch_shapes=[VMEM((width, wide), F32), pltpu.SemaphoreType.DMA((2 * Z,))],
        compiler_params=params(16),
        cost_estimate=cost(2 * tokens * wide * width),
    )(where, tie(diff, (gz, gz_give)), full, p_norm, turned)

    def step(kernel, term, got, work=10**9):
        return pl.pallas_call(
            kernel,
            in_specs=[anywhere, whole()],
            out_specs=whole(),
            out_shape=shape(deep, wide),
            scratch_shapes=[pltpu.SemaphoreType.DMA((1,))],
            compiler_params=params(16),
            cost_estimate=cost(work) if work else None,
        )(term, got)

    up, down = along_z(rel[4], 1), along_z(rel[5], -1)
    up = step(first_step_kernel(False), rel[3], up)
    down = step(first_step_kernel(True), rel[6], down)
    (gz,) = call(sum_kernel, [shape(own, width)], gz, gz_got)
    gz_parts = lax.all_to_all(
        tie(gz, rel).reshape(RING, own // RING, width), "proto", 0, 0
    )
    (gz_share,) = call(share_kernel, [shape(RING, own // RING, width)], gz_parts)
    up, down = along_z(up, 1), along_z(down, -1)
    up, down = tie((up, down), gz_share)
    up = step(step_kernel, rel[2], up)
    down = step(step_kernel, rel[7], down)
    gz = lax.all_to_all(gz_share, "proto", 0, 0).reshape(own, width)
    (grad_student,) = call(
        last_kernel, [shape(images, patches, width)], gz, student_feats, mask_index
    )
    up, down = along_z(up, 1), along_z(down, -1)
    up, down = tie((up, down), gz)
    up = step(step_kernel, rel[1], up)
    down = step(step_kernel, rel[8], down)
    up, down = along_z(up, 1), along_z(down, -1)
    up, down, grad_student = lax.optimization_barrier((up, down, grad_student))
    keep, give = pl.pallas_call(
        last_sum_kernel,
        in_specs=[anywhere, whole(), whole()],
        out_specs=[whole()] * 2,
        out_shape=[shape(near, wide)] * 2,
        scratch_shapes=[VMEM((deep, wide), F32), pltpu.SemaphoreType.DMA((1,))],
        compiler_params=params(16),
    )(rel[0], up, down)
    got = other_core(give)
    (grad_protos,) = placed(place_kernel, [shape(near, 2 * wide)], keep, got)
    return (grad_student, grad_protos)


def solution(mesh):
    in_specs = (P("batch", None, None), P("batch", None, None), P(None, "proto"), P("batch", None))
    out_specs = (P("batch", None, None), P("batch", "proto"))
    return jax.shard_map(
        on_device, mesh=mesh, in_specs=in_specs, out_specs=out_specs, check_vma=False
    )
```

```python
import jax
import jax.numpy as jnp
from jax import lax
from jax.experimental import pallas as pl
from jax.experimental.pallas import tpu as pltpu
from jax.sharding import PartitionSpec as P

ITERS = 3
TEACHER_TEMP = 0.04
STUDENT_TEMP = 0.1
EPSILON = 1e-06
LANES = 128
Z = 8
RING = 16
ROWS = 32
WIDE = 1024
MIB = 1024 * 1024
F32 = jnp.float32
BF16 = jnp.bfloat16

VMEM = pltpu.VMEM
Z_GROUPS = [[2 * z + c for z in range(Z)] for c in range(2)]
ROW_GROUPS = [[ROWS * z + i for i in range(ROWS)] for z in range(Z)]


def whole():
    return pl.BlockSpec(memory_space=VMEM)


def cost(flops, transcendentals=0, moved=0):
    return pl.CostEstimate(
        flops=flops, transcendentals=transcendentals, bytes_accessed=moved
    )


def params(vmem):
    return pltpu.CompilerParams(vmem_limit_bytes=vmem * MIB)


def call(kernel, outs, *args, scratch=(), vmem=16, cost_estimate=None):
    return pl.pallas_call(
        kernel,
        out_shape=outs,
        in_specs=[whole()] * len(args),
        out_specs=[whole()] * len(outs),
        scratch_shapes=list(scratch),
        compiler_params=params(vmem),
        cost_estimate=cost_estimate,
    )(*args)


def one_hot_t(mask_row, patches, dtype):
    slots = mask_row.shape[1]
    patch = lax.broadcasted_iota(jnp.int32, (patches, slots), 0)
    return jnp.where(patch == mask_row, 1.0, 0.0).astype(dtype)


def fetch(pairs, sems):
    copies = [pltpu.make_async_copy(src, dst, sems.at[i]) for i, (src, dst) in enumerate(pairs)]
    for copy in copies:
        copy.start()
    return copies


def masked_rows(feats, mask_row):
    hot = one_hot_t(mask_row, feats.shape[0], BF16)
    rows = lax.dot_general(hot, feats, (((0,), (0,)), ((), ())), preferred_element_type=F32)
    return rows, jnp.sqrt(jnp.sum(rows * rows, axis=1, keepdims=True) + EPSILON)


def prep_kernel(
    teacher_hbm, student_hbm, mask_hbm, zt_ref, zs_ref, teacher_ref, student_ref, mask_ref, sems
):
    mask_copy, teacher_copy, student_copy = fetch(
        ((mask_hbm, mask_ref), (teacher_hbm, teacher_ref), (student_hbm, student_ref)), sems
    )
    mask_copy.wait()
    slots = mask_ref.shape[1]
    for copy, feats, out in (
        (teacher_copy, teacher_ref, zt_ref), (student_copy, student_ref, zs_ref)
    ):
        copy.wait()
        for i in range(feats.shape[0]):
            rows, norm = masked_rows(feats[i], mask_ref[i : i + 1, :])
            out[i * slots : (i + 1) * slots, :] = (rows / norm).astype(BF16).astype(F32)


def proto_kernel(where_ref, proto_ref, full_ref, unit_ref, back_ref, scale_ref):
    p = proto_ref[...].astype(F32)
    scale = 1.0 / jnp.sqrt(jnp.sum(p * p, axis=0, keepdims=True) + EPSILON)
    full = p * scale
    full_ref[...] = full
    unit_ref[...] = full.astype(BF16)
    back_ref[...] = full.T.astype(BF16)
    scale_ref[...] = scale


def core_rows(where_ref, side, half):
    return pl.ds(pl.multiple_of(lax.rem(where_ref[0] + side, 2) * half, half), half)


def write_lanes(out_ref, value, row, copies):
    for m in range(copies):
        out_ref[m, pl.ds(row, 1), :] = value


def write_rows(out_ref, acc_ref, first=0):
    pieces = []
    for i in range(acc_ref.shape[0] // LANES):
        tile = acc_ref[i * LANES : (i + 1) * LANES, :].T
        pieces.append(jnp.sum(tile, axis=0, keepdims=True))
    value = jnp.concatenate(pieces, axis=0)
    for m in range(out_ref.shape[0]):
        out_ref[m, first : first + 8, :] = value


def teacher_exp_kernel(where_ref, own_ref, other_ref, unit_ref, e_ref, col_ref):
    half = own_ref.shape[0]
    wide = unit_ref.shape[1]
    block = 256
    for w in range(wide // WIDE):
        columns = pl.ds(w * WIDE, WIDE)
        unit = unit_ref[:, columns]
        total = jnp.zeros((8, WIDE), F32)
        for side, ref in enumerate((own_ref, other_ref)):
            place = core_rows(where_ref, side, half)
            for b in range(half // block):
                z = ref[b * block : (b + 1) * block, :].astype(BF16)
                e = jnp.exp(
                    jnp.dot(z, unit, preferred_element_type=F32) * (1.0 / TEACHER_TEMP)
                )
                e_ref[pl.ds(place.start + b * block, block), columns] = e
                for g in range(block // 8):
                    total += e[g * 8 : (g + 1) * 8, :]
        total = jnp.sum(total, axis=0, keepdims=True)
        for i in range(WIDE // LANES):
            write_lanes(
                col_ref, total[:, i * LANES : (i + 1) * LANES], w * (WIDE // LANES) + i, Z
            )


def student_exp_kernel(
    where_ref, own_ref, other_ref, unit_ref, s_ref, mass_ref, turned_ref
):
    half = own_ref.shape[0]
    wide = unit_ref.shape[1]
    block = 256
    for side, ref in enumerate((own_ref, other_ref)):
        turned_ref[:, core_rows(where_ref, side, half)] = ref[...].T.astype(BF16)
    for w in range(wide // WIDE):
        columns = pl.ds(w * WIDE, WIDE)
        unit = unit_ref[:, columns]
        for side, ref in enumerate((own_ref, other_ref)):
            place = core_rows(where_ref, side, half)
            for b in range(half // block):
                rows = pl.ds(place.start + b * block, block)
                z = ref[b * block : (b + 1) * block, :].astype(BF16)
                s = jnp.exp(
                    jnp.dot(z, unit, preferred_element_type=F32) * (1.0 / STUDENT_TEMP)
                )
                s_ref[rows, columns] = s
                part = sum(s[:, j * LANES : (j + 1) * LANES] for j in range(WIDE // LANES))
                if w:
                    mass_ref[rows, :] += part
                else:
                    mass_ref[rows, :] = part


def row_kernel(e_ref, parts_ref, out_ref, c_ref, acc_ref):
    c = 1.0 / jnp.sum(parts_ref[...], axis=0)
    c_ref[...] = c
    tiles = c.shape[0]
    block = 64

    def body(b, carry):
        rows = pl.ds(pl.multiple_of(b * block, block), block)
        acc = jnp.zeros((block, LANES), F32)
        for j in range(tiles):
            acc += e_ref[rows, j * LANES : (j + 1) * LANES] * c[j : j + 1, :]
        acc_ref[rows, :] = acc
        return carry

    lax.fori_loop(0, e_ref.shape[0] // block, body, 0)
    write_rows(out_ref, acc_ref)


def row_mass_kernel(e_ref, parts_ref, mass_ref, out_ref, c_ref, acc_ref):
    row_kernel(e_ref, parts_ref, out_ref, c_ref, acc_ref)
    write_rows(out_ref, mass_ref, first=8)


def spread(ref, value):
    for i in range(value.shape[0]):
        ref[i * LANES : (i + 1) * LANES, :] = jnp.broadcast_to(
            value[i : i + 1, :], (LANES, LANES)
        ).T


def col_kernel(e_ref, parts_ref, out_ref, r_ref):
    spread(r_ref, 1.0 / jnp.sum(parts_ref[:, :8, :], axis=0))
    tiles = e_ref.shape[1] // LANES
    block = 32

    def body(b, acc):
        rows = pl.ds(pl.multiple_of(b * block, block), block)
        r = r_ref[rows, :]
        out = []
        for j in range(tiles):
            value = acc[j]
            tile = e_ref[rows, j * LANES : (j + 1) * LANES] * r
            for g in range(block // 8):
                value = value + tile[g * 8 : (g + 1) * 8, :]
            out.append(value)
        return tuple(out)

    zero = tuple(jnp.zeros((8, LANES), F32) for _ in range(tiles))
    acc = lax.fori_loop(0, e_ref.shape[0] // block, body, zero)
    value = jnp.concatenate([jnp.sum(a, axis=0, keepdims=True) for a in acc], axis=0)
    for m in range(Z):
        out_ref[m] = value


def diff_kernel(
    e_ref, s_ref, c_ref, parts_ref, mass_ref, diff_ref, r_ref, m_ref
):
    scale = 1.0 / STUDENT_TEMP
    spread(r_ref, scale / jnp.sum(parts_ref[...], axis=0))
    spread(m_ref, scale / jnp.sum(mass_ref[:, 8:, :], axis=0))
    tiles = e_ref.shape[1] // LANES
    block = 16

    def body(b, carry):
        rows = pl.ds(pl.multiple_of(b * block, block), block)
        r = r_ref[rows, :]
        m = m_ref[rows, :]
        for j in range(tiles):
            lanes = slice(j * LANES, (j + 1) * LANES)
            targets = (r * e_ref[rows, lanes]) * c_ref[j : j + 1, :]
            probs = s_ref[rows, lanes] * m
            diff_ref[rows, lanes] = (probs - targets).astype(BF16)
        return carry

    lax.fori_loop(0, e_ref.shape[0] // block, body, 0)


def token_kernel(where_ref, diff_ref, back_ref, own_ref, give_ref):
    for side, out in enumerate((own_ref, give_ref)):
        rows = core_rows(where_ref, side, out.shape[0])
        out[...] = jnp.dot(diff_ref[rows, :], back_ref[...], preferred_element_type=F32)


def grad_kernel(where_ref, diff_ref, full_ref, scale_ref, turned_ref, *refs):
    outs, (g_ref, sems) = refs[:-2], refs[-2:]
    wide = full_ref.shape[1]
    core, z = where_ref[0], where_ref[1]
    deep = g_ref.shape[0] // Z
    near = deep // 2
    copies = []
    for w in range(wide // WIDE):
        columns = slice(w * WIDE, (w + 1) * WIDE)
        grad = jnp.dot(turned_ref[...], diff_ref[:, columns], preferred_element_type=F32)
        full = full_ref[:, columns]
        proj = jnp.sum(full.astype(BF16).astype(F32) * grad, axis=0, keepdims=True)
        g_ref[:, columns] = (grad - full * proj) * scale_ref[:, columns]
        pairs = []
        for j in range(Z):
            top = lax.rem(z + j, Z) * deep
            for side in range(2):
                take = pl.multiple_of(top + lax.rem(core + side, 2) * near, near)
                if j == 4:
                    out = outs[4 + side].at[:, columns]
                else:
                    out = outs[j + (j > 4)].at[pl.ds(side * near, near), columns]
                pairs.append((g_ref.at[pl.ds(take, near), columns], out))
        copies += fetch(pairs, sems.at[w])
    for copy in copies:
        copy.wait()


def share_kernel(parts_ref, out_ref):
    total = sum(parts_ref[i] for i in range(parts_ref.shape[0]))
    for m in range(out_ref.shape[0]):
        out_ref[m] = total


def last_kernel(gz_ref, feats_ref, mask_ref, out_ref):
    slots = mask_ref.shape[1]
    for i in range(out_ref.shape[0]):
        mask = mask_ref[i : i + 1, :]
        xs, norm = masked_rows(feats_ref[i], mask)
        zsf = xs / norm
        gz = gz_ref[i * slots : (i + 1) * slots, :]
        proj = jnp.sum(zsf * gz, axis=1, keepdims=True)
        grad = (gz - zsf * proj) / norm
        hot = one_hot_t(mask, out_ref.shape[1], BF16)
        high = grad.astype(BF16)
        low = (grad - high.astype(F32)).astype(BF16)
        out_ref[i] = jnp.dot(hot, high, preferred_element_type=F32) + jnp.dot(
            hot, low, preferred_element_type=F32
        )


def sum_kernel(a_ref, b_ref, out_ref):
    out_ref[...] = a_ref[...] + b_ref[...]


def first_step_kernel(low):
    def kernel(rel_hbm, got_ref, out_ref, sem):
        for copy in fetch(((rel_hbm, out_ref),), sem):
            copy.wait()
        near = got_ref.shape[0]
        rows = slice(near, 2 * near) if low else slice(0, near)
        out_ref[rows, :] += got_ref[...]

    return kernel


def step_kernel(rel_hbm, got_ref, out_ref, sem):
    for copy in fetch(((rel_hbm, out_ref),), sem):
        copy.wait()
    out_ref[...] += got_ref[...]


def last_sum_kernel(rel_hbm, up_ref, down_ref, keep_ref, give_ref, rel, sem):
    for copy in fetch(((rel_hbm, rel),), sem):
        copy.wait()
    near = keep_ref.shape[0]
    total = rel[...] + (up_ref[...] + down_ref[...])
    keep_ref[...] = total[:near, :]
    give_ref[...] = total[near:, :]


def place_kernel(where_ref, keep_ref, got_ref, out_ref):
    wide = keep_ref.shape[1]
    for side, ref in enumerate((keep_ref, got_ref)):
        first = lax.rem(where_ref[0] + side, 2) * wide
        out_ref[:, pl.ds(pl.multiple_of(first, wide), wide)] = ref[...]


def shape(*dims, dtype=F32):
    return jax.ShapeDtypeStruct(dims, dtype)


def hold(*dims, dtype=F32):
    return pltpu.VMEM(dims, dtype)


def far(*dims):
    return pltpu.HBM(dims, F32)


def in_hbm(x):
    return pltpu.with_memory_space_constraint(x, pltpu.HBM)


def other_core(x):
    return lax.ppermute(x, "batch", [(i, i ^ 1) for i in range(RING)])


def along_z(x, d):
    return lax.ppermute(
        x, "batch", [(i, ((i // 2 + d) % Z) * 2 + i % 2) for i in range(RING)]
    )


def all_columns(x):
    return lax.all_to_all(x, "batch", 0, 0, axis_index_groups=Z_GROUPS)


def all_rows(x):
    return lax.all_to_all(x, ("batch", "proto"), 0, 0, axis_index_groups=ROW_GROUPS)


def tie(x, y):
    return lax.optimization_barrier((x, y))[0]


def on_device(teacher_feats, student_feats, prototypes, mask_index):
    images, patches, width = teacher_feats.shape
    slots = mask_index.shape[1]
    own = images * slots
    tokens = 2 * own
    wide = prototypes.shape[1] // 2
    lane_tiles = wide // LANES
    row_tiles = tokens // LANES
    place = lax.axis_index("batch")
    where = jnp.stack([lax.rem(place, 2), lax.div(place, 2)]).astype(jnp.int32)
    scalars = pl.BlockSpec(memory_space=pltpu.SMEM)

    def placed(kernel, outs, *args, **kw):
        return pl.pallas_call(
            kernel,
            in_specs=[scalars] + [whole()] * len(args),
            out_specs=[whole()] * len(outs),
            out_shape=outs,
            scratch_shapes=kw.get("scratch", []),
            compiler_params=params(16),
            cost_estimate=kw.get("cost_estimate"),
        )(where, *args)

    zt, zs = pl.pallas_call(
        prep_kernel,
        in_specs=[pl.BlockSpec(memory_space=pl.ANY)] * 3,
        out_specs=[whole()] * 2,
        out_shape=[shape(own, width), shape(own, width)],
        scratch_shapes=[
            VMEM(teacher_feats.shape, BF16), VMEM(student_feats.shape, BF16),
            VMEM(mask_index.shape, jnp.int32), pltpu.SemaphoreType.DMA((3,)),
        ],
        compiler_params=params(16),
    )(in_hbm(teacher_feats), in_hbm(student_feats), in_hbm(mask_index))
    zt_other = other_core(zt)
    zs_other = other_core(zs)
    steps = 2
    column_spec = pl.BlockSpec((width, wide // steps), lambda j, w: (0, j))
    full, unit, back, p_scale = pl.pallas_call(
        proto_kernel,
        grid_spec=pltpu.PrefetchScalarGridSpec(
            num_scalar_prefetch=1,
            grid=(steps,),
            in_specs=[
                pl.BlockSpec((width, wide // steps), lambda j, w: (0, w[0] * steps + j))
            ],
            out_specs=[
                column_spec, column_spec,
                pl.BlockSpec((wide // steps, width), lambda j, w: (j, 0)),
                pl.BlockSpec((1, wide // steps), lambda j, w: (0, j)),
            ],
        ),
        out_shape=[
            shape(width, wide), shape(width, wide, dtype=BF16),
            shape(wide, width, dtype=BF16), shape(1, wide),
        ],
        compiler_params=params(16),
    )(where, in_hbm(prototypes))

    exp_cost = cost(2 * tokens * wide * width, tokens * wide)
    e, col_out = placed(
        teacher_exp_kernel,
        [hold(tokens, wide), shape(Z, lane_tiles, LANES)],
        zt, zt_other, unit, cost_estimate=exp_cost,
    )
    s, mass_acc, turned = placed(
        student_exp_kernel,
        [hold(tokens, wide), shape(tokens, LANES), shape(width, tokens, dtype=BF16)],
        zs, zs_other, unit, cost_estimate=exp_cost,
    )
    col_out = tie(col_out, mass_acc)

    mass = None
    for sweep in range(ITERS):
        col_parts = all_columns(col_out)
        extra = [mass_acc] if sweep == 0 else []
        row_out, c = call(
            row_kernel if sweep else row_mass_kernel,
            [shape(ROWS, row_tiles * (1 + len(extra)), LANES), shape(lane_tiles, LANES)],
            e, col_parts, *extra,
            scratch=[VMEM((tokens, LANES), F32)],
        )
        row_parts = all_rows(row_out)
        if sweep == 0:
            mass = row_parts
        if sweep < ITERS - 1:
            (col_out,) = call(
                col_kernel, [shape(Z, lane_tiles, LANES)], e, row_parts,
                scratch=[VMEM((tokens, LANES), F32)],
            )

    (diff,) = call(
        diff_kernel, [shape(tokens, wide, dtype=BF16)], e, s, c, row_parts, mass,
        scratch=[VMEM((tokens, LANES), F32), VMEM((tokens, LANES), F32)],
    )
    gz, gz_give = placed(
        token_kernel, [shape(own, width)] * 2, diff, back,
        cost_estimate=cost(2 * tokens * wide * width),
    )
    gz_got = other_core(gz_give)
    deep = width // Z
    near = deep // 2
    anywhere = pl.BlockSpec(memory_space=pltpu.HBM)
    rel = pl.pallas_call(
        grad_kernel,
        in_specs=[scalars] + [whole()] * 4,
        out_specs=[anywhere] * 9,
        out_shape=[far(deep, wide)] * 4 + [far(near, wide)] * 2 + [far(deep, wide)] * 3,
        scratch_shapes=[VMEM((width, wide), F32), pltpu.SemaphoreType.DMA((wide // WIDE, 2 * Z))],
        compiler_params=params(16),
        cost_estimate=cost(2 * tokens * wide * width),
    )(where, tie(diff, (gz, gz_give)), full, p_scale, turned)

    def step(kernel, term, got, work=0):
        return pl.pallas_call(
            kernel,
            in_specs=[anywhere, whole()],
            out_specs=whole(),
            out_shape=shape(deep, wide),
            scratch_shapes=[pltpu.SemaphoreType.DMA((1,))],
            compiler_params=params(16),
            cost_estimate=cost(work) if work else None,
        )(term, got)

    up, down = along_z(rel[4], 1), along_z(rel[5], -1)
    up = step(first_step_kernel(False), rel[3], up, 2 * 10**9)
    down = step(first_step_kernel(True), rel[6], down, 2 * 10**9)
    (gz,) = call(sum_kernel, [shape(own, width)], gz, gz_got)
    gz_parts = lax.all_to_all(
        tie(gz, rel).reshape(RING, own // RING, width), "proto", 0, 0
    )
    (gz_share,) = call(share_kernel, [shape(RING, own // RING, width)], gz_parts)
    up, down = along_z(up, 1), along_z(down, -1)
    up = step(step_kernel, rel[2], up)
    down = step(step_kernel, rel[7], down)
    gz = lax.all_to_all(gz_share, "proto", 0, 0).reshape(own, width)
    (grad_student,) = call(
        last_kernel, [shape(images, patches, width)], gz, student_feats, mask_index
    )
    up, down = along_z(up, 1), along_z(down, -1)
    up, down = tie((up, down), gz_share)
    up = step(step_kernel, rel[1], up)
    down = step(step_kernel, rel[8], down)
    up, down = along_z(up, 1), along_z(down, -1)
    up = tie(up, gz)
    keep, give = pl.pallas_call(
        last_sum_kernel,
        in_specs=[anywhere, whole(), whole()],
        out_specs=[whole()] * 2,
        out_shape=[shape(near, wide)] * 2,
        scratch_shapes=[VMEM((deep, wide), F32), pltpu.SemaphoreType.DMA((1,))],
        compiler_params=params(16),
    )(rel[0], up, down)
    got = other_core(give)
    (grad_protos,) = placed(place_kernel, [shape(near, 2 * wide)], keep, got)
    return (grad_student, grad_protos)


def solution(mesh):
    in_specs = (P("batch", None, None), P("batch", None, None), P(None, "proto"), P("batch", None))
    out_specs = (P("batch", None, None), P("batch", "proto"))
    return jax.shard_map(
        on_device, mesh=mesh, in_specs=in_specs, out_specs=out_specs, check_vma=False
    )
```

```python
import jax
import jax.numpy as jnp
from jax import lax
from jax.experimental import pallas as pl
from jax.experimental.pallas import tpu as pltpu
from jax.sharding import PartitionSpec as P

ITERS = 3
TEACHER_TEMP = 0.04
STUDENT_TEMP = 0.1
EPSILON = 1e-06
LANES = 128
Z = 8
RING = 16
ROWS = 32
WIDE = 1024
MIB = 1024 * 1024
F32 = jnp.float32
BF16 = jnp.bfloat16

VMEM = pltpu.VMEM
Z_GROUPS = [[2 * z + c for z in range(Z)] for c in range(2)]
ROW_GROUPS = [[ROWS * z + i for i in range(ROWS)] for z in range(Z)]


def whole():
    return pl.BlockSpec(memory_space=VMEM)


def cost(flops, transcendentals=0, moved=0):
    return pl.CostEstimate(
        flops=flops, transcendentals=transcendentals, bytes_accessed=moved
    )


def params(vmem):
    return pltpu.CompilerParams(vmem_limit_bytes=vmem * MIB)


def call(kernel, outs, *args, scratch=(), vmem=16, cost_estimate=None):
    return pl.pallas_call(
        kernel,
        out_shape=outs,
        in_specs=[whole()] * len(args),
        out_specs=[whole()] * len(outs),
        scratch_shapes=list(scratch),
        compiler_params=params(vmem),
        cost_estimate=cost_estimate,
    )(*args)


def one_hot_t(mask_row, patches, dtype):
    slots = mask_row.shape[1]
    patch = lax.broadcasted_iota(jnp.int32, (patches, slots), 0)
    return jnp.where(patch == mask_row, 1.0, 0.0).astype(dtype)


def fetch(pairs, sems):
    copies = [pltpu.make_async_copy(src, dst, sems.at[i]) for i, (src, dst) in enumerate(pairs)]
    for copy in copies:
        copy.start()
    return copies


def masked_rows(feats, mask_row):
    hot = one_hot_t(mask_row, feats.shape[0], BF16)
    rows = lax.dot_general(hot, feats, (((0,), (0,)), ((), ())), preferred_element_type=F32)
    return rows, jnp.sqrt(jnp.sum(rows * rows, axis=1, keepdims=True) + EPSILON)


def prep_kernel(
    where_ref, teacher_hbm, student_hbm, mask_hbm, proto_hbm, zt_ref, zs_ref, proto_ref,
    teacher_ref, student_ref, mask_ref, sems,
):
    wide = proto_ref.shape[1]
    mine = pl.ds(pl.multiple_of(where_ref[0] * wide, wide), wide)
    mask_copy, teacher_copy, student_copy, proto_copy = fetch(
        (
            (mask_hbm, mask_ref), (teacher_hbm, teacher_ref), (student_hbm, student_ref),
            (proto_hbm.at[:, mine], proto_ref),
        ),
        sems,
    )
    mask_copy.wait()
    slots = mask_ref.shape[1]
    for copy, feats, out in (
        (teacher_copy, teacher_ref, zt_ref), (student_copy, student_ref, zs_ref)
    ):
        copy.wait()
        for i in range(feats.shape[0]):
            rows, norm = masked_rows(feats[i], mask_ref[i : i + 1, :])
            out[i * slots : (i + 1) * slots, :] = (rows / norm).astype(BF16).astype(F32)
    proto_copy.wait()


def proto_kernel(proto_ref, full_ref, unit_ref, back_ref, scale_ref):
    p = proto_ref[...].astype(F32)
    scale = 1.0 / jnp.sqrt(jnp.sum(p * p, axis=0, keepdims=True) + EPSILON)
    full = p * scale
    full_ref[...] = full
    unit_ref[...] = full.astype(BF16)
    back_ref[...] = full.T.astype(BF16)
    scale_ref[...] = scale


def core_rows(where_ref, side, half):
    return pl.ds(pl.multiple_of(lax.rem(where_ref[0] + side, 2) * half, half), half)


def write_lanes(out_ref, value, row, copies):
    for m in range(copies):
        out_ref[m, pl.ds(row, 1), :] = value


def write_rows(out_ref, acc_ref, first=0):
    pieces = []
    for i in range(acc_ref.shape[0] // LANES):
        tile = acc_ref[i * LANES : (i + 1) * LANES, :].T
        pieces.append(jnp.sum(tile, axis=0, keepdims=True))
    value = jnp.concatenate(pieces, axis=0)
    for m in range(out_ref.shape[0]):
        out_ref[m, first : first + 8, :] = value


def teacher_exp_kernel(where_ref, own_ref, other_ref, unit_ref, e_ref, col_ref):
    half = own_ref.shape[0]
    wide = unit_ref.shape[1]
    block = 256
    for w in range(wide // WIDE):
        columns = pl.ds(w * WIDE, WIDE)
        unit = unit_ref[:, columns]
        total = jnp.zeros((8, WIDE), F32)
        for side, ref in enumerate((own_ref, other_ref)):
            place = core_rows(where_ref, side, half)
            for b in range(half // block):
                z = ref[b * block : (b + 1) * block, :].astype(BF16)
                e = jnp.exp(
                    jnp.dot(z, unit, preferred_element_type=F32) * (1.0 / TEACHER_TEMP)
                )
                e_ref[pl.ds(place.start + b * block, block), columns] = e
                for g in range(block // 8):
                    total += e[g * 8 : (g + 1) * 8, :]
        total = jnp.sum(total, axis=0, keepdims=True)
        for i in range(WIDE // LANES):
            write_lanes(
                col_ref, total[:, i * LANES : (i + 1) * LANES], w * (WIDE // LANES) + i, Z
            )


def student_exp_kernel(
    where_ref, own_ref, other_ref, unit_ref, s_ref, mass_ref, turned_ref
):
    half = own_ref.shape[0]
    wide = unit_ref.shape[1]
    block = 256
    for side, ref in enumerate((own_ref, other_ref)):
        turned_ref[:, core_rows(where_ref, side, half)] = ref[...].T.astype(BF16)
    for w in range(wide // WIDE):
        columns = pl.ds(w * WIDE, WIDE)
        unit = unit_ref[:, columns]
        for side, ref in enumerate((own_ref, other_ref)):
            place = core_rows(where_ref, side, half)
            for b in range(half // block):
                rows = pl.ds(place.start + b * block, block)
                z = ref[b * block : (b + 1) * block, :].astype(BF16)
                s = jnp.exp(
                    jnp.dot(z, unit, preferred_element_type=F32) * (1.0 / STUDENT_TEMP)
                )
                s_ref[rows, columns] = s
                part = sum(s[:, j * LANES : (j + 1) * LANES] for j in range(WIDE // LANES))
                if w:
                    mass_ref[rows, :] += part
                else:
                    mass_ref[rows, :] = part


def row_kernel(e_ref, parts_ref, out_ref, c_ref, acc_ref):
    c = 1.0 / jnp.sum(parts_ref[...], axis=0)
    c_ref[...] = c
    tiles = c.shape[0]
    block = 128

    def body(b, carry):
        rows = pl.ds(pl.multiple_of(b * block, block), block)
        acc = jnp.zeros((block, LANES), F32)
        for j in range(tiles):
            acc += e_ref[rows, j * LANES : (j + 1) * LANES] * c[j : j + 1, :]
        acc_ref[rows, :] = acc
        return carry

    lax.fori_loop(0, e_ref.shape[0] // block, body, 0)
    write_rows(out_ref, acc_ref)


def row_mass_kernel(e_ref, parts_ref, mass_ref, out_ref, c_ref, acc_ref):
    row_kernel(e_ref, parts_ref, out_ref, c_ref, acc_ref)
    write_rows(out_ref, mass_ref, first=8)


def spread(ref, value):
    for i in range(value.shape[0]):
        ref[i * LANES : (i + 1) * LANES, :] = jnp.broadcast_to(
            value[i : i + 1, :], (LANES, LANES)
        ).T


def col_kernel(e_ref, parts_ref, out_ref, r_ref):
    spread(r_ref, 1.0 / jnp.sum(parts_ref[:, :8, :], axis=0))
    tiles = e_ref.shape[1] // LANES
    block = 32

    def body(b, acc):
        rows = pl.ds(pl.multiple_of(b * block, block), block)
        r = r_ref[rows, :]
        out = []
        for j in range(tiles):
            value = acc[j]
            tile = e_ref[rows, j * LANES : (j + 1) * LANES] * r
            for g in range(block // 8):
                value = value + tile[g * 8 : (g + 1) * 8, :]
            out.append(value)
        return tuple(out)

    zero = tuple(jnp.zeros((8, LANES), F32) for _ in range(tiles))
    acc = lax.fori_loop(0, e_ref.shape[0] // block, body, zero, unroll=2)
    value = jnp.concatenate([jnp.sum(a, axis=0, keepdims=True) for a in acc], axis=0)
    for m in range(Z):
        out_ref[m] = value


def diff_kernel(
    e_ref, s_ref, c_ref, parts_ref, mass_ref, diff_ref, r_ref, m_ref
):
    scale = 1.0 / STUDENT_TEMP
    spread(r_ref, scale / jnp.sum(parts_ref[...], axis=0))
    spread(m_ref, scale / jnp.sum(mass_ref[:, 8:, :], axis=0))
    tiles = e_ref.shape[1] // LANES
    block = 64

    def body(b, carry):
        rows = pl.ds(pl.multiple_of(b * block, block), block)
        r = r_ref[rows, :]
        m = m_ref[rows, :]
        for j in range(tiles):
            lanes = slice(j * LANES, (j + 1) * LANES)
            targets = (r * e_ref[rows, lanes]) * c_ref[j : j + 1, :]
            probs = s_ref[rows, lanes] * m
            diff_ref[rows, lanes] = (probs - targets).astype(BF16)
        return carry

    lax.fori_loop(0, e_ref.shape[0] // block, body, 0)


def token_kernel(where_ref, diff_ref, back_ref, own_ref, give_ref):
    for side, out in enumerate((own_ref, give_ref)):
        rows = core_rows(where_ref, side, out.shape[0])
        out[...] = jnp.dot(diff_ref[rows, :], back_ref[...], preferred_element_type=F32)


def grad_kernel(where_ref, diff_ref, full_ref, scale_ref, turned_ref, *refs):
    outs, (g_ref, sems) = refs[:-2], refs[-2:]
    wide = full_ref.shape[1]
    core, z = where_ref[0], where_ref[1]
    deep = g_ref.shape[0] // Z
    near = deep // 2
    copies = []
    for w in range(wide // WIDE):
        columns = slice(w * WIDE, (w + 1) * WIDE)
        grad = jnp.dot(turned_ref[...], diff_ref[:, columns], preferred_element_type=F32)
        full = full_ref[:, columns]
        proj = jnp.sum(full.astype(BF16).astype(F32) * grad, axis=0, keepdims=True)
        g_ref[:, columns] = (grad - full * proj) * scale_ref[:, columns]
        pairs = []
        for j in range(Z):
            top = lax.rem(z + j, Z) * deep
            for side in range(2):
                take = pl.multiple_of(top + lax.rem(core + side, 2) * near, near)
                if j == 4:
                    out = outs[4 + side].at[:, columns]
                else:
                    out = outs[j + (j > 4)].at[pl.ds(side * near, near), columns]
                pairs.append((g_ref.at[pl.ds(take, near), columns], out))
        copies += fetch(pairs, sems.at[w])
    for copy in copies:
        copy.wait()


def share_kernel(parts_ref, out_ref):
    total = sum(parts_ref[i] for i in range(parts_ref.shape[0]))
    for m in range(out_ref.shape[0]):
        out_ref[m] = total


def last_kernel(
    where_ref, keep_ref, got_ref, gz_ref, feats_ref, mask_ref, student_hbm, protos_hbm,
    out_ref, sems, place_sems,
):
    core, wide = where_ref[0], keep_ref.shape[1]
    copies = fetch(
        [
            (ref, protos_hbm.at[:, pl.ds(pl.multiple_of(lax.rem(core + side, 2) * wide, wide), wide)])
            for side, ref in enumerate((keep_ref, got_ref))
        ],
        place_sems,
    )
    slots = mask_ref.shape[1]
    for i in range(out_ref.shape[0]):
        mask = mask_ref[i : i + 1, :]
        xs, norm = masked_rows(feats_ref[i], mask)
        zsf = xs / norm
        gz = gz_ref[i * slots : (i + 1) * slots, :]
        proj = jnp.sum(zsf * gz, axis=1, keepdims=True)
        grad = (gz - zsf * proj) / norm
        hot = one_hot_t(mask, out_ref.shape[1], BF16)
        high = grad.astype(BF16)
        low = (grad - high.astype(F32)).astype(BF16)
        out_ref[i] = jnp.dot(hot, high, preferred_element_type=F32) + jnp.dot(
            hot, low, preferred_element_type=F32
        )
        copies += fetch(((out_ref.at[i], student_hbm.at[i]),), sems.at[pl.ds(i, 1)])
    for copy in copies:
        copy.wait()


def sum_kernel(a_ref, b_ref, out_ref):
    out_ref[...] = a_ref[...] + b_ref[...]


def first_step_kernel(low):
    def kernel(rel_hbm, got_ref, out_ref, sem):
        for copy in fetch(((rel_hbm, out_ref),), sem):
            copy.wait()
        near = got_ref.shape[0]
        rows = slice(near, 2 * near) if low else slice(0, near)
        out_ref[rows, :] += got_ref[...]

    return kernel


def step_kernel(rel_hbm, got_ref, out_ref, sem):
    for copy in fetch(((rel_hbm, out_ref),), sem):
        copy.wait()
    out_ref[...] += got_ref[...]


def last_sum_kernel(rel_hbm, up_ref, down_ref, keep_ref, give_ref, rel, sem):
    for copy in fetch(((rel_hbm, rel),), sem):
        copy.wait()
    near = keep_ref.shape[0]
    total = rel[...] + (up_ref[...] + down_ref[...])
    keep_ref[...] = total[:near, :]
    give_ref[...] = total[near:, :]


def shape(*dims, dtype=F32):
    return jax.ShapeDtypeStruct(dims, dtype)


def hold(*dims, dtype=F32):
    return pltpu.VMEM(dims, dtype)


def far(*dims):
    return pltpu.HBM(dims, F32)


def in_hbm(x):
    return pltpu.with_memory_space_constraint(x, pltpu.HBM)


def other_core(x):
    return lax.ppermute(x, "batch", [(i, i ^ 1) for i in range(RING)])


def along_z(x, d):
    return lax.ppermute(
        x, "batch", [(i, ((i // 2 + d) % Z) * 2 + i % 2) for i in range(RING)]
    )


def all_columns(x):
    return lax.all_to_all(x, "batch", 0, 0, axis_index_groups=Z_GROUPS)


def all_rows(x):
    return lax.all_to_all(x, ("batch", "proto"), 0, 0, axis_index_groups=ROW_GROUPS)


def tie(x, y):
    return lax.optimization_barrier((x, y))[0]


def on_device(teacher_feats, student_feats, prototypes, mask_index):
    images, patches, width = teacher_feats.shape
    slots = mask_index.shape[1]
    own = images * slots
    tokens = 2 * own
    wide = prototypes.shape[1] // 2
    lane_tiles = wide // LANES
    row_tiles = tokens // LANES
    place = lax.axis_index("batch")
    where = jnp.stack([lax.rem(place, 2), lax.div(place, 2)]).astype(jnp.int32)
    scalars = pl.BlockSpec(memory_space=pltpu.SMEM)

    def placed(kernel, outs, *args, **kw):
        return pl.pallas_call(
            kernel,
            in_specs=[scalars] + [whole()] * len(args),
            out_specs=[whole()] * len(outs),
            out_shape=outs,
            scratch_shapes=kw.get("scratch", []),
            compiler_params=params(16),
            cost_estimate=kw.get("cost_estimate"),
        )(where, *args)

    zt, zs, protos = pl.pallas_call(
        prep_kernel,
        in_specs=[scalars] + [pl.BlockSpec(memory_space=pl.ANY)] * 4,
        out_specs=[whole()] * 3,
        out_shape=[shape(own, width), shape(own, width), hold(width, wide, dtype=BF16)],
        scratch_shapes=[
            VMEM(teacher_feats.shape, BF16), VMEM(student_feats.shape, BF16),
            VMEM(mask_index.shape, jnp.int32), pltpu.SemaphoreType.DMA((4,)),
        ],
        compiler_params=params(16),
    )(where, in_hbm(teacher_feats), in_hbm(student_feats), in_hbm(mask_index), in_hbm(prototypes))
    zt_other = other_core(zt)
    zs_other = other_core(zs)
    full, unit, back, p_scale = call(
        proto_kernel,
        [
            hold(width, wide), hold(width, wide, dtype=BF16), hold(wide, width, dtype=BF16),
            shape(1, wide),
        ],
        protos,
    )

    exp_cost = cost(2 * tokens * wide * width, tokens * wide)
    e, col_out = placed(
        teacher_exp_kernel,
        [hold(tokens, wide), shape(Z, lane_tiles, LANES)],
        zt, zt_other, unit, cost_estimate=exp_cost,
    )
    s, mass_acc, turned = placed(
        student_exp_kernel,
        [hold(tokens, wide), shape(tokens, LANES), shape(width, tokens, dtype=BF16)],
        zs, zs_other, unit, cost_estimate=exp_cost,
    )
    col_out = tie(col_out, mass_acc)

    mass = None
    for sweep in range(ITERS):
        col_parts = all_columns(col_out)
        extra = [mass_acc] if sweep == 0 else []
        row_out, c = call(
            row_kernel if sweep else row_mass_kernel,
            [shape(ROWS, row_tiles * (1 + len(extra)), LANES), shape(lane_tiles, LANES)],
            e, col_parts, *extra,
            scratch=[VMEM((tokens, LANES), F32)],
        )
        row_parts = all_rows(row_out)
        if sweep == 0:
            mass = row_parts
        if sweep < ITERS - 1:
            (col_out,) = call(
                col_kernel, [shape(Z, lane_tiles, LANES)], e, row_parts,
                scratch=[VMEM((tokens, LANES), F32)],
            )

    (diff,) = call(
        diff_kernel, [shape(tokens, wide, dtype=BF16)], e, s, c, row_parts, mass,
        scratch=[VMEM((tokens, LANES), F32), VMEM((tokens, LANES), F32)],
    )
    gz, gz_give = placed(
        token_kernel, [hold(own, width), shape(own, width)], diff, back,
        cost_estimate=cost(2 * tokens * wide * width),
    )
    gz_got = other_core(gz_give)
    deep = width // Z
    near = deep // 2
    anywhere = pl.BlockSpec(memory_space=pltpu.HBM)
    rel = pl.pallas_call(
        grad_kernel,
        in_specs=[scalars] + [whole()] * 4,
        out_specs=[anywhere] * 9,
        out_shape=[far(deep, wide)] * 4 + [far(near, wide)] * 2 + [far(deep, wide)] * 3,
        scratch_shapes=[VMEM((width, wide), F32), pltpu.SemaphoreType.DMA((wide // WIDE, 2 * Z))],
        compiler_params=params(16),
        cost_estimate=cost(2 * tokens * wide * width),
    )(where, tie(diff, (gz, gz_give)), full, p_scale, turned)

    def step(kernel, term, got, work=0):
        return pl.pallas_call(
            kernel,
            in_specs=[anywhere, whole()],
            out_specs=whole(),
            out_shape=shape(deep, wide),
            scratch_shapes=[pltpu.SemaphoreType.DMA((1,))],
            compiler_params=params(16),
            cost_estimate=cost(work) if work else None,
        )(term, got)

    up, down = along_z(rel[4], 1), along_z(rel[5], -1)
    up = step(first_step_kernel(False), rel[3], up, 2 * 10**9)
    down = step(first_step_kernel(True), rel[6], down, 2 * 10**9)
    (gz,) = call(sum_kernel, [shape(own, width)], gz, gz_got)
    gz_parts = lax.all_to_all(
        tie(gz, rel).reshape(RING, own // RING, width), "proto", 0, 0
    )
    (gz_share,) = call(share_kernel, [shape(RING, own // RING, width)], gz_parts)
    up, down = along_z(up, 1), along_z(down, -1)
    up = step(step_kernel, rel[2], up)
    down = step(step_kernel, rel[7], down)
    gz = lax.all_to_all(gz_share, "proto", 0, 0).reshape(own, width)
    up, down = along_z(up, 1), along_z(down, -1)
    up, down = tie((up, down), gz_share)
    up = step(step_kernel, rel[1], up)
    down = step(step_kernel, rel[8], down)
    up, down = along_z(up, 1), along_z(down, -1)
    up = tie(up, gz)
    keep, give = pl.pallas_call(
        last_sum_kernel,
        in_specs=[anywhere, whole(), whole()],
        out_specs=[whole()] * 2,
        out_shape=[shape(near, wide)] * 2,
        scratch_shapes=[VMEM((deep, wide), F32), pltpu.SemaphoreType.DMA((1,))],
        compiler_params=params(16),
    )(rel[0], up, down)
    got = other_core(give)
    grad_student, grad_protos = pl.pallas_call(
        last_kernel,
        in_specs=[scalars] + [whole()] * 5,
        out_specs=[pl.BlockSpec(memory_space=pl.ANY)] * 2,
        out_shape=[shape(images, patches, width), shape(near, 2 * wide)],
        scratch_shapes=[
            VMEM((images, patches, width), F32), pltpu.SemaphoreType.DMA((images,)),
            pltpu.SemaphoreType.DMA((2,)),
        ],
        compiler_params=params(16),
    )(where, keep, got, gz, student_feats, mask_index)
    return (grad_student, grad_protos)


def solution(mesh):
    in_specs = (P("batch", None, None), P("batch", None, None), P(None, "proto"), P("batch", None))
    out_specs = (P("batch", None, None), P("batch", "proto"))
    return jax.shard_map(
        on_device, mesh=mesh, in_specs=in_specs, out_specs=out_specs, check_vma=False
    )
```

```python
import jax
import jax.numpy as jnp
from jax import lax
from jax.experimental import pallas as pl
from jax.experimental.pallas import tpu as pltpu
from jax.sharding import PartitionSpec as P

ITERS = 3
TEACHER_TEMP = 0.04
STUDENT_TEMP = 0.1
EPSILON = 1e-06
LANES = 128
Z = 8
RING = 16
ROWS = 32
WIDE = 1024
MIB = 1024 * 1024
F32 = jnp.float32
BF16 = jnp.bfloat16

VMEM = pltpu.VMEM
Z_GROUPS = [[2 * z + c for z in range(Z)] for c in range(2)]
ROW_GROUPS = [[ROWS * z + i for i in range(ROWS)] for z in range(Z)]


def whole():
    return pl.BlockSpec(memory_space=VMEM)


def cost(flops, transcendentals=0, moved=0):
    return pl.CostEstimate(
        flops=flops, transcendentals=transcendentals, bytes_accessed=moved
    )


def params(vmem):
    return pltpu.CompilerParams(vmem_limit_bytes=vmem * MIB)


def call(kernel, outs, *args, scratch=(), vmem=16, cost_estimate=None):
    return pl.pallas_call(
        kernel,
        out_shape=outs,
        in_specs=[whole()] * len(args),
        out_specs=[whole()] * len(outs),
        scratch_shapes=list(scratch),
        compiler_params=params(vmem),
        cost_estimate=cost_estimate,
    )(*args)


def one_hot_t(mask_row, patches, dtype):
    slots = mask_row.shape[1]
    patch = lax.broadcasted_iota(jnp.int32, (patches, slots), 0)
    return jnp.where(patch == mask_row, 1.0, 0.0).astype(dtype)


def fetch(pairs, sems):
    copies = [pltpu.make_async_copy(src, dst, sems.at[i]) for i, (src, dst) in enumerate(pairs)]
    for copy in copies:
        copy.start()
    return copies


def masked_rows(feats, mask_row):
    hot = one_hot_t(mask_row, feats.shape[0], BF16)
    rows = lax.dot_general(hot, feats, (((0,), (0,)), ((), ())), preferred_element_type=F32)
    return rows, jnp.sqrt(jnp.sum(rows * rows, axis=1, keepdims=True) + EPSILON)


def prep_kernel(
    where_ref, teacher_hbm, student_hbm, mask_hbm, proto_hbm, zt_ref, zs_ref, proto_ref,
    teacher_ref, student_ref, mask_ref, sems,
):
    wide = proto_ref.shape[1]
    mine = pl.ds(pl.multiple_of(where_ref[0] * wide, wide), wide)
    mask_copy, teacher_copy, student_copy, proto_copy = fetch(
        (
            (mask_hbm, mask_ref), (teacher_hbm, teacher_ref), (student_hbm, student_ref),
            (proto_hbm.at[:, mine], proto_ref),
        ),
        sems,
    )
    mask_copy.wait()
    slots = mask_ref.shape[1]
    for copy, feats, out in (
        (teacher_copy, teacher_ref, zt_ref), (student_copy, student_ref, zs_ref)
    ):
        copy.wait()
        for i in range(feats.shape[0]):
            rows, norm = masked_rows(feats[i], mask_ref[i : i + 1, :])
            out[i * slots : (i + 1) * slots, :] = (rows / norm).astype(BF16).astype(F32)
    proto_copy.wait()


def proto_kernel(proto_ref, full_ref, unit_ref, back_ref, scale_ref):
    p = proto_ref[...].astype(F32)
    scale = 1.0 / jnp.sqrt(jnp.sum(p * p, axis=0, keepdims=True) + EPSILON)
    full = p * scale
    full_ref[...] = full
    unit_ref[...] = full.astype(BF16)
    back_ref[...] = full.T.astype(BF16)
    scale_ref[...] = scale


def core_rows(where_ref, side, half):
    return pl.ds(pl.multiple_of(lax.rem(where_ref[0] + side, 2) * half, half), half)


def write_lanes(out_ref, value, row, copies):
    for m in range(copies):
        out_ref[m, pl.ds(row, 1), :] = value


def write_rows(out_ref, acc_ref, first=0):
    pieces = []
    for i in range(acc_ref.shape[0] // LANES):
        tile = acc_ref[i * LANES : (i + 1) * LANES, :].T
        pieces.append(jnp.sum(tile, axis=0, keepdims=True))
    value = jnp.concatenate(pieces, axis=0)
    for m in range(out_ref.shape[0]):
        out_ref[m, first : first + 8, :] = value


def teacher_exp_kernel(where_ref, own_ref, other_ref, unit_ref, e_ref, col_ref):
    half = own_ref.shape[0]
    wide = unit_ref.shape[1]
    block = 256
    for w in range(wide // WIDE):
        columns = pl.ds(w * WIDE, WIDE)
        unit = unit_ref[:, columns]
        total = jnp.zeros((8, WIDE), F32)
        for side, ref in enumerate((own_ref, other_ref)):
            place = core_rows(where_ref, side, half)
            for b in range(half // block):
                z = ref[b * block : (b + 1) * block, :].astype(BF16)
                e = jnp.exp(
                    jnp.dot(z, unit, preferred_element_type=F32) * (1.0 / TEACHER_TEMP)
                )
                e_ref[pl.ds(place.start + b * block, block), columns] = e
                for g in range(block // 8):
                    total += e[g * 8 : (g + 1) * 8, :]
        total = jnp.sum(total, axis=0, keepdims=True)
        for i in range(WIDE // LANES):
            write_lanes(
                col_ref, total[:, i * LANES : (i + 1) * LANES], w * (WIDE // LANES) + i, Z
            )


def student_exp_kernel(
    where_ref, own_ref, other_ref, unit_ref, s_ref, mass_ref, turned_ref
):
    half = own_ref.shape[0]
    wide = unit_ref.shape[1]
    block = 256
    for side, ref in enumerate((own_ref, other_ref)):
        turned_ref[:, core_rows(where_ref, side, half)] = ref[...].T.astype(BF16)
    for w in range(wide // WIDE):
        columns = pl.ds(w * WIDE, WIDE)
        unit = unit_ref[:, columns]
        for side, ref in enumerate((own_ref, other_ref)):
            place = core_rows(where_ref, side, half)
            for b in range(half // block):
                rows = pl.ds(place.start + b * block, block)
                z = ref[b * block : (b + 1) * block, :].astype(BF16)
                s = jnp.exp(
                    jnp.dot(z, unit, preferred_element_type=F32) * (1.0 / STUDENT_TEMP)
                )
                s_ref[rows, columns] = s
                part = sum(s[:, j * LANES : (j + 1) * LANES] for j in range(WIDE // LANES))
                if w:
                    mass_ref[rows, :] += part
                else:
                    mass_ref[rows, :] = part


def row_kernel(e_ref, parts_ref, out_ref, c_ref, acc_ref):
    c = 1.0 / jnp.sum(parts_ref[...], axis=0)
    c_ref[...] = c
    tiles = c.shape[0]
    block = 128

    def body(b, carry):
        rows = pl.ds(pl.multiple_of(b * block, block), block)
        acc = jnp.zeros((block, LANES), F32)
        for j in range(tiles):
            acc += e_ref[rows, j * LANES : (j + 1) * LANES] * c[j : j + 1, :]
        acc_ref[rows, :] = acc
        return carry

    lax.fori_loop(0, e_ref.shape[0] // block, body, 0)
    write_rows(out_ref, acc_ref)


def row_mass_kernel(e_ref, parts_ref, mass_ref, out_ref, c_ref, acc_ref):
    row_kernel(e_ref, parts_ref, out_ref, c_ref, acc_ref)
    write_rows(out_ref, mass_ref, first=8)


def spread(ref, value):
    for i in range(value.shape[0]):
        ref[i * LANES : (i + 1) * LANES, :] = jnp.broadcast_to(
            value[i : i + 1, :], (LANES, LANES)
        ).T


def col_kernel(e_ref, parts_ref, out_ref, r_ref):
    spread(r_ref, 1.0 / jnp.sum(parts_ref[:, :8, :], axis=0))
    tiles = e_ref.shape[1] // LANES
    block = 32

    def body(b, acc):
        rows = pl.ds(pl.multiple_of(b * block, block), block)
        r = r_ref[rows, :]
        out = []
        for j in range(tiles):
            value = acc[j]
            tile = e_ref[rows, j * LANES : (j + 1) * LANES] * r
            for g in range(block // 8):
                value = value + tile[g * 8 : (g + 1) * 8, :]
            out.append(value)
        return tuple(out)

    zero = tuple(jnp.zeros((8, LANES), F32) for _ in range(tiles))
    acc = lax.fori_loop(0, e_ref.shape[0] // block, body, zero, unroll=2)
    value = jnp.concatenate([jnp.sum(a, axis=0, keepdims=True) for a in acc], axis=0)
    for m in range(Z):
        out_ref[m] = value


def diff_kernel(
    e_ref, s_ref, c_ref, parts_ref, mass_ref, diff_ref, r_ref, m_ref
):
    scale = 1.0 / STUDENT_TEMP
    spread(r_ref, scale / jnp.sum(parts_ref[...], axis=0))
    spread(m_ref, scale / jnp.sum(mass_ref[:, 8:, :], axis=0))
    tiles = e_ref.shape[1] // LANES
    block = 64

    def body(b, carry):
        rows = pl.ds(pl.multiple_of(b * block, block), block)
        r = r_ref[rows, :]
        m = m_ref[rows, :]
        for j in range(tiles):
            lanes = slice(j * LANES, (j + 1) * LANES)
            targets = (r * e_ref[rows, lanes]) * c_ref[j : j + 1, :]
            probs = s_ref[rows, lanes] * m
            diff_ref[rows, lanes] = (probs - targets).astype(BF16)
        return carry

    lax.fori_loop(0, e_ref.shape[0] // block, body, 0)


def token_kernel(where_ref, diff_ref, back_ref, own_ref, give_ref):
    for side, out in enumerate((own_ref, give_ref)):
        rows = core_rows(where_ref, side, out.shape[0])
        out[...] = jnp.dot(diff_ref[rows, :], back_ref[...], preferred_element_type=F32)


def grad_kernel(where_ref, diff_ref, full_ref, scale_ref, turned_ref, *refs):
    outs, (g_ref, sems) = refs[:-2], refs[-2:]
    wide = full_ref.shape[1]
    core, z = where_ref[0], where_ref[1]
    deep = g_ref.shape[0] // Z
    near = deep // 2
    copies = []
    for w in range(wide // WIDE):
        columns = slice(w * WIDE, (w + 1) * WIDE)
        grad = jnp.dot(turned_ref[...], diff_ref[:, columns], preferred_element_type=F32)
        full = full_ref[:, columns]
        proj = jnp.sum(full.astype(BF16).astype(F32) * grad, axis=0, keepdims=True)
        g_ref[:, columns] = (grad - full * proj) * scale_ref[:, columns]
        pairs = []
        for j in range(Z):
            top = lax.rem(z + j, Z) * deep
            for side in range(2):
                take = pl.multiple_of(top + lax.rem(core + side, 2) * near, near)
                if j == 4:
                    out = outs[4 + side].at[:, columns]
                else:
                    out = outs[j + (j > 4)].at[pl.ds(side * near, near), columns]
                pairs.append((g_ref.at[pl.ds(take, near), columns], out))
        copies += fetch(pairs, sems.at[w])
    for copy in copies:
        copy.wait()


def share_kernel(parts_ref, out_ref):
    total = sum(parts_ref[i] for i in range(parts_ref.shape[0]))
    for m in range(out_ref.shape[0]):
        out_ref[m] = total


def again_kernel(feats_ref, mask_ref, full_ref, norm_ref, hot_ref):
    slots = mask_ref.shape[1]
    for i in range(feats_ref.shape[0]):
        rows = slice(i * slots, (i + 1) * slots)
        mask = mask_ref[i : i + 1, :]
        xs, norm = masked_rows(feats_ref[i], mask)
        full_ref[rows, :] = xs / norm
        norm_ref[rows, :] = norm
        hot_ref[i] = one_hot_t(mask, feats_ref.shape[1], BF16)


def last_kernel(
    where_ref, keep_ref, got_ref, gz_ref, full_ref, norm_ref, hot_ref, student_hbm, protos_hbm,
    out_ref, sems, place_sems,
):
    core, wide = where_ref[0], keep_ref.shape[1]
    copies = fetch(
        [
            (ref, protos_hbm.at[:, pl.ds(pl.multiple_of(lax.rem(core + side, 2) * wide, wide), wide)])
            for side, ref in enumerate((keep_ref, got_ref))
        ],
        place_sems,
    )
    slots = hot_ref.shape[2]
    for i in range(out_ref.shape[0]):
        rows = slice(i * slots, (i + 1) * slots)
        zsf = full_ref[rows, :]
        gz = gz_ref[rows, :]
        proj = jnp.sum(zsf * gz, axis=1, keepdims=True)
        grad = (gz - zsf * proj) / norm_ref[rows, :]
        hot = hot_ref[i]
        high = grad.astype(BF16)
        low = (grad - high.astype(F32)).astype(BF16)
        out_ref[i] = jnp.dot(hot, high, preferred_element_type=F32) + jnp.dot(
            hot, low, preferred_element_type=F32
        )
        copies += fetch(((out_ref.at[i], student_hbm.at[i]),), sems.at[pl.ds(i, 1)])
    for copy in copies:
        copy.wait()


def sum_kernel(a_ref, b_ref, out_ref):
    out_ref[...] = a_ref[...] + b_ref[...]


def first_step_kernel(low):
    def kernel(rel_hbm, got_ref, out_ref, sem):
        for copy in fetch(((rel_hbm, out_ref),), sem):
            copy.wait()
        near = got_ref.shape[0]
        rows = slice(near, 2 * near) if low else slice(0, near)
        out_ref[rows, :] += got_ref[...]

    return kernel


def step_kernel(rel_hbm, got_ref, out_ref, sem):
    for copy in fetch(((rel_hbm, out_ref),), sem):
        copy.wait()
    out_ref[...] += got_ref[...]


def last_sum_kernel(rel_hbm, up_ref, down_ref, keep_ref, give_ref, rel, sem):
    for copy in fetch(((rel_hbm, rel),), sem):
        copy.wait()
    near = keep_ref.shape[0]
    total = rel[...] + (up_ref[...] + down_ref[...])
    keep_ref[...] = total[:near, :]
    give_ref[...] = total[near:, :]


def shape(*dims, dtype=F32):
    return jax.ShapeDtypeStruct(dims, dtype)


def hold(*dims, dtype=F32):
    return pltpu.VMEM(dims, dtype)


def far(*dims):
    return pltpu.HBM(dims, F32)


def in_hbm(x):
    return pltpu.with_memory_space_constraint(x, pltpu.HBM)


def other_core(x):
    return lax.ppermute(x, "batch", [(i, i ^ 1) for i in range(RING)])


def along_z(x, d):
    return lax.ppermute(
        x, "batch", [(i, ((i // 2 + d) % Z) * 2 + i % 2) for i in range(RING)]
    )


def all_columns(x):
    return lax.all_to_all(x, "batch", 0, 0, axis_index_groups=Z_GROUPS)


def all_rows(x):
    return lax.all_to_all(x, ("batch", "proto"), 0, 0, axis_index_groups=ROW_GROUPS)


def tie(x, y):
    return lax.optimization_barrier((x, y))[0]


def on_device(teacher_feats, student_feats, prototypes, mask_index):
    images, patches, width = teacher_feats.shape
    slots = mask_index.shape[1]
    own = images * slots
    tokens = 2 * own
    wide = prototypes.shape[1] // 2
    lane_tiles = wide // LANES
    row_tiles = tokens // LANES
    place = lax.axis_index("batch")
    where = jnp.stack([lax.rem(place, 2), lax.div(place, 2)]).astype(jnp.int32)
    scalars = pl.BlockSpec(memory_space=pltpu.SMEM)

    def placed(kernel, outs, *args, **kw):
        return pl.pallas_call(
            kernel,
            in_specs=[scalars] + [whole()] * len(args),
            out_specs=[whole()] * len(outs),
            out_shape=outs,
            scratch_shapes=kw.get("scratch", []),
            compiler_params=params(16),
            cost_estimate=kw.get("cost_estimate"),
        )(where, *args)

    zt, zs, protos = pl.pallas_call(
        prep_kernel,
        in_specs=[scalars] + [pl.BlockSpec(memory_space=pl.ANY)] * 4,
        out_specs=[whole()] * 3,
        out_shape=[shape(own, width), shape(own, width), hold(width, wide, dtype=BF16)],
        scratch_shapes=[
            VMEM(teacher_feats.shape, BF16), VMEM(student_feats.shape, BF16),
            VMEM(mask_index.shape, jnp.int32), pltpu.SemaphoreType.DMA((4,)),
        ],
        compiler_params=params(16),
    )(where, in_hbm(teacher_feats), in_hbm(student_feats), in_hbm(mask_index), in_hbm(prototypes))
    zt_other = other_core(zt)
    zs_other = other_core(zs)
    full, unit, back, p_scale = call(
        proto_kernel,
        [
            hold(width, wide), hold(width, wide, dtype=BF16), hold(wide, width, dtype=BF16),
            shape(1, wide),
        ],
        protos,
    )

    exp_cost = cost(2 * tokens * wide * width, tokens * wide)
    e, col_out = placed(
        teacher_exp_kernel,
        [hold(tokens, wide), shape(Z, lane_tiles, LANES)],
        zt, zt_other, unit, cost_estimate=exp_cost,
    )
    s, mass_acc, turned = placed(
        student_exp_kernel,
        [hold(tokens, wide), shape(tokens, LANES), shape(width, tokens, dtype=BF16)],
        zs, zs_other, unit, cost_estimate=exp_cost,
    )
    col_out = tie(col_out, mass_acc)

    mass = None
    for sweep in range(ITERS):
        col_parts = all_columns(col_out)
        extra = [mass_acc] if sweep == 0 else []
        row_out, c = call(
            row_kernel if sweep else row_mass_kernel,
            [shape(ROWS, row_tiles * (1 + len(extra)), LANES), shape(lane_tiles, LANES)],
            e, col_parts, *extra,
            scratch=[VMEM((tokens, LANES), F32)],
        )
        row_parts = all_rows(row_out)
        if sweep == 0:
            mass = row_parts
        if sweep < ITERS - 1:
            (col_out,) = call(
                col_kernel, [shape(Z, lane_tiles, LANES)], e, row_parts,
                scratch=[VMEM((tokens, LANES), F32)],
            )

    (diff,) = call(
        diff_kernel, [shape(tokens, wide, dtype=BF16)], e, s, c, row_parts, mass,
        scratch=[VMEM((tokens, LANES), F32), VMEM((tokens, LANES), F32)],
    )
    gz, gz_give = placed(
        token_kernel, [hold(own, width), shape(own, width)], diff, back,
        cost_estimate=cost(2 * tokens * wide * width),
    )
    gz_got = other_core(gz_give)
    deep = width // Z
    near = deep // 2
    anywhere = pl.BlockSpec(memory_space=pltpu.HBM)
    rel = pl.pallas_call(
        grad_kernel,
        in_specs=[scalars] + [whole()] * 4,
        out_specs=[anywhere] * 9,
        out_shape=[far(deep, wide)] * 4 + [far(near, wide)] * 2 + [far(deep, wide)] * 3,
        scratch_shapes=[VMEM((width, wide), F32), pltpu.SemaphoreType.DMA((wide // WIDE, 2 * Z))],
        compiler_params=params(16),
        cost_estimate=cost(2 * tokens * wide * width),
    )(where, tie(diff, (gz, gz_give)), full, p_scale, turned)

    def step(kernel, term, got, work=0):
        return pl.pallas_call(
            kernel,
            in_specs=[anywhere, whole()],
            out_specs=whole(),
            out_shape=shape(deep, wide),
            scratch_shapes=[pltpu.SemaphoreType.DMA((1,))],
            compiler_params=params(16),
            cost_estimate=cost(work) if work else None,
        )(term, got)

    up, down = along_z(rel[4], 1), along_z(rel[5], -1)
    up = step(first_step_kernel(False), rel[3], up, 2 * 10**9)
    down = step(first_step_kernel(True), rel[6], down, 2 * 10**9)
    (gz,) = call(sum_kernel, [shape(own, width)], gz, gz_got)
    gz_parts = lax.all_to_all(
        tie(gz, rel).reshape(RING, own // RING, width), "proto", 0, 0
    )
    (gz_share,) = call(share_kernel, [shape(RING, own // RING, width)], gz_parts)
    up, down = along_z(up, 1), along_z(down, -1)
    up = step(step_kernel, rel[2], up)
    down = step(step_kernel, rel[7], down)
    gz = lax.all_to_all(gz_share, "proto", 0, 0).reshape(own, width)
    up, down = along_z(up, 1), along_z(down, -1)
    up, down = tie((up, down), gz_share)
    up = step(step_kernel, rel[1], up)
    down = step(step_kernel, rel[8], down)
    up, down = along_z(up, 1), along_z(down, -1)
    up = tie(up, gz)
    keep, give = pl.pallas_call(
        last_sum_kernel,
        in_specs=[anywhere, whole(), whole()],
        out_specs=[whole()] * 2,
        out_shape=[shape(near, wide)] * 2,
        scratch_shapes=[VMEM((deep, wide), F32), pltpu.SemaphoreType.DMA((1,))],
        compiler_params=params(16),
    )(rel[0], up, down)
    got = other_core(give)
    again = call(
        again_kernel,
        [shape(own, width), shape(own, 1), shape(images, patches, slots, dtype=BF16)],
        student_feats, tie(mask_index, give),
    )
    grad_student, grad_protos = pl.pallas_call(
        last_kernel,
        in_specs=[scalars] + [whole()] * 6,
        out_specs=[pl.BlockSpec(memory_space=pl.ANY)] * 2,
        out_shape=[shape(images, patches, width), shape(near, 2 * wide)],
        scratch_shapes=[
            VMEM((images, patches, width), F32), pltpu.SemaphoreType.DMA((images,)),
            pltpu.SemaphoreType.DMA((2,)),
        ],
        compiler_params=params(16),
    )(where, keep, got, gz, *again)
    return (grad_student, grad_protos)


def solution(mesh):
    in_specs = (P("batch", None, None), P("batch", None, None), P(None, "proto"), P("batch", None))
    out_specs = (P("batch", None, None), P("batch", "proto"))
    return jax.shard_map(
        on_device, mesh=mesh, in_specs=in_specs, out_specs=out_specs, check_vma=False
    )
```

```python
import jax
import jax.numpy as jnp
from jax import lax
from jax.experimental import pallas as pl
from jax.experimental.pallas import tpu as pltpu
from jax.sharding import PartitionSpec as P

ITERS = 3
TEACHER_TEMP = 0.04
STUDENT_TEMP = 0.1
EPSILON = 1e-06
LANES = 128
Z = 8
RING = 16
ROWS = 32
WIDE = 1024
MIB = 1024 * 1024
F32 = jnp.float32
BF16 = jnp.bfloat16

VMEM = pltpu.VMEM
Z_GROUPS = [[2 * z + c for z in range(Z)] for c in range(2)]
ROW_GROUPS = [[ROWS * z + i for i in range(ROWS)] for z in range(Z)]


def whole():
    return pl.BlockSpec(memory_space=VMEM)


def cost(flops, transcendentals=0, moved=0):
    return pl.CostEstimate(
        flops=flops, transcendentals=transcendentals, bytes_accessed=moved
    )


def params(vmem):
    return pltpu.CompilerParams(vmem_limit_bytes=vmem * MIB)


def call(kernel, outs, *args, scratch=(), vmem=16, cost_estimate=None):
    return pl.pallas_call(
        kernel,
        out_shape=outs,
        in_specs=[whole()] * len(args),
        out_specs=[whole()] * len(outs),
        scratch_shapes=list(scratch),
        compiler_params=params(vmem),
        cost_estimate=cost_estimate,
    )(*args)


def one_hot_t(mask_row, patches, dtype):
    slots = mask_row.shape[1]
    patch = lax.broadcasted_iota(jnp.int32, (patches, slots), 0)
    return jnp.where(patch == mask_row, 1.0, 0.0).astype(dtype)


def fetch(pairs, sems):
    copies = [pltpu.make_async_copy(src, dst, sems.at[i]) for i, (src, dst) in enumerate(pairs)]
    for copy in copies:
        copy.start()
    return copies


def masked_rows(feats, mask_row):
    hot = one_hot_t(mask_row, feats.shape[0], BF16)
    rows = lax.dot_general(hot, feats, (((0,), (0,)), ((), ())), preferred_element_type=F32)
    return rows, jnp.sqrt(jnp.sum(rows * rows, axis=1, keepdims=True) + EPSILON)


def prep_kernel(
    where_ref, teacher_hbm, student_hbm, mask_hbm, proto_hbm, zt_ref, zs_ref, proto_ref,
    teacher_ref, student_ref, mask_ref, sems,
):
    wide = proto_ref.shape[1]
    mine = pl.ds(pl.multiple_of(where_ref[0] * wide, wide), wide)
    mask_copy, teacher_copy, student_copy, proto_copy = fetch(
        (
            (mask_hbm, mask_ref), (teacher_hbm, teacher_ref), (student_hbm, student_ref),
            (proto_hbm.at[:, mine], proto_ref),
        ),
        sems,
    )
    mask_copy.wait()
    slots = mask_ref.shape[1]
    for copy, feats, out in (
        (teacher_copy, teacher_ref, zt_ref), (student_copy, student_ref, zs_ref)
    ):
        copy.wait()
        for i in range(feats.shape[0]):
            rows, norm = masked_rows(feats[i], mask_ref[i : i + 1, :])
            out[i * slots : (i + 1) * slots, :] = (rows / norm).astype(BF16).astype(F32)
    proto_copy.wait()


def proto_kernel(proto_ref, full_ref, unit_ref, back_ref, scale_ref):
    p = proto_ref[...].astype(F32)
    scale = 1.0 / jnp.sqrt(jnp.sum(p * p, axis=0, keepdims=True) + EPSILON)
    full = p * scale
    full_ref[...] = full
    unit_ref[...] = full.astype(BF16)
    back_ref[...] = full.T.astype(BF16)
    scale_ref[...] = scale


def core_rows(where_ref, side, half):
    return pl.ds(pl.multiple_of(lax.rem(where_ref[0] + side, 2) * half, half), half)


def write_lanes(out_ref, value, row, copies):
    for m in range(copies):
        out_ref[m, pl.ds(row, 1), :] = value


def write_rows(out_ref, acc_ref, first=0):
    pieces = []
    for i in range(acc_ref.shape[0] // LANES):
        tile = acc_ref[i * LANES : (i + 1) * LANES, :].T
        pieces.append(jnp.sum(tile, axis=0, keepdims=True))
    value = jnp.concatenate(pieces, axis=0)
    for m in range(out_ref.shape[0]):
        out_ref[m, first : first + 8, :] = value


def teacher_exp_kernel(where_ref, own_ref, other_ref, unit_ref, e_ref, col_ref):
    half = own_ref.shape[0]
    wide = unit_ref.shape[1]
    block = 512
    for w in range(wide // WIDE):
        columns = pl.ds(w * WIDE, WIDE)
        unit = unit_ref[:, columns]
        total = jnp.zeros((8, WIDE), F32)
        for side, ref in enumerate((own_ref, other_ref)):
            place = core_rows(where_ref, side, half)
            for b in range(half // block):
                z = ref[b * block : (b + 1) * block, :].astype(BF16)
                e = jnp.exp(
                    jnp.dot(z, unit, preferred_element_type=F32) * (1.0 / TEACHER_TEMP)
                )
                e_ref[pl.ds(place.start + b * block, block), columns] = e
                for g in range(block // 8):
                    total += e[g * 8 : (g + 1) * 8, :]
        total = jnp.sum(total, axis=0, keepdims=True)
        for i in range(WIDE // LANES):
            write_lanes(
                col_ref, total[:, i * LANES : (i + 1) * LANES], w * (WIDE // LANES) + i, Z
            )


def student_exp_kernel(
    where_ref, own_ref, other_ref, unit_ref, s_ref, mass_ref, turned_ref
):
    half = own_ref.shape[0]
    wide = unit_ref.shape[1]
    block = 512
    for side, ref in enumerate((own_ref, other_ref)):
        turned_ref[:, core_rows(where_ref, side, half)] = ref[...].T.astype(BF16)
    for w in range(wide // WIDE):
        columns = pl.ds(w * WIDE, WIDE)
        unit = unit_ref[:, columns]
        for side, ref in enumerate((own_ref, other_ref)):
            place = core_rows(where_ref, side, half)
            for b in range(half // block):
                rows = pl.ds(place.start + b * block, block)
                z = ref[b * block : (b + 1) * block, :].astype(BF16)
                s = jnp.exp(
                    jnp.dot(z, unit, preferred_element_type=F32) * (1.0 / STUDENT_TEMP)
                )
                s_ref[rows, columns] = s
                part = sum(s[:, j * LANES : (j + 1) * LANES] for j in range(WIDE // LANES))
                if w:
                    mass_ref[rows, :] += part
                else:
                    mass_ref[rows, :] = part


def row_kernel(e_ref, parts_ref, out_ref, c_ref, acc_ref):
    c = 1.0 / jnp.sum(parts_ref[...], axis=0)
    c_ref[...] = c
    tiles = c.shape[0]
    block = 128

    def body(b, carry):
        rows = pl.ds(pl.multiple_of(b * block, block), block)
        acc = jnp.zeros((block, LANES), F32)
        for j in range(tiles):
            acc += e_ref[rows, j * LANES : (j + 1) * LANES] * c[j : j + 1, :]
        acc_ref[rows, :] = acc
        return carry

    lax.fori_loop(0, e_ref.shape[0] // block, body, 0)
    write_rows(out_ref, acc_ref)


def row_mass_kernel(e_ref, parts_ref, mass_ref, out_ref, c_ref, acc_ref):
    row_kernel(e_ref, parts_ref, out_ref, c_ref, acc_ref)
    write_rows(out_ref, mass_ref, first=8)


def spread(ref, value):
    for i in range(value.shape[0]):
        ref[i * LANES : (i + 1) * LANES, :] = jnp.broadcast_to(
            value[i : i + 1, :], (LANES, LANES)
        ).T


def col_kernel(e_ref, parts_ref, out_ref, r_ref):
    spread(r_ref, 1.0 / jnp.sum(parts_ref[:, :8, :], axis=0))
    tiles = e_ref.shape[1] // LANES
    block = 32

    def body(b, acc):
        rows = pl.ds(pl.multiple_of(b * block, block), block)
        r = r_ref[rows, :]
        out = []
        for j in range(tiles):
            value = acc[j]
            tile = e_ref[rows, j * LANES : (j + 1) * LANES] * r
            for g in range(block // 8):
                value = value + tile[g * 8 : (g + 1) * 8, :]
            out.append(value)
        return tuple(out)

    zero = tuple(jnp.zeros((8, LANES), F32) for _ in range(tiles))
    acc = lax.fori_loop(0, e_ref.shape[0] // block, body, zero, unroll=2)
    value = jnp.concatenate([jnp.sum(a, axis=0, keepdims=True) for a in acc], axis=0)
    for m in range(Z):
        out_ref[m] = value


def diff_kernel(
    e_ref, s_ref, c_ref, parts_ref, mass_ref, diff_ref, r_ref, m_ref
):
    scale = 1.0 / STUDENT_TEMP
    spread(r_ref, scale / jnp.sum(parts_ref[...], axis=0))
    spread(m_ref, scale / jnp.sum(mass_ref[:, 8:, :], axis=0))
    tiles = e_ref.shape[1] // LANES
    block = 64

    def body(b, carry):
        rows = pl.ds(pl.multiple_of(b * block, block), block)
        r = r_ref[rows, :]
        m = m_ref[rows, :]
        for j in range(tiles):
            lanes = slice(j * LANES, (j + 1) * LANES)
            targets = (r * e_ref[rows, lanes]) * c_ref[j : j + 1, :]
            probs = s_ref[rows, lanes] * m
            diff_ref[rows, lanes] = (probs - targets).astype(BF16)
        return carry

    lax.fori_loop(0, e_ref.shape[0] // block, body, 0)


def token_kernel(where_ref, diff_ref, back_ref, own_ref, give_ref):
    for side, out in enumerate((own_ref, give_ref)):
        rows = core_rows(where_ref, side, out.shape[0])
        out[...] = jnp.dot(diff_ref[rows, :], back_ref[...], preferred_element_type=F32)


def grad_kernel(where_ref, diff_ref, full_ref, scale_ref, turned_ref, *refs):
    outs, (g_ref, sems) = refs[:-2], refs[-2:]
    wide = full_ref.shape[1]
    core, z = where_ref[0], where_ref[1]
    deep = g_ref.shape[0] // Z
    near = deep // 2
    copies = []
    for w in range(wide // WIDE):
        columns = slice(w * WIDE, (w + 1) * WIDE)
        grad = jnp.dot(turned_ref[...], diff_ref[:, columns], preferred_element_type=F32)
        full = full_ref[:, columns]
        proj = jnp.sum(full.astype(BF16).astype(F32) * grad, axis=0, keepdims=True)
        g_ref[:, columns] = (grad - full * proj) * scale_ref[:, columns]
        pairs = []
        for j in range(Z):
            top = lax.rem(z + j, Z) * deep
            for side in range(2):
                take = pl.multiple_of(top + lax.rem(core + side, 2) * near, near)
                if j == 4:
                    out = outs[4 + side].at[:, columns]
                else:
                    out = outs[j + (j > 4)].at[pl.ds(side * near, near), columns]
                pairs.append((g_ref.at[pl.ds(take, near), columns], out))
        copies += fetch(pairs, sems.at[w])
    for copy in copies:
        copy.wait()


def share_kernel(parts_ref, out_ref):
    total = sum(parts_ref[i] for i in range(parts_ref.shape[0]))
    for m in range(out_ref.shape[0]):
        out_ref[m] = total


def again_kernel(feats_ref, mask_ref, full_ref, norm_ref, hot_ref):
    slots = mask_ref.shape[1]
    for i in range(feats_ref.shape[0]):
        rows = slice(i * slots, (i + 1) * slots)
        mask = mask_ref[i : i + 1, :]
        xs, norm = masked_rows(feats_ref[i], mask)
        full_ref[rows, :] = xs / norm
        norm_ref[rows, :] = norm
        hot_ref[i] = one_hot_t(mask, feats_ref.shape[1], BF16)


def last_kernel(
    where_ref, keep_ref, got_ref, gz_ref, full_ref, norm_ref, hot_ref, student_hbm, protos_hbm,
    out_ref, sems, place_sems,
):
    core, wide = where_ref[0], keep_ref.shape[1]
    copies = fetch(
        [
            (ref, protos_hbm.at[:, pl.ds(pl.multiple_of(lax.rem(core + side, 2) * wide, wide), wide)])
            for side, ref in enumerate((keep_ref, got_ref))
        ],
        place_sems,
    )
    slots = hot_ref.shape[2]
    for i in range(out_ref.shape[0]):
        rows = slice(i * slots, (i + 1) * slots)
        zsf = full_ref[rows, :]
        gz = gz_ref[rows, :]
        proj = jnp.sum(zsf * gz, axis=1, keepdims=True)
        grad = (gz - zsf * proj) / norm_ref[rows, :]
        hot = hot_ref[i]
        high = grad.astype(BF16)
        low = (grad - high.astype(F32)).astype(BF16)
        out_ref[i] = jnp.dot(hot, high, preferred_element_type=F32) + jnp.dot(
            hot, low, preferred_element_type=F32
        )
        copies += fetch(((out_ref.at[i], student_hbm.at[i]),), sems.at[pl.ds(i, 1)])
    for copy in copies:
        copy.wait()


def sum_kernel(a_ref, b_ref, out_ref):
    out_ref[...] = a_ref[...] + b_ref[...]


def first_step_kernel(low):
    def kernel(rel_hbm, got_ref, out_ref, sem):
        for copy in fetch(((rel_hbm, out_ref),), sem):
            copy.wait()
        near = got_ref.shape[0]
        rows = slice(near, 2 * near) if low else slice(0, near)
        out_ref[rows, :] += got_ref[...]

    return kernel


def step_kernel(rel_hbm, got_ref, out_ref, sem):
    for copy in fetch(((rel_hbm, out_ref),), sem):
        copy.wait()
    out_ref[...] += got_ref[...]


def last_sum_kernel(rel_hbm, up_ref, down_ref, keep_ref, give_ref, rel, sem):
    for copy in fetch(((rel_hbm, rel),), sem):
        copy.wait()
    near = keep_ref.shape[0]
    total = rel[...] + (up_ref[...] + down_ref[...])
    keep_ref[...] = total[:near, :]
    give_ref[...] = total[near:, :]


def shape(*dims, dtype=F32):
    return jax.ShapeDtypeStruct(dims, dtype)


def hold(*dims, dtype=F32):
    return pltpu.VMEM(dims, dtype)


def far(*dims):
    return pltpu.HBM(dims, F32)


def in_hbm(x):
    return pltpu.with_memory_space_constraint(x, pltpu.HBM)


def other_core(x):
    return lax.ppermute(x, "batch", [(i, i ^ 1) for i in range(RING)])


def along_z(x, d):
    return lax.ppermute(
        x, "batch", [(i, ((i // 2 + d) % Z) * 2 + i % 2) for i in range(RING)]
    )


def all_columns(x):
    return lax.all_to_all(x, "batch", 0, 0, axis_index_groups=Z_GROUPS)


def all_rows(x):
    return lax.all_to_all(x, ("batch", "proto"), 0, 0, axis_index_groups=ROW_GROUPS)


def tie(x, y):
    return lax.optimization_barrier((x, y))[0]


def on_device(teacher_feats, student_feats, prototypes, mask_index):
    images, patches, width = teacher_feats.shape
    slots = mask_index.shape[1]
    own = images * slots
    tokens = 2 * own
    wide = prototypes.shape[1] // 2
    lane_tiles = wide // LANES
    row_tiles = tokens // LANES
    place = lax.axis_index("batch")
    where = jnp.stack([lax.rem(place, 2), lax.div(place, 2)]).astype(jnp.int32)
    scalars = pl.BlockSpec(memory_space=pltpu.SMEM)

    def placed(kernel, outs, *args, **kw):
        return pl.pallas_call(
            kernel,
            in_specs=[scalars] + [whole()] * len(args),
            out_specs=[whole()] * len(outs),
            out_shape=outs,
            scratch_shapes=kw.get("scratch", []),
            compiler_params=params(16),
            cost_estimate=kw.get("cost_estimate"),
        )(where, *args)

    zt, zs, protos = pl.pallas_call(
        prep_kernel,
        in_specs=[scalars] + [pl.BlockSpec(memory_space=pl.ANY)] * 4,
        out_specs=[whole()] * 3,
        out_shape=[shape(own, width), shape(own, width), hold(width, wide, dtype=BF16)],
        scratch_shapes=[
            VMEM(teacher_feats.shape, BF16), VMEM(student_feats.shape, BF16),
            VMEM(mask_index.shape, jnp.int32), pltpu.SemaphoreType.DMA((4,)),
        ],
        compiler_params=params(16),
    )(where, in_hbm(teacher_feats), in_hbm(student_feats), in_hbm(mask_index), in_hbm(prototypes))
    zt_other = other_core(zt)
    zs_other = other_core(zs)
    full, unit, back, p_scale = call(
        proto_kernel,
        [
            hold(width, wide), hold(width, wide, dtype=BF16), hold(wide, width, dtype=BF16),
            shape(1, wide),
        ],
        protos,
    )

    exp_cost = cost(2 * tokens * wide * width, tokens * wide)
    e, col_out = placed(
        teacher_exp_kernel,
        [hold(tokens, wide), shape(Z, lane_tiles, LANES)],
        zt, zt_other, unit, cost_estimate=exp_cost,
    )
    s, mass_acc, turned = placed(
        student_exp_kernel,
        [hold(tokens, wide), shape(tokens, LANES), shape(width, tokens, dtype=BF16)],
        zs, zs_other, unit, cost_estimate=exp_cost,
    )
    col_out = tie(col_out, mass_acc)

    mass = None
    for sweep in range(ITERS):
        col_parts = all_columns(col_out)
        extra = [mass_acc] if sweep == 1 else []
        row_out, c = call(
            row_mass_kernel if extra else row_kernel,
            [shape(ROWS, row_tiles * (1 + len(extra)), LANES), shape(lane_tiles, LANES)],
            e, col_parts, *extra,
            scratch=[VMEM((tokens, LANES), F32)],
        )
        row_parts = all_rows(row_out)
        if extra:
            mass = row_parts
        if sweep < ITERS - 1:
            (col_out,) = call(
                col_kernel, [shape(Z, lane_tiles, LANES)], e, row_parts,
                scratch=[VMEM((tokens, LANES), F32)],
            )

    (diff,) = call(
        diff_kernel, [shape(tokens, wide, dtype=BF16)], e, s, c, row_parts, mass,
        scratch=[VMEM((tokens, LANES), F32), VMEM((tokens, LANES), F32)],
    )
    gz, gz_give = placed(
        token_kernel, [hold(own, width), shape(own, width)], diff, back,
        cost_estimate=cost(2 * tokens * wide * width),
    )
    gz_got = other_core(gz_give)
    deep = width // Z
    near = deep // 2
    anywhere = pl.BlockSpec(memory_space=pltpu.HBM)
    rel = pl.pallas_call(
        grad_kernel,
        in_specs=[scalars] + [whole()] * 4,
        out_specs=[anywhere] * 9,
        out_shape=[far(deep, wide)] * 4 + [far(near, wide)] * 2 + [far(deep, wide)] * 3,
        scratch_shapes=[VMEM((width, wide), F32), pltpu.SemaphoreType.DMA((wide // WIDE, 2 * Z))],
        compiler_params=params(16),
        cost_estimate=cost(2 * tokens * wide * width),
    )(where, tie(diff, (gz, gz_give)), full, p_scale, turned)

    def step(kernel, term, got, work=0):
        return pl.pallas_call(
            kernel,
            in_specs=[anywhere, whole()],
            out_specs=whole(),
            out_shape=shape(deep, wide),
            scratch_shapes=[pltpu.SemaphoreType.DMA((1,))],
            compiler_params=params(16),
            cost_estimate=cost(work) if work else None,
        )(term, got)

    up, down = along_z(rel[4], 1), along_z(rel[5], -1)
    up = step(first_step_kernel(False), rel[3], up, 2 * 10**9)
    down = step(first_step_kernel(True), rel[6], down, 2 * 10**9)
    (gz,) = call(sum_kernel, [shape(own, width)], gz, gz_got)
    gz_parts = lax.all_to_all(
        tie(gz, rel).reshape(RING, own // RING, width), "proto", 0, 0
    )
    (gz_share,) = call(share_kernel, [shape(RING, own // RING, width)], gz_parts)
    up, down = along_z(up, 1), along_z(down, -1)
    up = step(step_kernel, rel[2], up)
    down = step(step_kernel, rel[7], down)
    gz = lax.all_to_all(gz_share, "proto", 0, 0).reshape(own, width)
    up, down = along_z(up, 1), along_z(down, -1)
    up, down = tie((up, down), gz_share)
    up = step(step_kernel, rel[1], up)
    down = step(step_kernel, rel[8], down)
    up, down = along_z(up, 1), along_z(down, -1)
    up = tie(up, gz)
    keep, give = pl.pallas_call(
        last_sum_kernel,
        in_specs=[anywhere, whole(), whole()],
        out_specs=[whole()] * 2,
        out_shape=[shape(near, wide)] * 2,
        scratch_shapes=[VMEM((deep, wide), F32), pltpu.SemaphoreType.DMA((1,))],
        compiler_params=params(16),
    )(rel[0], up, down)
    got = other_core(give)
    again = call(
        again_kernel,
        [shape(own, width), shape(own, 1), shape(images, patches, slots, dtype=BF16)],
        student_feats, tie(mask_index, give),
    )
    grad_student, grad_protos = pl.pallas_call(
        last_kernel,
        in_specs=[scalars] + [whole()] * 6,
        out_specs=[pl.BlockSpec(memory_space=pl.ANY)] * 2,
        out_shape=[shape(images, patches, width), shape(near, 2 * wide)],
        scratch_shapes=[
            VMEM((images, patches, width), F32), pltpu.SemaphoreType.DMA((images,)),
            pltpu.SemaphoreType.DMA((2,)),
        ],
        compiler_params=params(16),
    )(where, keep, got, gz, *again)
    return (grad_student, grad_protos)


def solution(mesh):
    in_specs = (P("batch", None, None), P("batch", None, None), P(None, "proto"), P("batch", None))
    out_specs = (P("batch", None, None), P("batch", "proto"))
    return jax.shard_map(
        on_device, mesh=mesh, in_specs=in_specs, out_specs=out_specs, check_vma=False
    )
```
